32 devices in a mesh: parts: 1, clus: 4 (over z), lvl: 4 (over y, x), rep: 2 (over core).
Axes of the slice: x: 2, y: 2, z: 4, core: 2. Of those that a mesh axis runs over, the one named last changes fastest.
Arguments:
- voxel_field: bfloat16 [256, 24, 512], P(('lvl', 'rep'), None, ('parts', 'clus')), may hold values from -6 to 6
- row_basis: bfloat16 [256, 64, 512], P(('lvl', 'rep'), None, ('parts', 'clus')), may hold values from -0.375 to 0.375
- near_block: bfloat16 [256, 256, 512], P(('lvl', 'rep'), None, ('parts', 'clus')), may hold values from -0.375 to 0.375
- up_transfer: bfloat16 [64, 64, 512], P(None, None, ('parts', 'clus')), may hold values from -0.25 to 0.25
- coupling: bfloat16 [64, 64, 8, 2, 512], P(None, None, ('lvl', 'rep'), None, ('parts', 'clus')), may hold values from -0.1875 to 0.1875
- parent_coupling: bfloat16 [64, 64, 8, 2, 64], P(None, None, ('lvl', 'rep'), None, ('parts', 'clus')), may hold values from -0.1875 to 0.1875
- down_transfer: bfloat16 [64, 64, 512], P(None, None, ('parts', 'clus')), may hold values from -0.75 to 0.75
- column_basis: bfloat16 [64, 256, 512], P(None, ('lvl', 'rep'), ('parts', 'clus')), may hold values from -0.75 to 0.75
- parent_perm: int32 [64], P('parts'), may hold values from 0 to 63, as said below
- partner_owner: int32 [8, 512, 2], P(('lvl', 'rep'), ('parts', 'clus')), may hold values from 0 to 3, all different within a row; in each aligned block of 128 rows (0 to 127, 128 to 255, ..., all dimensions but the last counted through in order) at most 128 rows name the same one
- partner_local: int32 [8, 512, 2], P(('lvl', 'rep'), ('parts', 'clus')), may hold values from 0 to 127
- parent_owner: int32 [8, 64, 2], P(('lvl', 'rep'), ('parts', 'clus')), may hold values from 0 to 3, all different within a row; in each aligned block of 16 rows (0 to 15, 16 to 31, ..., all dimensions but the last counted through in order) at most 16 rows name the same one
- parent_local: int32 [8, 64, 2], P(('lvl', 'rep'), ('parts', 'clus')), may hold values from 0 to 15
- block_count: int32 [512], P(('parts', 'clus')), may hold values from 4 to 16
Outputs:
- adjoint: bfloat16 [256, 24, 512], P(('lvl', 'rep'), None, ('parts', 'clus'))
The draws below stay inside these ranges and needn't reach their ends.
Inputs may be any that keep to these rules, and one draw needn't show every extreme that they name: `parent_perm`: a permutation of the 64 parents; of the 16 parents of each aligned block, exactly 4 land in each aligned block of 16. `partner_owner`: the slots of one leaf in one slot group name distinct owners; in the rows of one device (one slot group, 128 leaves of one owner) no owner is named by more than 128 slots. `parent_owner`: the slots of one parent in one slot group name distinct owners; in the rows of one device (one slot group, 16 parents of one owner) no owner is named by more than 16 slots.
All inputs are finite; a program needn't handle non-finite values.
Results may differ from the reference program's by a relative error of at most 0.0059.
Values may be sent and summed in bfloat16 or wider, within the bound.
No kernel may reach another device: no remote copies, remote signals or barrier semaphores. Data moves between devices by JAX's collectives and lax.ppermute only.
A program may use at most 128 MiB of HBM per device.

```python
import math
import jax
import jax.numpy as jnp
import numpy as np
from jax import lax

K = 64
M = 256
CH = 8
PAR_DEV = 16
NB = 16
NBP = 16
NVEC = 24
GROUP = 8
OWNERS = 4
LEAF_DEV = 128
NPAR = 64
NLEAF = 512
SLOT_DEV = 2
PSLOT_DEV = 2
PEER_PAR = 4
CAP = 128
PCAP = 16


def draw_parent_perm(key, part):
    key = jax.random.fold_in(key, 11)
    send_keys = jax.random.split(jax.random.fold_in(key, 1), OWNERS)
    land_keys = jax.random.split(jax.random.fold_in(key, 2), OWNERS)
    spread = jax.vmap(lambda single: jax.random.permutation(single, PAR_DEV))(send_keys).astype(jnp.int32)
    landing = jax.vmap(lambda single: jax.random.permutation(single, PAR_DEV))(land_keys).astype(jnp.int32)
    source = jnp.arange(OWNERS, dtype=jnp.int32)[:, None]
    target_owner = spread // PEER_PAR
    arrival = source * PEER_PAR + spread % PEER_PAR
    position = landing[target_owner, arrival]
    return (target_owner * PAR_DEV + position).reshape(-1).astype(jnp.int32)


def with_ends(drawn, own_key, low, largest):
    place = [jax.random.randint(jax.random.fold_in(own_key, axis), (), 0, length) for axis, length in enumerate(drawn.shape)]
    longest = drawn.shape.index(max(drawn.shape))
    neighbour = place[:longest] + [(place[longest] + 1) % drawn.shape[longest]] + place[longest + 1:]
    return drawn.at[tuple(place)].set(low).at[tuple(neighbour)].set(largest)


def block_levels(stream_key, shape, shards, smallest, high):
    factor_of, own = 1.0, jax.random.fold_in(stream_key, 6)
    for dim, parts in shards:
        steps = jnp.exp(jax.random.uniform(jax.random.fold_in(own, dim), (parts,), jnp.float32, smallest / len(shards), high / len(shards)))
        factor_of = factor_of * jnp.repeat(steps, shape[dim] // parts).reshape([-1 if axis == dim else 1 for axis in range(len(shape))])
    return factor_of


def routed_block(stream_key, own, number, rows, count, top, bound, slope):
    order = jax.random.permutation(stream_key, count)
    crowded, ordinary = shares(count, rows * top, bound, slope, True), shares(count, rows * top, bound, slope, False)
    places = jnp.arange(count)

    def named(tallies, rotation):
        used = int((tallies > 0).sum())
        fixed = max(1, used // 4)
        passed = fixed + (places - fixed + rotation * (used - fixed)) % max(1, count - fixed)
        return jnp.zeros((count,), jnp.int32).at[order[jnp.where(places < fixed, places, passed)]].set(jnp.asarray(tallies, jnp.int32))

    tallies = jnp.where(number % 4 == 0, named(crowded, number // 4), named(ordinary, number - number // 4 - 1))
    mixed = jax.random.permutation(jax.random.fold_in(own, 3), count)
    donor, taker = mixed[0:count // 2 * 2:2], mixed[1:count // 2 * 2:2]
    margin = jnp.minimum(tallies[donor] - 1, bound - tallies[taker]) // 2
    margin = jnp.where((donor == order[0]) | (taker == order[0]) | (tallies[taker] == 0), 0, jnp.maximum(margin, 0))
    passed = jax.random.randint(jax.random.fold_in(own, 4), (count // 2,), 0, 1 << 20) % (margin + 1)
    tallies = tallies.at[donor].add(-passed).at[taker].add(passed)
    labels = jnp.searchsorted(jnp.cumsum(tallies), jnp.arange(rows * top), side="right").astype(jnp.int32)
    table = labels.reshape(top, rows).T
    table = table[jax.random.permutation(jax.random.fold_in(own, 1), rows)]
    rotation = jax.random.randint(jax.random.fold_in(own, 2), (rows, 1), 0, top)
    return jnp.take_along_axis(table, (jnp.arange(top)[None, :] + rotation) % top, axis=1)


def shares(count, total, bound, lean, full):
    loads = [(1 << 20) // math.isqrt(standing ** lean) + 1 for standing in range(1, count + 1)]
    largest = bound if full else min(bound, max(-(-total // count), total * loads[0] // sum(loads)))
    least = 1 if total - largest >= count - 1 else 0
    counts, spare = [largest] + [least] * (count - 1), total - largest - least * (count - 1)
    while spare > 0:
        free = [i for i in range(1, count) if counts[i] < largest] or [i for i in range(1, count) if counts[i] < bound]
        whole, left = sum([loads[i] for i in free]), spare
        for i in free:
            extra = min(bound - counts[i], max(1, left * loads[i] // whole), spare)
            counts[i] = counts[i] + extra
            spare = spare - extra
    return np.array(counts)


def scatter_about(rng, shape, scale, limit, shards=(), kind=jnp.bfloat16):
    values = scale * jax.random.normal(rng, shape, jnp.float32)
    if shards:
        values = values * block_levels(rng, shape, shards, -0.22, 0.18)
    return jnp.clip(values, -limit, limit).astype(kind)


def setup_inputs(seed: int = 0, part: int = 0) -> dict:
    splits = jax.random.split(jax.random.key(seed), 15)
    part_keys = jax.random.split(jax.random.fold_in(splits[14], part), 15)
    voxel_field = scatter_about(part_keys[0], (M, NVEC, NLEAF), 1.0, 6.0, ((0, 8), (2, 4)))
    row_basis = scatter_about(part_keys[1], (M, K, NLEAF), M ** -0.5, 0.375, ((0, 8), (2, 4)))
    near_block = scatter_about(part_keys[2], (M, M, NLEAF), M ** -0.5, 0.375, ((0, 8), (2, 4)))
    up_transfer = scatter_about(part_keys[3], (K, K, NLEAF), (CH * K) ** -0.5, 0.25, ((2, 4),))
    coupling = scatter_about(part_keys[4], (K, K, GROUP, SLOT_DEV, NLEAF), (NB * K) ** -0.5, 0.1875, ((2, 8), (4, 4)))
    parent_coupling = scatter_about(part_keys[5], (K, K, GROUP, PSLOT_DEV, NPAR), (NBP * K) ** -0.5, 0.1875, ((2, 8), (4, 4)))
    down_transfer = scatter_about(part_keys[6], (K, K, NLEAF), K ** -0.5, 0.75, ((2, 4),))
    column_basis = scatter_about(part_keys[7], (K, M, NLEAF), K ** -0.5, 0.75, ((1, 8), (2, 4)))
    parent_perm = draw_parent_perm(jax.random.fold_in(jax.random.fold_in(splits[14], part), 71), part)
    partner_owner_keys = jax.random.split(jax.random.fold_in(part_keys[9], 1), GROUP * NLEAF // LEAF_DEV)
    partner_owner_turns = jax.random.permutation(jax.random.fold_in(part_keys[9], 3), GROUP * NLEAF // LEAF_DEV)
    partner_owner = jax.vmap(lambda own, number: routed_block(jax.random.fold_in(part_keys[9], 2), own, number, LEAF_DEV, OWNERS, SLOT_DEV, CAP, 2))(partner_owner_keys, partner_owner_turns).reshape((GROUP, NLEAF, SLOT_DEV))
    partner_local = with_ends(jax.random.randint(part_keys[10], (GROUP, NLEAF, SLOT_DEV), 0, LEAF_DEV), jax.random.fold_in(part_keys[10], 1), 0, LEAF_DEV - 1).astype(jnp.int32)
    parent_owner_keys = jax.random.split(jax.random.fold_in(part_keys[11], 1), GROUP * NPAR // PAR_DEV)
    parent_owner_turns = jax.random.permutation(jax.random.fold_in(part_keys[11], 3), GROUP * NPAR // PAR_DEV)
    parent_owner = jax.vmap(lambda own, number: routed_block(jax.random.fold_in(part_keys[11], 2), own, number, PAR_DEV, OWNERS, PSLOT_DEV, PCAP, 2))(parent_owner_keys, parent_owner_turns).reshape((GROUP, NPAR, PSLOT_DEV))
    parent_local = with_ends(jax.random.randint(part_keys[12], (GROUP, NPAR, PSLOT_DEV), 0, PAR_DEV), jax.random.fold_in(part_keys[12], 1), 0, PAR_DEV - 1).astype(jnp.int32)
    block_count = with_ends(jax.random.randint(part_keys[13], (NLEAF,), NB // 4, NB + 1), jax.random.fold_in(part_keys[13], 1), NB // 4, NB).astype(jnp.int32)
    return dict(voxel_field=voxel_field, row_basis=row_basis, near_block=near_block, up_transfer=up_transfer, coupling=coupling, parent_coupling=parent_coupling, down_transfer=down_transfer, column_basis=column_basis, parent_perm=parent_perm, partner_owner=partner_owner, partner_local=partner_local, parent_owner=parent_owner, parent_local=parent_local, block_count=block_count)


def blockwise(compute, arrays, count):

    def one_block(block_index):
        pieces = []
        for array in arrays:
            width = array.shape[-1] // count
            pieces.append(lax.dynamic_slice_in_dim(array, block_index * width, width, array.ndim - 1))
        return compute(*pieces)
    stacked = lax.map(one_block, jnp.arange(count, dtype=jnp.int32))
    moved = jnp.moveaxis(stacked, 0, -2)
    return moved.reshape(moved.shape[:-2] + (-1,))

def near_product(blocks, values):
    return jnp.einsum('pml,pvl->mvl', blocks.astype(jnp.float32), values.astype(jnp.float32))

def leaf_product(blocks, rows):
    return jnp.einsum('jkgil,vjgil->vkl', blocks.astype(jnp.float32), rows.astype(jnp.float32))

def reference(voxel_field, row_basis, near_block, up_transfer, coupling, parent_coupling, down_transfer, column_basis, parent_perm, partner_owner, partner_local, parent_owner, parent_local, block_count):
    inverse = jnp.argsort(parent_perm).astype(jnp.int32)
    blocks = voxel_field.reshape(M, NVEC, NPAR, CH)
    regrouped = jnp.take(blocks, inverse, axis=2).reshape(M, NVEC, NLEAF)
    coeffs = jnp.einsum('mvl,mkl->vkl', regrouped.astype(jnp.float32), row_basis.astype(jnp.float32)).astype(jnp.bfloat16)
    parent_coeffs = jnp.einsum('jkpc,vjpc->vkp', up_transfer.reshape(K, K, NPAR, CH).astype(jnp.float32), coeffs.reshape(NVEC, K, NPAR, CH).astype(jnp.float32)).astype(jnp.bfloat16)
    near = blockwise(near_product, [near_block, regrouped], OWNERS)
    target = jnp.transpose(partner_owner * LEAF_DEV + partner_local, (0, 2, 1)).astype(jnp.int32)
    slot_index = jnp.arange(GROUP, dtype=jnp.int32)[:, None, None] * SLOT_DEV + jnp.arange(SLOT_DEV, dtype=jnp.int32)[None, :, None]
    live_mask = slot_index < block_count[None, None, :]
    leaf_rows = jnp.take(coeffs, target, axis=2)
    leaf_rows = jnp.where(live_mask[None, None], leaf_rows, jnp.zeros_like(leaf_rows))
    leaf_far = blockwise(leaf_product, [coupling, leaf_rows], OWNERS)
    parent_target = jnp.transpose(parent_owner * PAR_DEV + parent_local, (0, 2, 1)).astype(jnp.int32)
    parent_rows = jnp.take(parent_coeffs, parent_target, axis=2)
    parent_far = jnp.einsum('jkgip,vjgip->vkp', parent_coupling.astype(jnp.float32), parent_rows.astype(jnp.float32)).astype(jnp.bfloat16)
    downward = jnp.einsum('jkpc,vjp->vkpc', down_transfer.reshape(K, K, NPAR, CH).astype(jnp.float32), parent_far.astype(jnp.float32))
    far_coeffs = (leaf_far + downward.reshape(NVEC, K, NLEAF)).astype(jnp.bfloat16)
    far_field = jnp.einsum('kml,vkl->mvl', column_basis.astype(jnp.float32), far_coeffs.astype(jnp.float32))
    return (near + far_field).astype(jnp.bfloat16)
```

```python
import functools

import jax
import jax.numpy as jnp
from jax import lax
from jax.experimental import pallas as pl
from jax.experimental.pallas import tpu as pltpu
from jax.sharding import PartitionSpec as P

F32 = jnp.float32
BF16 = jnp.bfloat16
VMEM_LIMIT = 40 * 1024 * 1024


def vmem():
    return pl.BlockSpec(memory_space=pltpu.VMEM)


def smem():
    return pl.BlockSpec(memory_space=pltpu.SMEM)


def params(**more):
    return pltpu.CompilerParams(vmem_limit_bytes=VMEM_LIMIT, **more)


def cost(flops, nbytes):
    return pl.CostEstimate(flops=flops, bytes_accessed=nbytes, transcendentals=0)


def iota(shape, dim):
    return lax.broadcasted_iota(jnp.int32, shape, dim)


def row_of(ref, row):
    return ref[pl.ds(row, 1), :]


def mac_rows(total_steps, weight_at, row_at, accs, unroll):
    def body(step, carry):
        weight = weight_at(step)
        return tuple(acc + weight * row_at(step, n) for n, acc in enumerate(carry))

    return lax.fori_loop(0, total_steps, body, tuple(accs), unroll=unroll)


def pack_kernel(owners, vh, perm_ref, ids_ref, own_ref, peer_ref, out_ref, rows_scr, count_scr):
    slab, vectors, leaves = own_ref.shape
    parents = perm_ref.shape[0] // owners
    children = leaves // parents
    reps = vectors // vh
    width = leaves // owners
    me, parity = ids_ref[0], ids_ref[2]
    for owner in range(owners):
        count_scr[owner] = 0
    row = iota((leaves, leaves), 0)
    lane = iota((leaves, leaves), 1)
    parent_of_row = row // children
    target = row % children
    for parent in range(parents):
        place = perm_ref[me * parents + parent]
        owner = place // parents
        rank = count_scr[owner]
        count_scr[owner] = rank + 1
        code = (owner ^ me) * leaves + rank * children
        target = target + jnp.where(parent_of_row == parent, code, 0)
    part = (slab // owners) * vh
    rows_scr[0] = own_ref[...].reshape(slab * vectors, leaves).astype(F32)
    rows_scr[1] = peer_ref[...].reshape(slab * vectors, leaves).astype(F32)
    pieces = []
    for q in range(owners):
        start = q * (slab // owners) * vectors + parity
        pieces.append(
            jnp.concatenate(
                [rows_scr[s, pl.ds(start, part, stride=reps), :] for s in range(2)], axis=0
            ).astype(BF16)
        )
    for s in range(owners):
        total = jnp.zeros((2 * part, leaves), F32)
        for q in range(owners):
            onehot = jnp.where(target + (q * width - s * leaves) == lane, 1.0, 0.0).astype(BF16)
            total = total + jnp.dot(pieces[q], onehot, preferred_element_type=F32)
        out_ref[s] = total.astype(BF16)


def place_kernel(owners, children, perm_ref, ids_ref, out_ref, code_scr, count_scr):
    leaves = out_ref.shape[1]
    everyone = perm_ref.shape[0]
    parents = everyone // owners
    me = ids_ref[0]
    for owner in range(owners):
        count_scr[owner] = 0

    def body(parent, carry):
        place = perm_ref[parent]
        source = parent // parents
        mine = (place // parents) == me
        rank = count_scr[source]
        slot = jnp.where(mine, place % parents, parents)
        code_scr[slot] = (source ^ me) * leaves + rank * children
        count_scr[source] = rank + jnp.where(mine, 1, 0)
        return carry

    lax.fori_loop(0, everyone, body, 0, unroll=8)
    lane = iota(out_ref.shape, 1)
    code = lane % children
    for parent in range(parents):
        code = code + jnp.where(lane // children == parent, code_scr[parent], 0)
    out_ref[...] = code


def coeff_kernel(owners, lvls, vh, vs, ids_ref, code_ref, *refs):
    chunks = refs[:owners]
    own_ref, peer_ref = refs[owners : owners + 2]
    field_ref, keep_ref = refs[owners + 2 : owners + 4]
    sends = refs[owners + 4 :]
    slab, rank_width, leaves = own_ref.shape
    width = leaves // owners
    part = (slab // owners) * vh
    lvl = ids_ref[1]
    code = jnp.broadcast_to(code_ref[0:1, :], (leaves, leaves))
    row = iota((leaves, leaves), 0)
    for q in range(owners):
        total = jnp.zeros((2 * part, leaves), F32)
        for s in range(owners):
            onehot = jnp.where(code + (q * width - s * leaves) == row, 1.0, 0.0).astype(BF16)
            total = total + jnp.dot(chunks[s][...], onehot, preferred_element_type=F32)
        for half in range(2):
            field_ref[half, q * part : (q + 1) * part, :] = total[half * part : (half + 1) * part]
    for t in list(range(1, lvls)) + [0]:
        first = (lvl ^ t) * vs
        accs = [jnp.zeros((rank_width, leaves), F32) for _ in range(vs)]
        for half, ref in enumerate((own_ref, peer_ref)):
            accs = mac_rows(
                slab,
                lambda m, ref=ref: ref[m].astype(F32),
                lambda m, n, half=half: field_ref[
                    half, pl.ds(m * vh + jnp.minimum(first + n, vh - 1), 1), :
                ],
                accs,
                4,
            )
        for n in range(vs):
            block = slice(n * rank_width, (n + 1) * rank_width)
            if t == 0:
                keep_ref[block, :] = accs[n]
            else:
                sends[t - 1][block, :] = accs[n].astype(BF16)


def packed_rows(vs, rank_width, children):
    rows = vs * rank_width + vs * (rank_width // children)
    return -(-rows // 32) * 32


def up_kernel(vs, children, keep_ref, *refs):
    recvs, up_ref, out_ref, coeff_scr = refs[:-3], refs[-3], refs[-2], refs[-1]
    rank_width, _, leaves = up_ref.shape
    high_count = rank_width // children
    total = keep_ref[...]
    for ref in recvs:
        total = total + ref[...].astype(F32)
    coeffs = total.astype(BF16)
    out_ref[0 : vs * rank_width, :] = coeffs
    coeff_scr[...] = coeffs.astype(F32)
    accs = mac_rows(
        rank_width,
        lambda j: up_ref[j].astype(F32),
        lambda j, n: row_of(coeff_scr, n * rank_width + j),
        [jnp.zeros((rank_width, leaves), F32) for _ in range(vs)],
        8,
    )
    each = jnp.concatenate(accs, axis=0)
    high = each.astype(BF16)
    rest = each - high.astype(F32)
    low = rest.astype(BF16)
    last = (rest - low.astype(F32)).astype(BF16)
    same = (iota((leaves, leaves), 0) // children) == (iota((leaves, leaves), 1) // children)
    group = jnp.where(same, 1.0, 0.0).astype(BF16)
    summed = (
        jnp.dot(high, group, preferred_element_type=F32)
        + jnp.dot(low, group, preferred_element_type=F32)
        + jnp.dot(last, group, preferred_element_type=F32)
    )
    summed = summed.reshape(vs * high_count, children, leaves)
    diagonal = iota(summed.shape, 1) == iota(summed.shape, 2) % children
    parents = jnp.where(diagonal, summed, 0.0).sum(axis=1)
    extra = out_ref.shape[0] - vs * rank_width
    padded = jnp.concatenate(
        [parents, jnp.zeros((extra - vs * high_count, leaves), F32)], axis=0
    )
    out_ref[vs * rank_width :, :] = padded.astype(BF16)


def table_kernel(children, leaf_ref, parent_ref, leaf_out, parent_out, spread_out):
    slots, leaves = leaf_ref.shape
    sources = leaf_out.shape[0]
    for codes, out in ((leaf_ref, leaf_out), (parent_ref, parent_out)):
        for i in range(codes.shape[0]):
            code = jnp.broadcast_to(codes[i : i + 1, :], (sources, leaves))
            hit = code == iota((sources, leaves), 0)
            out[:, i * leaves : (i + 1) * leaves] = jnp.where(hit, 1.0, 0.0).astype(BF16)
    row = iota((leaves, leaves), 0)
    base = (iota((leaves, leaves), 1) // children) * children
    for low in range(children):
        spread_out[:, low * leaves : (low + 1) * leaves] = jnp.where(
            row == base + low, 1.0, 0.0
        ).astype(BF16)


def far_kernel(
    owners, vs, children, leaf_table, parent_table, spread_ref, block_ref, couple_ref, pcouple_ref,
    out_ref, rows_scr, prows_scr, acc_scr, pacc_scr,
):
    step, steps = pl.program_id(0), pl.num_programs(0)
    _, rank_width, _, leaves = couple_ref.shape
    slots = leaf_table.shape[1] // leaves
    pslots = parent_table.shape[1] // leaves
    high_count = rank_width // children
    per_block = block_ref.shape[0] // owners
    mine = vs * rank_width
    tail = per_block - mine

    @pl.when(step == 0)
    def _():
        rows = jnp.zeros((mine, slots * leaves), F32)
        prows = jnp.zeros((tail, pslots * leaves), F32)
        for o in range(owners):
            part = slice(o * leaves, (o + 1) * leaves)
            start = o * per_block
            rows = rows + jnp.dot(
                block_ref[start : start + mine, :], leaf_table[part, :],
                preferred_element_type=F32,
            )
            prows = prows + jnp.dot(
                block_ref[start + mine : start + per_block, :], parent_table[part, :],
                preferred_element_type=F32,
            )
        for i in range(slots):
            rows_scr[i] = rows[:, i * leaves : (i + 1) * leaves]
        for i in range(pslots):
            wide = jnp.dot(
                prows[:, i * leaves : (i + 1) * leaves].astype(BF16), spread_ref[...],
                preferred_element_type=F32,
            )
            for low in range(children):
                prows_scr[i, low] = wide[:, low * leaves : (low + 1) * leaves]
        acc_scr[...] = jnp.zeros_like(acc_scr)
        pacc_scr[...] = jnp.zeros_like(pacc_scr)

    accs = mac_rows(
        rank_width,
        lambda j: couple_ref[0, j].astype(F32),
        lambda j, n: rows_scr[step, pl.ds(n * rank_width + j, 1), :],
        [acc_scr[n * rank_width : (n + 1) * rank_width, :] for n in range(vs)],
        8,
    )
    for n in range(vs):
        acc_scr[n * rank_width : (n + 1) * rank_width, :] = accs[n]

    def body(high, carry):
        for low in range(children):
            weight = pcouple_ref[0, high * children + low]
            carry = tuple(
                acc + weight * prows_scr[step, low, pl.ds(n * high_count + high, 1), :]
                for n, acc in enumerate(carry)
            )
        return carry

    paccs = lax.fori_loop(
        0, high_count, body,
        tuple(pacc_scr[n * high_count : (n + 1) * high_count, :] for n in range(vs)),
    )
    for n in range(vs):
        pacc_scr[n * high_count : (n + 1) * high_count, :] = paccs[n]

    @pl.when(step == steps - 1)
    def _():
        out_ref[0:mine, :] = acc_scr[...].astype(out_ref.dtype)
        out_ref[mine:, :] = pacc_scr[...].astype(out_ref.dtype)


def down_kernel(vs, children, spread_ref, keep_ref, *refs):
    recvs, down_ref, out_ref, rows_scr = refs[:-3], refs[-3], refs[-2], refs[-1]
    rank_width, _, leaves = down_ref.shape
    high_count = rank_width // children
    total = keep_ref[...]
    for ref in recvs:
        total = total + ref[...].astype(F32)
    mine = vs * rank_width
    wide = jnp.dot(total[mine:, :].astype(BF16), spread_ref[...], preferred_element_type=F32)
    for low in range(children):
        rows_scr[low] = wide[:, low * leaves : (low + 1) * leaves]

    def body(high, carry):
        for low in range(children):
            weight = down_ref[high * children + low].astype(F32)
            carry = tuple(
                acc + weight * rows_scr[low, pl.ds(n * high_count + high, 1), :]
                for n, acc in enumerate(carry)
            )
        return carry

    accs = lax.fori_loop(
        0, high_count, body,
        tuple(total[n * rank_width : (n + 1) * rank_width, :] for n in range(vs)),
    )
    for n in range(vs):
        out_ref[n * rank_width : (n + 1) * rank_width, :] = accs[n].astype(BF16)


def near_kernel(vh, place_ref, field_ref, own_ref, peer_ref, out_ref):
    slab, rows, leaves = own_ref.shape
    halves = 2
    voxels = rows // halves
    group = 6
    for half in range(halves):
        span = slice(half * voxels, (half + 1) * voxels)
        for first in range(0, vh, group):
            accs = [jnp.zeros((voxels, leaves), F32) for _ in range(group)]
            for slice_of, ref in enumerate((own_ref, peer_ref)):
                accs = mac_rows(
                    slab,
                    lambda p, ref=ref: ref[p, span, :].astype(F32),
                    lambda p, n, s=slice_of, first=first: field_ref[
                        s, pl.ds(p * vh + first + n, 1), :
                    ],
                    accs,
                    4,
                )
            for n in range(group):
                start = half * vh * voxels + (first + n) * voxels
                out_ref[start : start + voxels, :] = accs[n].astype(out_ref.dtype)


def near_sum_kernel(ids_ref, keep_ref, *refs):
    recvs, mine_ref, send_ref = refs[:-2], refs[-2], refs[-1]
    count = mine_ref.shape[0]
    parity = ids_ref[2]

    def summed(start):
        start = pl.multiple_of(start, count)
        total = keep_ref[pl.ds(start, count), :]
        for ref in recvs:
            total = total + ref[pl.ds(start, count), :].astype(F32)
        return total

    mine_ref[...] = summed(parity * count)
    send_ref[...] = summed((1 - parity) * count).astype(BF16)


def out_kernel(lvls, vh, vs, ids_ref, column_ref, near_mine, near_peer, *refs):
    blocks, out_ref, rows_scr, out_scr = refs[: 2 * lvls], refs[-3], refs[-2], refs[-1]
    rank_width, voxels, leaves = column_ref.shape
    vectors = out_ref.shape[1]
    lvl, parity = ids_ref[1], ids_ref[2]
    for b, ref in enumerate(blocks):
        rows_scr[b] = ref[...].astype(F32)
    for t in range(lvls):
        first = (lvl ^ t) * vs
        accs = mac_rows(
            rank_width,
            lambda k: column_ref[k].astype(F32),
            lambda k, n: rows_scr[
                (n // vs) * lvls + t, pl.ds((n % vs) * rank_width + k, 1), :
            ],
            [jnp.zeros((voxels, leaves), F32) for _ in range(2 * vs)],
            4,
        )
        for n in range(2 * vs):
            rep = n // vs
            place = first + n % vs
            near_ref = (near_mine, near_peer)[rep]

            def store(n=n, rep=rep, place=place, near_ref=near_ref):
                start = pl.multiple_of(place * voxels, voxels)
                near = near_ref[pl.ds(start, voxels), :].astype(F32)
                vector = place * 2 + (parity if rep == 0 else 1 - parity)
                out_scr[pl.ds(vector, voxels, stride=vectors), :] = accs[n] + near

            if lvls * vs == vh:
                store()
            else:
                pl.when(place < vh)(store)
    out_ref[...] = out_scr[...].reshape(voxels, vectors, leaves).astype(BF16)


def per_device(sizes, *args):
    (
        voxel_field, row_basis, near_block, up_transfer, coupling, parent_coupling,
        down_transfer, column_basis, parent_perm, partner_owner, partner_local,
        parent_owner, parent_local, block_count,
    ) = args
    owners, lvls, reps = sizes
    slab, vectors, leaves = voxel_field.shape
    rank_width = row_basis.shape[1]
    parents = parent_coupling.shape[4]
    children = leaves // parents
    slot_dev = partner_owner.shape[2]
    pslot_dev = parent_owner.shape[2]
    vh = vectors // reps
    vs = -(-vh // lvls)
    high_count = rank_width // children
    sds = jax.ShapeDtypeStruct

    me = lax.axis_index("clus")
    lvl = lax.axis_index("lvl")
    parity = lax.axis_index("rep")
    ids = jnp.stack([me, lvl, parity]).astype(jnp.int32)

    def swap(value, axis, count, step):
        return lax.ppermute(value, axis, [(i, i ^ step) for i in range(count)])

    def other(value):
        return swap(value, "rep", reps, 1)

    with jax.named_scope("swap_cores"):
        field_peer = other(voxel_field)
        row_peer = other(row_basis)

    chunk_rows = 2 * (slab // owners) * vh
    with jax.named_scope("pack_field"):
        packed = pl.pallas_call(
            functools.partial(pack_kernel, owners, vh),
            out_shape=[sds((owners, chunk_rows, leaves), BF16)],
            in_specs=[smem(), smem(), vmem(), vmem()],
            out_specs=[vmem()],
            scratch_shapes=[
                pltpu.VMEM((2, slab * vectors, leaves), F32),
                pltpu.SMEM((owners,), jnp.int32),
            ],
            compiler_params=params(),
            cost_estimate=cost(2 * 768 * 128 * 512, 800000),
        )(parent_perm, ids, voxel_field, field_peer)[0]
    with jax.named_scope("regroup_sends"):
        chunks = [packed[0]] + [swap(packed[s], "clus", owners, s) for s in range(1, owners)]
    with jax.named_scope("place_codes"):
        codes = pl.pallas_call(
            functools.partial(place_kernel, owners, children),
            out_shape=sds((8, leaves), jnp.int32),
            in_specs=[smem(), smem()],
            out_specs=vmem(),
            scratch_shapes=[
                pltpu.SMEM((parents + 1,), jnp.int32),
                pltpu.SMEM((owners,), jnp.int32),
            ],
            compiler_params=params(),
        )(parent_perm, ids)

    with jax.named_scope("partner_codes"):
        group = lvl * reps + parity
        slot_number = group * slot_dev + jnp.arange(slot_dev, dtype=jnp.int32)[:, None]
        live = slot_number < block_count[None, :]
        leaf_code = (partner_owner[0] ^ me).T * leaves + partner_local[0].T
        leaf_code = jnp.where(live, leaf_code, -1)
        up_code = (parent_owner[0] ^ me).T * leaves + parent_local[0].T * children
        up_code = (up_code[:, :, None] + jnp.arange(children, dtype=jnp.int32)).reshape(
            pslot_dev, leaves
        )
        both = jnp.concatenate([leaf_code, up_code], axis=0)
        both_peer = other(both)
        leaf_code = jnp.concatenate([both[:slot_dev], both_peer[:slot_dev]], axis=0)
        up_code = jnp.concatenate([both[slot_dev:], both_peer[slot_dev:]], axis=0)
    slots, pslots = 2 * slot_dev, 2 * pslot_dev
    with jax.named_scope("partner_tables"):
        leaf_table, parent_table, spread = pl.pallas_call(
            functools.partial(table_kernel, children),
            out_shape=[
                sds((owners * leaves, slots * leaves), BF16),
                sds((owners * leaves, pslots * leaves), BF16),
                sds((leaves, children * leaves), BF16),
            ],
            in_specs=[vmem(), vmem()],
            out_specs=[vmem(), vmem(), vmem()],
            compiler_params=params(),
        )(leaf_code, up_code)

    with jax.named_scope("coupling_layout"):
        couple = jnp.moveaxis(coupling[:, :, 0], 2, 0)
        couple_all = jnp.concatenate([couple, other(couple)], axis=0)
        pcouple = parent_coupling[:, :, 0].reshape(
            rank_width, high_count, children, pslot_dev, parents
        )
        pcouple = jnp.transpose(pcouple, (3, 0, 1, 4, 2)).reshape(
            pslot_dev, rank_width, high_count, leaves
        )
        pcouple_all = jnp.concatenate([pcouple, other(pcouple)], axis=0).astype(F32)
        near_other = other(near_block)

    with jax.named_scope("leaf_coeffs"):
        outs = pl.pallas_call(
            functools.partial(coeff_kernel, owners, lvls, vh, vs),
            out_shape=[
                sds((2, slab * vh, leaves), F32),
                sds((vs * rank_width, leaves), F32),
            ]
            + [sds((vs * rank_width, leaves), BF16)] * (lvls - 1),
            in_specs=[smem(), vmem()] + [vmem()] * (owners + 2),
            out_specs=[vmem()] * (lvls + 1),
            compiler_params=params(),
            cost_estimate=cost(4 * 25 * 10**6, 3000000),
        )(ids, codes, *chunks, row_basis, row_peer)
    field, keep, sends = outs[0], outs[1], outs[2:]
    with jax.named_scope("coeff_sends"):
        recvs = [swap(sends[t - 1], "lvl", lvls, t) for t in range(1, lvls)]
    block_rows = packed_rows(vs, rank_width, children)
    with jax.named_scope("parent_coeffs"):
        block = pl.pallas_call(
            functools.partial(up_kernel, vs, children),
            out_shape=sds((block_rows, leaves), BF16),
            in_specs=[vmem()] * (lvls + 1),
            out_specs=vmem(),
            scratch_shapes=[pltpu.VMEM((vs * rank_width, leaves), F32)],
            compiler_params=params(),
            cost_estimate=cost(10**7, 1500000),
        )(keep, *recvs, up_transfer)

    def near_part(t):
        with jax.named_scope("self_blocks"):
            return pl.pallas_call(
                functools.partial(near_kernel, vh),
                out_shape=sds((2 * vh * slab, leaves), F32 if t == 0 else BF16),
                grid_spec=pltpu.PrefetchScalarGridSpec(
                    num_scalar_prefetch=1,
                    grid=(1,),
                    in_specs=[
                        pl.BlockSpec((2, slab * vh, leaves), lambda i, place: (0, 0, 0)),
                        pl.BlockSpec((slab, 2 * slab, leaves), lambda i, place: (0, place[0], 0)),
                        pl.BlockSpec((slab, 2 * slab, leaves), lambda i, place: (0, place[0], 0)),
                    ],
                    out_specs=pl.BlockSpec((2 * vh * slab, leaves), lambda i, place: (0, 0)),
                ),
                compiler_params=params(),
                cost_estimate=cost(4 * 25 * 10**6, 2000000),
            )((lvl ^ t).reshape(1).astype(jnp.int32), field, near_block, near_other)

    near_parts = [near_part(t) for t in range(lvls)]

    with jax.named_scope("owner_sends"):
        blocks = [block] + [swap(block, "clus", owners, s) for s in range(1, owners)]
        mine = jnp.concatenate(blocks, axis=0)
    with jax.named_scope("level_sends"):
        alls = [mine] + [swap(mine, "lvl", lvls, t) for t in range(1, lvls)]

    with jax.named_scope("self_sends"):
        near_recvs = [swap(near_parts[t], "lvl", lvls, t) for t in range(1, lvls)]
        near_mine, near_send = pl.pallas_call(
            near_sum_kernel,
            out_shape=[sds((vh * slab, leaves), F32), sds((vh * slab, leaves), BF16)],
            in_specs=[smem()] + [vmem()] * lvls,
            out_specs=[vmem()] * 2,
            compiler_params=params(),
            cost_estimate=cost(10**6, 2500000),
        )(ids, near_parts[0], *near_recvs)
        near_peer = other(near_send)

    def far_part(t):
        with jax.named_scope("coupling_products"):
            return pl.pallas_call(
                functools.partial(far_kernel, owners, vs, children),
                out_shape=sds((block_rows, leaves), F32 if t == 0 else BF16),
                grid=(slots,),
                in_specs=[
                    pl.BlockSpec(leaf_table.shape, lambda i: (0, 0)),
                    pl.BlockSpec(parent_table.shape, lambda i: (0, 0)),
                    pl.BlockSpec(spread.shape, lambda i: (0, 0)),
                    pl.BlockSpec(mine.shape, lambda i: (0, 0)),
                    pl.BlockSpec((1, rank_width, rank_width, leaves), lambda i: (i, 0, 0, 0)),
                    pl.BlockSpec((1, rank_width, high_count, leaves), lambda i: (i, 0, 0, 0)),
                ],
                out_specs=pl.BlockSpec((block_rows, leaves), lambda i: (0, 0)),
                scratch_shapes=[
                    pltpu.VMEM((slots, vs * rank_width, leaves), F32),
                    pltpu.VMEM((pslots, children, block_rows - vs * rank_width, leaves), F32),
                    pltpu.VMEM((vs * rank_width, leaves), F32),
                    pltpu.VMEM((block_rows - vs * rank_width, leaves), F32),
                ],
                compiler_params=params(),
                cost_estimate=cost(4 * 25 * 10**6, 5000000),
            )(leaf_table, parent_table, spread, alls[t], couple_all, pcouple_all)

    far_parts = [far_part(t) for t in range(lvls)]
    with jax.named_scope("far_sends"):
        far_recvs = [swap(far_parts[t], "lvl", lvls, t) for t in range(1, lvls)]
    with jax.named_scope("down_products"):
        far = pl.pallas_call(
            functools.partial(down_kernel, vs, children),
            out_shape=sds((vs * rank_width, leaves), BF16),
            in_specs=[vmem()] * (lvls + 2),
            out_specs=vmem(),
            scratch_shapes=[
                pltpu.VMEM((children, block_rows - vs * rank_width, leaves), F32)
            ],
            compiler_params=params(),
            cost_estimate=cost(10**7, 1500000),
        )(spread, far_parts[0], *far_recvs, down_transfer)
    with jax.named_scope("far_coeff_sends"):
        far_blocks = [far] + [swap(far, "lvl", lvls, t) for t in range(1, lvls)]
        far_others = [other(value) for value in far_blocks]
    with jax.named_scope("column_products"):
        return pl.pallas_call(
            functools.partial(out_kernel, lvls, vh, vs),
            out_shape=sds((slab, vectors, leaves), BF16),
            in_specs=[smem()] + [vmem()] * (3 + 2 * lvls),
            out_specs=vmem(),
            scratch_shapes=[
                pltpu.VMEM((2 * lvls, vs * rank_width, leaves), F32),
                pltpu.VMEM((slab * vectors, leaves), F32),
            ],
            compiler_params=params(),
            cost_estimate=cost(4 * 25 * 10**6, 3000000),
        )(ids, column_basis, near_mine, near_peer, *far_blocks, *far_others)


def solution(mesh):
    sizes = (mesh.shape["clus"], mesh.shape["lvl"], mesh.shape["rep"])
    return jax.shard_map(
        functools.partial(per_device, sizes),
        mesh=mesh,
        in_specs=(
            P(("lvl", "rep"), None, ("parts", "clus")),
            P(("lvl", "rep"), None, ("parts", "clus")),
            P(("lvl", "rep"), None, ("parts", "clus")),
            P(None, None, ("parts", "clus")),
            P(None, None, ("lvl", "rep"), None, ("parts", "clus")),
            P(None, None, ("lvl", "rep"), None, ("parts", "clus")),
            P(None, None, ("parts", "clus")),
            P(None, ("lvl", "rep"), ("parts", "clus")),
            P("parts"),
            P(("lvl", "rep"), ("parts", "clus"), None),
            P(("lvl", "rep"), ("parts", "clus"), None),
            P(("lvl", "rep"), ("parts", "clus"), None),
            P(("lvl", "rep"), ("parts", "clus"), None),
            P(("parts", "clus")),
        ),
        out_specs=P(("lvl", "rep"), None, ("parts", "clus")),
        check_vma=False,
    )
```

```python
import functools

import jax
import jax.numpy as jnp
from jax import lax
from jax.experimental import pallas as pl
from jax.experimental.pallas import tpu as pltpu
from jax.sharding import PartitionSpec as P

F32 = jnp.float32
BF16 = jnp.bfloat16
VMEM_LIMIT = 12 * 1024 * 1024


def vmem():
    return pl.BlockSpec(memory_space=pltpu.VMEM)


def smem():
    return pl.BlockSpec(memory_space=pltpu.SMEM)


def params(**more):
    return pltpu.CompilerParams(vmem_limit_bytes=VMEM_LIMIT, **more)


def cost(flops, nbytes):
    return pl.CostEstimate(flops=flops, bytes_accessed=nbytes, transcendentals=0)


def iota(shape, dim):
    return lax.broadcasted_iota(jnp.int32, shape, dim)


def row_of(ref, row):
    return ref[pl.ds(row, 1), :]


def mac_rows(total_steps, weight_at, row_at, accs, unroll):
    def body(step, carry):
        weight = weight_at(step)
        return tuple(acc + weight * row_at(step, n) for n, acc in enumerate(carry))

    return lax.fori_loop(0, total_steps, body, tuple(accs), unroll=unroll)


def pack_kernel(owners, vh, parents, ids_ref, own_ref, out_ref, rows_scr):
    slab, vectors, leaves = own_ref.shape
    children = leaves // parents
    reps = vectors // vh
    width = leaves // owners
    me, parity = ids_ref[0], ids_ref[2]
    row = iota((leaves, leaves), 0)
    lane = iota((leaves, leaves), 1)
    parent_of_row = row // children
    target = row % children
    bits = 32 // owners
    counts = jnp.int32(0)
    for parent in range(parents):
        owner = ids_ref[3 + me * parents + parent] // parents
        shift = owner * bits
        rank = lax.shift_right_logical(counts, shift) & ((1 << bits) - 1)
        counts = counts + lax.shift_left(jnp.int32(1), shift)
        code = (owner ^ me) * leaves + rank * children
        target = target + jnp.where(parent_of_row == parent, code, 0)
    part = (slab // owners) * vh
    rows_scr[...] = own_ref[...].reshape(slab * vectors, leaves).astype(F32)
    pieces = []
    for q in range(owners):
        start = q * (slab // owners) * vectors
        pieces.append(
            jnp.concatenate(
                [
                    rows_scr[pl.ds(start + first, part, stride=reps), :]
                    for first in (parity, 1 - parity)
                ],
                axis=0,
            ).astype(BF16)
        )
    for s in range(owners):
        total = jnp.zeros((2 * part, leaves), F32)
        for q in range(owners):
            onehot = jnp.where(target + (q * width - s * leaves) == lane, 1.0, 0.0).astype(BF16)
            total = total + jnp.dot(pieces[q], onehot, preferred_element_type=F32)
        out_ref[s] = total.astype(BF16)


def place_kernel(owners, parents, ids_ref, out_ref, code_scr):
    leaves = out_ref.shape[1]
    children = leaves // parents
    me = ids_ref[0]
    for source in range(owners):
        rank = jnp.int32(0)
        base = (source ^ me) * leaves
        for parent in range(parents):
            place = ids_ref[3 + source * parents + parent]
            mine = (place // parents) == me
            slot = jnp.where(mine, place % parents, parents)
            code_scr[slot] = base + rank * children
            rank = rank + jnp.where(mine, 1, 0)
    lane = iota(out_ref.shape, 1)
    code = lane % children
    for parent in range(parents):
        code = code + jnp.where(lane // children == parent, code_scr[parent], 0)
    out_ref[...] = code


def regroup_kernel(owners, code_ref, *refs):
    chunks, mine_ref, other_ref = refs[:owners], refs[owners], refs[owners + 1]
    leaves = mine_ref.shape[1]
    width = leaves // owners
    part = mine_ref.shape[0] // owners
    code = jnp.broadcast_to(code_ref[0:1, :], (leaves, leaves))
    row = iota((leaves, leaves), 0)
    for q in range(owners):
        total = jnp.zeros((2 * part, leaves), F32)
        for s in range(owners):
            onehot = jnp.where(code + (q * width - s * leaves) == row, 1.0, 0.0).astype(BF16)
            total = total + jnp.dot(chunks[s][...], onehot, preferred_element_type=F32)
        mine_ref[q * part : (q + 1) * part, :] = total[:part]
        other_ref[q * part : (q + 1) * part, :] = total[part:].astype(BF16)


def coeff_products(lvl, lvls, vh, vs, basis_ref, field_ref, start_of, finish):
    slab, rank_width, leaves = basis_ref.shape
    for t in range(lvls):
        first = (lvl ^ t) * vs
        accs = mac_rows(
            slab,
            lambda m: basis_ref[m].astype(F32),
            lambda m, n: row_of(field_ref, m * vh + jnp.minimum(first + n, vh - 1)),
            [start_of(t, n) for n in range(vs)],
            8,
        )
        for n in range(vs):
            finish(t, n, accs[n])


def coeff_own_kernel(lvls, vh, vs, ids_ref, basis_ref, field_ref, out_ref):
    rank_width, leaves = basis_ref.shape[1:]

    def finish(t, n, acc):
        start = (t * vs + n) * rank_width
        out_ref[start : start + rank_width, :] = acc

    coeff_products(
        ids_ref[1], lvls, vh, vs, basis_ref, field_ref,
        lambda t, n: jnp.zeros((rank_width, leaves), F32), finish,
    )


def coeff_peer_kernel(
    lvls, vh, vs, ids_ref, basis_ref, field_ref, own_ref, wide_ref, keep_ref, *sends
):
    rank_width = basis_ref.shape[1]
    wide_ref[...] = field_ref[...].astype(F32)

    def start_of(t, n):
        start = (t * vs + n) * rank_width
        return own_ref[start : start + rank_width, :]

    def finish(t, n, acc):
        block = slice(n * rank_width, (n + 1) * rank_width)
        if t == 0:
            keep_ref[block, :] = acc
        else:
            sends[t - 1][block, :] = acc.astype(BF16)

    coeff_products(ids_ref[1], lvls, vh, vs, basis_ref, wide_ref, start_of, finish)


def packs(vs, rank_width, leaves):
    per = max(1, leaves // rank_width)
    return [list(range(first, min(first + per, vs))) for first in range(0, vs, per)]


def up_kernel(vs, parents, keep_ref, *refs):
    recvs, up_ref, out_ref, coeff_scr = refs[:-3], refs[-3], refs[-2], refs[-1]
    rank_width, _, leaves = up_ref.shape
    total = keep_ref[...]
    for ref in recvs:
        total = total + ref[...].astype(F32)
    coeffs = total.astype(BF16)
    out_ref[0 : vs * rank_width, :] = coeffs
    coeff_scr[...] = coeffs.astype(F32)
    accs = mac_rows(
        rank_width,
        lambda j: up_ref[j].astype(F32),
        lambda j, n: row_of(coeff_scr, n * rank_width + j),
        [jnp.zeros((rank_width, leaves), F32) for _ in range(vs)],
        8,
    )
    mine = (iota((parents, leaves), 1) // (leaves // parents)) == iota((parents, leaves), 0)
    group = jnp.where(mine, 1.0, 0.0).astype(BF16)
    for b, members in enumerate(packs(vs, rank_width, leaves)):
        sums = []
        for n in members:
            rest, result = accs[n], jnp.zeros((parents, rank_width), F32)
            for _ in range(3):
                piece = rest.astype(BF16)
                result = result + lax.dot_general(
                    group, piece, (((1,), (1,)), ((), ())), preferred_element_type=F32
                )
                rest = rest - piece.astype(F32)
            sums.append(result)
        missing = leaves - len(sums) * rank_width
        if missing:
            sums.append(jnp.zeros((parents, missing), F32))
        start = vs * rank_width + b * parents
        out_ref[start : start + parents, :] = jnp.concatenate(sums, axis=1).astype(BF16)


def table_kernel(
    owners, parents, slots, own_codes, peer_codes, own_ref, peer_ref,
    leaf_out, parent_out, couple_out, rows_scr,
):
    leaves = own_codes.shape[1]
    sources = leaf_out.shape[0]
    count = parent_out.shape[0] // 2
    for half, codes in enumerate((own_codes, peer_codes)):
        for i in range(slots):
            hit = jnp.broadcast_to(codes[i : i + 1, :], (sources, leaves)) == iota(
                (sources, leaves), 0
            )
            start = (half * slots + i) * leaves
            leaf_out[:, start : start + leaves] = jnp.where(hit, 1.0, 0.0).astype(BF16)
        uppers = owners * parents
        same = iota((uppers, uppers), 0) == iota((uppers, uppers), 1)
        same = jnp.where(same, 1.0, 0.0).astype(BF16)
        pslots = count // parents
        for i in range(pslots):
            code = jnp.broadcast_to(codes[slots + i : slots + i + 1, :], (uppers, leaves))
            hit = jnp.where(code == iota(code.shape, 0), 1.0, 0.0).astype(BF16)
            turned = lax.dot_general(
                hit, same, (((0,), (0,)), ((), ())), preferred_element_type=F32
            )
            start = half * count + i * parents
            parent_out[start : start + parents, :] = turned[:parents].astype(BF16)
    rank_width, pslots = own_ref.shape[0], own_ref.shape[1] // parents
    for half, ref in enumerate((own_ref, peer_ref)):
        rows_scr[...] = ref[...].reshape(rank_width * pslots * parents, rank_width).astype(F32)
        for i in range(pslots):
            place = (half * pslots + i) * rank_width
            for parent in range(parents):
                block = rows_scr[pl.ds(i * parents + parent, rank_width, stride=pslots * parents), :]
                couple_out[parent, place : place + rank_width, :] = block.astype(BF16)


def far_kernel(owners, vs, pslots, leaf_table, parent_table, pcouple_ref, block_ref, *refs):
    extras = refs[:-8]
    own_ref, peer_any, out_ref, rows_scr, prows_scr, pout_scr, couple_scr, sems = refs[-8:]
    slots, rank_width, _, leaves = own_ref.shape
    parents = pcouple_ref.shape[0]
    copies = []
    for i in range(slots):
        copies.append(pltpu.make_async_copy(peer_any.at[i], couple_scr.at[i], sems.at[i]))
        copies[-1].start()
    per_block = block_ref.shape[0] // owners
    mine = vs * rank_width
    rows = jnp.zeros((mine, 2 * slots * leaves), F32)
    for o in range(0, owners, 2):
        pair = [block_ref[p * per_block : p * per_block + mine, :] for p in (o, o + 1)]
        rows = rows + jnp.dot(
            jnp.concatenate(pair, axis=1),
            leaf_table[o * leaves : (o + 2) * leaves, :],
            preferred_element_type=F32,
        )
    for i in range(2 * slots):
        rows_scr[i] = rows[:, i * leaves : (i + 1) * leaves]

    for b, members in enumerate(packs(vs, rank_width, leaves)):
        source = jnp.concatenate(
            [
                block_ref[pl.ds(o * per_block + mine + b * parents, parents), :]
                for o in range(owners)
            ],
            axis=0,
        )
        picked = jnp.dot(parent_table[...], source, preferred_element_type=F32)
        for i in range(2 * pslots):
            for k, n in enumerate(members):
                prows_scr[:, n, i * rank_width : (i + 1) * rank_width] = picked[
                    i * parents : (i + 1) * parents, k * rank_width : (k + 1) * rank_width
                ]
    for parent in range(parents):
        pout_scr[parent] = jnp.dot(
            prows_scr[parent].astype(BF16), pcouple_ref[parent], preferred_element_type=F32
        )
    for b, members in enumerate(packs(vs, rank_width, leaves)):
        parts = [pout_scr[:, n, :] for n in members]
        missing = leaves - len(parts) * rank_width
        if missing:
            parts.append(jnp.zeros((parents, missing), F32))
        out_ref[mine + b * parents : mine + (b + 1) * parents, :] = jnp.concatenate(
            parts, axis=1
        ).astype(out_ref.dtype)
    start = mine + len(packs(vs, rank_width, leaves)) * parents
    for ref in extras:
        out_ref[start : start + ref.shape[0], :] = ref[...]
        start += ref.shape[0]

    accs = [jnp.zeros((rank_width, leaves), F32) for _ in range(vs)]
    for s in range(2 * slots):
        if s >= slots:
            copies[s - slots].wait()
        ref, i = (own_ref, s) if s < slots else (couple_scr, s - slots)
        accs = mac_rows(
            rank_width,
            lambda j, ref=ref, i=i: ref[i, j].astype(F32),
            lambda j, n, s=s: rows_scr[s, pl.ds(n * rank_width + j, 1), :],
            accs,
            8,
        )
    for n in range(vs):
        out_ref[n * rank_width : (n + 1) * rank_width, :] = accs[n].astype(out_ref.dtype)


def down_kernel(vs, parents, keep_ref, *refs):
    recvs, down_ref, out_ref, rows_scr = refs[:-3], refs[-3], refs[-2], refs[-1]
    rank_width, _, leaves = down_ref.shape
    total = keep_ref[...]
    for ref in recvs:
        total = total + ref[0 : total.shape[0], :].astype(F32)
    mine = vs * rank_width
    below = (iota((parents, leaves), 1) // (leaves // parents)) == iota((parents, leaves), 0)
    spread = jnp.where(below, 1.0, 0.0).astype(BF16)
    for b, members in enumerate(packs(vs, rank_width, leaves)):
        part = total[mine + b * parents : mine + (b + 1) * parents, :].astype(BF16)
        wide = lax.dot_general(
            part, spread, (((0,), (0,)), ((), ())), preferred_element_type=F32
        )
        count = len(members) * rank_width
        start = members[0] * rank_width
        rows_scr[start : start + count, :] = wide[:count]
    accs = mac_rows(
        rank_width,
        lambda j: down_ref[j].astype(F32),
        lambda j, n: row_of(rows_scr, n * rank_width + j),
        [total[n * rank_width : (n + 1) * rank_width, :] for n in range(vs)],
        8,
    )
    for n in range(vs):
        out_ref[n * rank_width : (n + 1) * rank_width, :] = accs[n].astype(BF16)


def near_kernel(
    vh, step, ids_ref, own_field, peer_field, own_ref, peer_any, out_ref, peer_scr, acc_scr, sem
):
    slab, _, leaves = own_ref.shape
    group = 6
    target = pl.multiple_of((ids_ref[1] ^ step) * (2 * slab), 2 * slab)
    copy = pltpu.make_async_copy(peer_any.at[:, pl.ds(target, 2 * slab), :], peer_scr, sem)
    copy.start()

    def products(field_ref, ref, base, first, half, accs):
        span = pl.ds(pl.multiple_of(base + half * slab, slab), slab)
        return mac_rows(
            slab,
            lambda p: ref[p, span, :].astype(F32),
            lambda p, n: row_of(field_ref, p * vh + first + n),
            accs,
            8,
        )

    places = [(half, first) for half in range(2) for first in range(0, vh, group)]
    for half, first in places:
        accs = [jnp.zeros((slab, leaves), F32) for _ in range(group)]
        accs = products(own_field, own_ref, target, first, half, accs)
        for n in range(group):
            start = (half * vh + first + n) * slab
            acc_scr[start : start + slab, :] = accs[n]
    copy.wait()
    for half, first in places:
        starts = [(half * vh + first + n) * slab for n in range(group)]
        accs = [acc_scr[start : start + slab, :] for start in starts]
        accs = products(peer_field, peer_scr, 0, first, half, accs)
        for n, start in enumerate(starts):
            out_ref[start : start + slab, :] = accs[n].astype(out_ref.dtype)


def near_sum_kernel(skip, ids_ref, keep_ref, *refs):
    recvs, mine_ref, send_ref = refs[:-2], refs[-2], refs[-1]
    count = mine_ref.shape[0]
    parity = ids_ref[2]

    def summed(start):
        start = pl.multiple_of(start, 16)
        total = keep_ref[pl.ds(start, count), :]
        for ref in recvs:
            total = total + ref[pl.ds(skip + start, count), :].astype(F32)
        return total

    mine_ref[...] = summed(parity * count)
    send_ref[...] = summed((1 - parity) * count).astype(BF16)


def column_kernel(vs, column_ref, mine_ref, other_ref, out_ref, rows_scr):
    rank_width, voxels, leaves = column_ref.shape
    rows_scr[0] = mine_ref[...].astype(F32)
    rows_scr[1] = other_ref[...].astype(F32)
    accs = mac_rows(
        rank_width,
        lambda k: column_ref[k].astype(F32),
        lambda k, n: rows_scr[n // vs, pl.ds((n % vs) * rank_width + k, 1), :],
        [jnp.zeros((voxels, leaves), F32) for _ in range(2 * vs)],
        8,
    )
    for n in range(2 * vs):
        out_ref[n * voxels : (n + 1) * voxels, :] = accs[n]


def out_kernel(lvls, vh, vs, early, ids_ref, column_ref, near_mine, near_peer, *refs):
    done, blocks = refs[:early], refs[early : -3]
    out_ref, rows_scr, out_scr = refs[-3:]
    rank_width, voxels, leaves = column_ref.shape
    vectors = out_ref.shape[1]
    lvl, parity = ids_ref[1], ids_ref[2]
    late = lvls - early
    for b, ref in enumerate(blocks):
        rows_scr[b] = ref[...].astype(F32)

    def store(place, rep, value):
        def write():
            vector = place * 2 + (parity if rep == 0 else 1 - parity)
            out_scr[pl.ds(vector, voxels, stride=vectors), :] = value

        if lvls * vs == vh:
            write()
        else:
            pl.when(place < vh)(write)

    for t in range(lvls):
        first = (lvl ^ t) * vs
        if t < early:
            accs = [done[t][n * voxels : (n + 1) * voxels, :] for n in range(2 * vs)]
        else:
            accs = mac_rows(
                rank_width,
                lambda k: column_ref[k].astype(F32),
                lambda k, n: rows_scr[
                    (n // vs) * late + t - early, pl.ds((n % vs) * rank_width + k, 1), :
                ],
                [jnp.zeros((voxels, leaves), F32) for _ in range(2 * vs)],
                8,
            )
        for n in range(2 * vs):
            place = first + n % vs
            near_ref = (near_mine, near_peer)[n // vs]
            inside = jnp.minimum(place, vh - 1)
            near = near_ref[pl.ds(pl.multiple_of(inside * voxels, voxels), voxels), :]
            store(place, n // vs, accs[n] + near.astype(F32))
    out_ref[...] = out_scr[...].reshape(voxels, vectors, leaves).astype(BF16)


def after(value, *others):
    return lax.optimization_barrier((value,) + others)[0]


def per_device(sizes, *args):
    (
        voxel_field, row_basis, near_block, up_transfer, coupling, parent_coupling,
        down_transfer, column_basis, parent_perm, partner_owner, partner_local,
        parent_owner, parent_local, block_count,
    ) = args
    owners, lvls, reps = sizes
    slab, vectors, leaves = voxel_field.shape
    rank_width = row_basis.shape[1]
    parents = parent_coupling.shape[4]
    children = leaves // parents
    slots = partner_owner.shape[2]
    pslots = parent_owner.shape[2]
    vh = vectors // reps
    vs = -(-vh // lvls)
    sds = jax.ShapeDtypeStruct

    me = lax.axis_index("clus")
    lvl = lax.axis_index("lvl")
    parity = lax.axis_index("rep")
    ids = jnp.concatenate([jnp.stack([me, lvl, parity]).astype(jnp.int32), parent_perm])

    def call(name, kernel, ins, outs, scratch=(), us=1.0, scalars=0, whole=()):
        specs = [
            smem() if i < scalars else pl.BlockSpec(memory_space=pltpu.HBM) if i in whole else vmem()
            for i in range(len(ins))
        ]
        with jax.named_scope(name):
            return pl.pallas_call(
                kernel,
                out_shape=outs,
                in_specs=specs,
                out_specs=jax.tree.map(lambda _: vmem(), outs),
                scratch_shapes=list(scratch),
                compiler_params=params(),
                cost_estimate=cost(0, int(us * 3.3e6)),
            )(*ins)

    def swap(value, axis, count, step):
        return lax.ppermute(value, axis, [(i, i ^ step) for i in range(count)])

    def other(value):
        return swap(value, "rep", reps, 1)

    with jax.named_scope("swap_row_basis"):
        row_peer = other(row_basis)
    with jax.named_scope("swap_parent_coupling"):
        pcouple = jnp.transpose(parent_coupling, (0, 2, 3, 4, 1)).reshape(
            rank_width, pslots * parents, rank_width
        )
        pcouple_peer = other(pcouple)
    with jax.named_scope("swap_self_blocks"):
        near_peer_block = other(near_block)

    chunk_rows = 2 * (slab // owners) * vh
    packed = call(
        "pack_field",
        functools.partial(pack_kernel, owners, vh, parents),
        (ids, voxel_field),
        sds((owners, chunk_rows, leaves), BF16),
        [pltpu.VMEM((slab * vectors, leaves), F32)],
        1.0, scalars=1,
    )
    with jax.named_scope("regroup_sends"):
        chunks = [packed[0]] + [swap(packed[s], "clus", owners, s) for s in range(1, owners)]
    codes = call(
        "place_codes",
        functools.partial(place_kernel, owners, parents),
        (after(ids, chunks[1]),),
        sds((8, leaves), jnp.int32),
        [pltpu.SMEM((parents + 1,), jnp.int32)],
        0.3, scalars=1,
    )
    with jax.named_scope("coupling_layout"):
        couple = jnp.moveaxis(after(coupling, chunks[1])[:, :, 0], 2, 0)

    codes = after(codes, couple, row_peer)

    field, field_send = call(
        "regroup_field",
        functools.partial(regroup_kernel, owners),
        (codes, *chunks),
        [sds((slab * vh, leaves), F32), sds((slab * vh, leaves), BF16)],
        (), 0.4,
    )
    with jax.named_scope("swap_field"):
        field_recv = other(field_send)
    coeff_own = call(
        "coeffs_own_slab",
        functools.partial(coeff_own_kernel, lvls, vh, vs),
        (ids, row_basis, field),
        sds((lvls * vs * rank_width, leaves), F32),
        (), 1.6, scalars=1,
    )
    outs = call(
        "coeffs_other_slab",
        functools.partial(coeff_peer_kernel, lvls, vh, vs),
        (ids, row_peer, field_recv, coeff_own),
        [sds((slab * vh, leaves), F32), sds((vs * rank_width, leaves), F32)]
        + [sds((vs * rank_width, leaves), BF16)] * (lvls - 1),
        (), 1.6, scalars=1,
    )
    field_peer, keep, sends = outs[0], outs[1], outs[2:]
    with jax.named_scope("coeff_sends"):
        recvs = [swap(sends[t - 1], "lvl", lvls, t) for t in range(1, lvls)]

    with jax.named_scope("partner_codes"):
        held = lax.optimization_barrier(
            (partner_owner, partner_local, parent_owner, parent_local, block_count, keep)
        )
        group = lvl * reps + parity
        slot_number = group * slots + jnp.arange(slots, dtype=jnp.int32)[:, None]
        leaf_code = (held[0][0] ^ me).T * leaves + held[1][0].T
        leaf_code = jnp.where(slot_number < held[4][None, :], leaf_code, -1)
        up_code = (held[2][0] ^ me).T * parents + held[3][0].T
        up_code = jnp.pad(up_code, ((0, 0), (0, leaves - parents)), constant_values=-1)
        partners = jnp.concatenate([leaf_code, up_code], axis=0)
        partners_peer = other(partners)
    with jax.named_scope("swap_coupling"):
        couple_peer = other(after(couple, keep))

    def near_part(t, place):
        return call(
            "self_blocks",
            functools.partial(near_kernel, vh, t),
            (ids, place, field_peer, near_block, near_peer_block),
            sds((2 * vh * slab, leaves), F32 if t == 0 else BF16),
            [
                pltpu.VMEM((slab, 2 * slab, leaves), BF16),
                pltpu.VMEM((2 * vh * slab, leaves), F32),
                pltpu.SemaphoreType.DMA,
            ],
            2.4, scalars=1, whole=(4,),
        )

    near_parts = [None] * lvls
    near_parts[1] = near_part(1, after(field, field_peer))
    up_after = after(up_transfer, near_parts[1], partners)

    block_rows = vs * rank_width + len(packs(vs, rank_width, leaves)) * parents
    block = call(
        "parent_coeffs",
        functools.partial(up_kernel, vs, parents),
        (keep, *recvs, up_after),
        sds((block_rows, leaves), BF16),
        [pltpu.VMEM((vs * rank_width, leaves), F32)],
        0.8,
    )
    with jax.named_scope("owner_sends"):
        blocks = [block] + [swap(block, "clus", owners, s) for s in range(1, owners)]
    later = after(field, block)
    for t in range(2, lvls):
        near_parts[t] = near_part(t, later)
    with jax.named_scope("all_owners"):
        blocks = list(lax.optimization_barrier(tuple(blocks) + tuple(near_parts[2:])))[:owners]
        mine = jnp.concatenate(blocks, axis=0)
    with jax.named_scope("level_sends"):
        alls = [mine] + [swap(mine, "lvl", lvls, t) for t in range(1, lvls)]

    near_parts[0] = near_part(0, after(field, mine))
    leaf_table, parent_table, pcouple_all = call(
        "partner_tables",
        functools.partial(table_kernel, owners, parents, slots),
        (after(partners, mine), partners_peer, pcouple, pcouple_peer),
        [
            sds((owners * leaves, 2 * slots * leaves), BF16),
            sds((2 * pslots * parents, owners * parents), BF16),
            sds((parents, 2 * pslots * rank_width, rank_width), BF16),
        ],
        [pltpu.VMEM((rank_width * pslots * parents, rank_width), F32)],
        1.5,
    )
    def far_part(t, block):
        extras = () if t == 0 else (near_parts[t],)
        rows = block_rows if t == 0 else block_rows + 2 * vh * slab
        return call(
            "coupling_products",
            functools.partial(far_kernel, owners, vs, pslots),
            (leaf_table, parent_table, pcouple_all, block, *extras, couple, couple_peer),
            sds((rows, leaves), F32 if t == 0 else BF16),
            [
                pltpu.VMEM((2 * slots, vs * rank_width, leaves), F32),
                pltpu.VMEM((parents, 8, 2 * pslots * rank_width), F32),
                pltpu.VMEM((parents, 8, rank_width), F32),
                pltpu.VMEM((slots, rank_width, rank_width, leaves), BF16),
                pltpu.SemaphoreType.DMA((slots,)),
            ],
            3.2, whole=(5 + len(extras),),
        )

    alls[1] = after(alls[1], near_parts[0])
    far_parts = [far_part(t, alls[t]) for t in range(lvls)]
    with jax.named_scope("far_sends"):
        far_recvs = [swap(far_parts[t], "lvl", lvls, t) for t in range(1, lvls)]
    far = call(
        "down_products",
        functools.partial(down_kernel, vs, parents),
        (far_parts[0], *far_recvs, down_transfer),
        sds((vs * rank_width, leaves), BF16),
        [pltpu.VMEM((vs * rank_width, leaves), F32)],
        0.8,
    )
    with jax.named_scope("far_coeff_sends"):
        far_blocks = [far] + [swap(far, "lvl", lvls, t) for t in range(1, lvls)]
        far_others = [other(value) for value in far_blocks]
    early = lvls - 1
    done = [
        call(
            "column_products_early",
            functools.partial(column_kernel, vs),
            (column_basis, far_blocks[t], far_others[t]),
            sds((2 * vs * slab, leaves), F32),
            [pltpu.VMEM((2, vs * rank_width, leaves), F32)],
            0.5,
        )
        for t in range(early)
    ]
    near_mine, near_send = call(
        "self_sums",
        functools.partial(near_sum_kernel, block_rows),
        (ids, after(near_parts[0], done[0]), *far_recvs),
        [sds((vh * slab, leaves), F32), sds((vh * slab, leaves), BF16)],
        (), 0.65, scalars=1,
    )
    with jax.named_scope("swap_self_sums"):
        near_peer = other(near_send)
    return call(
        "column_products",
        functools.partial(out_kernel, lvls, vh, vs, early),
        (
            ids, column_basis, near_mine, near_peer, *done,
            *far_blocks[early:], *far_others[early:],
        ),
        sds((slab, vectors, leaves), BF16),
        [
            pltpu.VMEM((2 * (lvls - early), vs * rank_width, leaves), F32),
            pltpu.VMEM((slab * vectors, leaves), F32),
        ],
        1.85, scalars=1,
    )


def solution(mesh):
    sizes = (mesh.shape["clus"], mesh.shape["lvl"], mesh.shape["rep"])
    return jax.shard_map(
        functools.partial(per_device, sizes),
        mesh=mesh,
        in_specs=(
            P(("lvl", "rep"), None, ("parts", "clus")),
            P(("lvl", "rep"), None, ("parts", "clus")),
            P(("lvl", "rep"), None, ("parts", "clus")),
            P(None, None, ("parts", "clus")),
            P(None, None, ("lvl", "rep"), None, ("parts", "clus")),
            P(None, None, ("lvl", "rep"), None, ("parts", "clus")),
            P(None, None, ("parts", "clus")),
            P(None, ("lvl", "rep"), ("parts", "clus")),
            P("parts"),
            P(("lvl", "rep"), ("parts", "clus"), None),
            P(("lvl", "rep"), ("parts", "clus"), None),
            P(("lvl", "rep"), ("parts", "clus"), None),
            P(("lvl", "rep"), ("parts", "clus"), None),
            P(("parts", "clus")),
        ),
        out_specs=P(("lvl", "rep"), None, ("parts", "clus")),
        check_vma=False,
    )
```

```python
import functools

import jax
import jax.numpy as jnp
from jax import lax
from jax.experimental import pallas as pl
from jax.experimental.pallas import tpu as pltpu
from jax.sharding import PartitionSpec as P

F32 = jnp.float32
BF16 = jnp.bfloat16
VMEM_LIMIT = 12 * 1024 * 1024


def vmem():
    return pl.BlockSpec(memory_space=pltpu.VMEM)


def smem():
    return pl.BlockSpec(memory_space=pltpu.SMEM)


def params(**more):
    return pltpu.CompilerParams(vmem_limit_bytes=VMEM_LIMIT, **more)


def cost(flops, nbytes):
    return pl.CostEstimate(flops=flops, bytes_accessed=nbytes, transcendentals=0)


def iota(shape, dim):
    return lax.broadcasted_iota(jnp.int32, shape, dim)


def row_of(ref, row):
    return ref[pl.ds(row, 1), :]


def mac_rows(total_steps, weight_at, row_at, accs, unroll):
    def body(step, carry):
        weight = weight_at(step)
        return tuple(acc + weight * row_at(step, n) for n, acc in enumerate(carry))

    return lax.fori_loop(0, total_steps, body, tuple(accs), unroll=unroll)


def pack_kernel(owners, vh, parents, ids_ref, own_ref, out_ref, rows_scr):
    slab, vectors, leaves = own_ref.shape
    children = leaves // parents
    reps = vectors // vh
    width = leaves // owners
    me, parity = ids_ref[0], ids_ref[2]
    row = iota((leaves, leaves), 0)
    lane = iota((leaves, leaves), 1)
    parent_of_row = row // children
    target = row % children
    bits = 32 // owners
    counts = jnp.int32(0)
    for parent in range(parents):
        owner = ids_ref[3 + me * parents + parent] // parents
        shift = owner * bits
        rank = lax.shift_right_logical(counts, shift) & ((1 << bits) - 1)
        counts = counts + lax.shift_left(jnp.int32(1), shift)
        code = (owner ^ me) * leaves + rank * children
        target = target + jnp.where(parent_of_row == parent, code, 0)
    part = (slab // owners) * vh
    rows_scr[...] = own_ref[...].reshape(slab * vectors, leaves).astype(F32)
    pieces = []
    for q in range(owners):
        start = q * (slab // owners) * vectors
        pieces.append(
            jnp.concatenate(
                [
                    rows_scr[pl.ds(start + first, part, stride=reps), :]
                    for first in (parity, 1 - parity)
                ],
                axis=0,
            ).astype(BF16)
        )
    for s in range(owners):
        total = jnp.zeros((2 * part, leaves), F32)
        for q in range(owners):
            onehot = jnp.where(target + (q * width - s * leaves) == lane, 1.0, 0.0).astype(BF16)
            total = total + jnp.dot(pieces[q], onehot, preferred_element_type=F32)
        out_ref[s] = total.astype(BF16)


def place_kernel(owners, parents, ids_ref, out_ref, code_scr):
    leaves = out_ref.shape[1]
    children = leaves // parents
    me = ids_ref[0]
    for source in range(owners):
        rank = jnp.int32(0)
        base = (source ^ me) * leaves
        for parent in range(parents):
            place = ids_ref[3 + source * parents + parent]
            mine = (place // parents) == me
            slot = jnp.where(mine, place % parents, parents)
            code_scr[slot] = base + rank * children
            rank = rank + jnp.where(mine, 1, 0)
    lane = iota(out_ref.shape, 1)
    code = lane % children
    for parent in range(parents):
        code = code + jnp.where(lane // children == parent, code_scr[parent], 0)
    out_ref[...] = code


def regroup_kernel(owners, code_ref, *refs):
    chunks, mine_ref, other_ref = refs[:owners], refs[owners], refs[owners + 1]
    leaves = mine_ref.shape[1]
    width = leaves // owners
    part = mine_ref.shape[0] // owners
    code = jnp.broadcast_to(code_ref[0:1, :], (leaves, leaves))
    row = iota((leaves, leaves), 0)
    for q in range(owners):
        total = jnp.zeros((2 * part, leaves), F32)
        for s in range(owners):
            onehot = jnp.where(code + (q * width - s * leaves) == row, 1.0, 0.0).astype(BF16)
            total = total + jnp.dot(chunks[s][...], onehot, preferred_element_type=F32)
        mine_ref[q * part : (q + 1) * part, :] = total[:part]
        other_ref[q * part : (q + 1) * part, :] = total[part:].astype(BF16)


def coeff_products(lvl, lvls, vh, vs, basis_ref, field_ref, start_of, finish):
    slab, rank_width, leaves = basis_ref.shape
    for t in range(lvls):
        first = (lvl ^ t) * vs
        accs = mac_rows(
            slab,
            lambda m: basis_ref[m].astype(F32),
            lambda m, n: row_of(field_ref, m * vh + jnp.minimum(first + n, vh - 1)),
            [start_of(t, n) for n in range(vs)],
            8,
        )
        for n in range(vs):
            finish(t, n, accs[n])


def coeff_own_kernel(lvls, vh, vs, ids_ref, basis_ref, field_ref, out_ref):
    rank_width, leaves = basis_ref.shape[1:]

    def finish(t, n, acc):
        start = (t * vs + n) * rank_width
        out_ref[start : start + rank_width, :] = acc

    coeff_products(
        ids_ref[1], lvls, vh, vs, basis_ref, field_ref,
        lambda t, n: jnp.zeros((rank_width, leaves), F32), finish,
    )


def coeff_peer_kernel(
    lvls, vh, vs, ids_ref, basis_ref, field_ref, own_ref, wide_ref, keep_ref, *sends
):
    rank_width = basis_ref.shape[1]
    wide_ref[...] = field_ref[...].astype(F32)

    def start_of(t, n):
        start = (t * vs + n) * rank_width
        return own_ref[start : start + rank_width, :]

    def finish(t, n, acc):
        block = slice(n * rank_width, (n + 1) * rank_width)
        if t == 0:
            keep_ref[block, :] = acc
        else:
            sends[t - 1][block, :] = acc.astype(BF16)

    coeff_products(ids_ref[1], lvls, vh, vs, basis_ref, wide_ref, start_of, finish)


def packs(vs, rank_width, leaves):
    per = max(1, leaves // rank_width)
    return [list(range(first, min(first + per, vs))) for first in range(0, vs, per)]


def up_kernel(vs, parents, keep_ref, *refs):
    recvs, up_ref, out_ref, coeff_scr = refs[:-3], refs[-3], refs[-2], refs[-1]
    rank_width, _, leaves = up_ref.shape
    total = keep_ref[...]
    for ref in recvs:
        total = total + ref[...].astype(F32)
    coeffs = total.astype(BF16)
    out_ref[0 : vs * rank_width, :] = coeffs
    coeff_scr[...] = coeffs.astype(F32)
    accs = mac_rows(
        rank_width,
        lambda j: up_ref[j].astype(F32),
        lambda j, n: row_of(coeff_scr, n * rank_width + j),
        [jnp.zeros((rank_width, leaves), F32) for _ in range(vs)],
        8,
    )
    mine = (iota((parents, leaves), 1) // (leaves // parents)) == iota((parents, leaves), 0)
    group = jnp.where(mine, 1.0, 0.0).astype(BF16)
    for b, members in enumerate(packs(vs, rank_width, leaves)):
        sums = []
        for n in members:
            rest, result = accs[n], jnp.zeros((parents, rank_width), F32)
            for _ in range(3):
                piece = rest.astype(BF16)
                result = result + lax.dot_general(
                    group, piece, (((1,), (1,)), ((), ())), preferred_element_type=F32
                )
                rest = rest - piece.astype(F32)
            sums.append(result)
        missing = leaves - len(sums) * rank_width
        if missing:
            sums.append(jnp.zeros((parents, missing), F32))
        start = vs * rank_width + b * parents
        out_ref[start : start + parents, :] = jnp.concatenate(sums, axis=1).astype(BF16)


def table_kernel(
    owners, parents, slots, own_codes, peer_codes, own_ref, peer_ref,
    leaf_out, parent_out, couple_out, rows_scr,
):
    leaves = own_codes.shape[1]
    sources = leaf_out.shape[0]
    count = parent_out.shape[0] // 2
    for half, codes in enumerate((own_codes, peer_codes)):
        for i in range(slots):
            hit = jnp.broadcast_to(codes[i : i + 1, :], (sources, leaves)) == iota(
                (sources, leaves), 0
            )
            start = (half * slots + i) * leaves
            leaf_out[:, start : start + leaves] = jnp.where(hit, 1.0, 0.0).astype(BF16)
        uppers = owners * parents
        same = iota((uppers, uppers), 0) == iota((uppers, uppers), 1)
        same = jnp.where(same, 1.0, 0.0).astype(BF16)
        pslots = count // parents
        for i in range(pslots):
            code = jnp.broadcast_to(codes[slots + i : slots + i + 1, :], (uppers, leaves))
            hit = jnp.where(code == iota(code.shape, 0), 1.0, 0.0).astype(BF16)
            turned = lax.dot_general(
                hit, same, (((0,), (0,)), ((), ())), preferred_element_type=F32
            )
            start = half * count + i * parents
            parent_out[start : start + parents, :] = turned[:parents].astype(BF16)
    rank_width, pslots = own_ref.shape[0], own_ref.shape[1] // parents
    for half, ref in enumerate((own_ref, peer_ref)):
        rows_scr[...] = ref[...].reshape(rank_width * pslots * parents, rank_width).astype(F32)
        for i in range(pslots):
            place = (half * pslots + i) * rank_width
            for parent in range(parents):
                block = rows_scr[pl.ds(i * parents + parent, rank_width, stride=pslots * parents), :]
                couple_out[parent, place : place + rank_width, :] = block.astype(BF16)


def far_kernel(owners, vs, pslots, leaf_table, parent_table, pcouple_ref, block_ref, *refs):
    extras = refs[:-8]
    own_ref, peer_any, out_ref, rows_scr, prows_scr, pout_scr, couple_scr, sems = refs[-8:]
    slots, rank_width, _, leaves = own_ref.shape
    parents = pcouple_ref.shape[0]
    copies = []
    for i in range(slots):
        copies.append(pltpu.make_async_copy(peer_any.at[i], couple_scr.at[i], sems.at[i]))
        copies[-1].start()
    per_block = block_ref.shape[0] // owners
    mine = vs * rank_width
    rows = jnp.zeros((mine, 2 * slots * leaves), F32)
    for o in range(0, owners, 2):
        pair = [block_ref[p * per_block : p * per_block + mine, :] for p in (o, o + 1)]
        rows = rows + jnp.dot(
            jnp.concatenate(pair, axis=1),
            leaf_table[o * leaves : (o + 2) * leaves, :],
            preferred_element_type=F32,
        )
    for i in range(2 * slots):
        rows_scr[i] = rows[:, i * leaves : (i + 1) * leaves]

    for b, members in enumerate(packs(vs, rank_width, leaves)):
        source = jnp.concatenate(
            [
                block_ref[pl.ds(o * per_block + mine + b * parents, parents), :]
                for o in range(owners)
            ],
            axis=0,
        )
        picked = jnp.dot(parent_table[...], source, preferred_element_type=F32)
        for i in range(2 * pslots):
            for k, n in enumerate(members):
                prows_scr[:, n, i * rank_width : (i + 1) * rank_width] = picked[
                    i * parents : (i + 1) * parents, k * rank_width : (k + 1) * rank_width
                ]
    for parent in range(parents):
        pout_scr[parent] = jnp.dot(
            prows_scr[parent].astype(BF16), pcouple_ref[parent], preferred_element_type=F32
        )
    for b, members in enumerate(packs(vs, rank_width, leaves)):
        parts = [pout_scr[:, n, :] for n in members]
        missing = leaves - len(parts) * rank_width
        if missing:
            parts.append(jnp.zeros((parents, missing), F32))
        out_ref[mine + b * parents : mine + (b + 1) * parents, :] = jnp.concatenate(
            parts, axis=1
        ).astype(out_ref.dtype)
    start = mine + len(packs(vs, rank_width, leaves)) * parents
    for ref in extras:
        out_ref[start : start + ref.shape[0], :] = ref[...]
        start += ref.shape[0]

    accs = [jnp.zeros((rank_width, leaves), F32) for _ in range(vs)]
    for s in range(2 * slots):
        if s >= slots:
            copies[s - slots].wait()
        ref, i = (own_ref, s) if s < slots else (couple_scr, s - slots)
        accs = mac_rows(
            rank_width,
            lambda j, ref=ref, i=i: ref[i, j].astype(F32),
            lambda j, n, s=s: rows_scr[s, pl.ds(n * rank_width + j, 1), :],
            accs,
            8,
        )
    for n in range(vs):
        out_ref[n * rank_width : (n + 1) * rank_width, :] = accs[n].astype(out_ref.dtype)


def down_kernel(vs, parents, keep_ref, *refs):
    recvs, down_ref, out_ref, rows_scr = refs[:-3], refs[-3], refs[-2], refs[-1]
    rank_width, _, leaves = down_ref.shape
    total = keep_ref[...]
    for ref in recvs:
        total = total + ref[0 : total.shape[0], :].astype(F32)
    mine = vs * rank_width
    below = (iota((parents, leaves), 1) // (leaves // parents)) == iota((parents, leaves), 0)
    spread = jnp.where(below, 1.0, 0.0).astype(BF16)
    for b, members in enumerate(packs(vs, rank_width, leaves)):
        part = total[mine + b * parents : mine + (b + 1) * parents, :].astype(BF16)
        wide = lax.dot_general(
            part, spread, (((0,), (0,)), ((), ())), preferred_element_type=F32
        )
        count = len(members) * rank_width
        start = members[0] * rank_width
        rows_scr[start : start + count, :] = wide[:count]
    accs = mac_rows(
        rank_width,
        lambda j: down_ref[j].astype(F32),
        lambda j, n: row_of(rows_scr, n * rank_width + j),
        [total[n * rank_width : (n + 1) * rank_width, :] for n in range(vs)],
        8,
    )
    for n in range(vs):
        out_ref[n * rank_width : (n + 1) * rank_width, :] = accs[n].astype(BF16)


def near_kernel(
    vh, step, ids_ref, own_field, peer_field, own_ref, peer_any, out_ref, peer_scr, acc_scr, sem
):
    slab, _, leaves = own_ref.shape
    group = 6
    target = pl.multiple_of((ids_ref[1] ^ step) * (2 * slab), 2 * slab)
    copy = pltpu.make_async_copy(peer_any.at[:, pl.ds(target, 2 * slab), :], peer_scr, sem)
    copy.start()

    def products(field_ref, ref, base, first, half, accs):
        span = pl.ds(pl.multiple_of(base + half * slab, slab), slab)
        return mac_rows(
            slab,
            lambda p: ref[p, span, :].astype(F32),
            lambda p, n: row_of(field_ref, p * vh + first + n),
            accs,
            8,
        )

    places = [(half, first) for half in range(2) for first in range(0, vh, group)]
    for half, first in places:
        accs = [jnp.zeros((slab, leaves), F32) for _ in range(group)]
        accs = products(own_field, own_ref, target, first, half, accs)
        for n in range(group):
            start = (half * vh + first + n) * slab
            acc_scr[start : start + slab, :] = accs[n]
    copy.wait()
    for half, first in places:
        starts = [(half * vh + first + n) * slab for n in range(group)]
        accs = [acc_scr[start : start + slab, :] for start in starts]
        accs = products(peer_field, peer_scr, 0, first, half, accs)
        for n, start in enumerate(starts):
            out_ref[start : start + slab, :] = accs[n].astype(out_ref.dtype)


def near_sum_kernel(skip, ids_ref, keep_ref, last_ref, *refs):
    recvs, mine_ref, send_ref = refs[:-2], refs[-2], refs[-1]
    count = mine_ref.shape[0]
    parity = ids_ref[2]

    def summed(start):
        start = pl.multiple_of(start, 16)
        total = keep_ref[pl.ds(start, count), :] + last_ref[pl.ds(start, count), :].astype(F32)
        for ref in recvs:
            total = total + ref[pl.ds(skip + start, count), :].astype(F32)
        return total

    mine_ref[...] = summed(parity * count)
    send_ref[...] = summed((1 - parity) * count).astype(BF16)


def column_kernel(vs, column_ref, mine_ref, other_ref, out_ref, rows_scr):
    rank_width, voxels, leaves = column_ref.shape
    rows_scr[0] = mine_ref[...].astype(F32)
    rows_scr[1] = other_ref[...].astype(F32)
    accs = mac_rows(
        rank_width,
        lambda k: column_ref[k].astype(F32),
        lambda k, n: rows_scr[n // vs, pl.ds((n % vs) * rank_width + k, 1), :],
        [jnp.zeros((voxels, leaves), F32) for _ in range(2 * vs)],
        8,
    )
    for n in range(2 * vs):
        out_ref[n * voxels : (n + 1) * voxels, :] = accs[n]


def out_kernel(lvls, vh, vs, early, ids_ref, column_ref, near_mine, near_peer, *refs):
    done, blocks = refs[:early], refs[early : -3]
    out_ref, rows_scr, out_scr = refs[-3:]
    rank_width, voxels, leaves = column_ref.shape
    vectors = out_ref.shape[1]
    lvl, parity = ids_ref[1], ids_ref[2]
    late = lvls - early
    for b, ref in enumerate(blocks):
        rows_scr[b] = ref[...].astype(F32)

    def store(place, rep, value):
        def write():
            vector = place * 2 + (parity if rep == 0 else 1 - parity)
            out_scr[pl.ds(vector, voxels, stride=vectors), :] = value

        if lvls * vs == vh:
            write()
        else:
            pl.when(place < vh)(write)

    for t in range(lvls):
        first = (lvl ^ t) * vs
        if t < early:
            accs = [done[t][n * voxels : (n + 1) * voxels, :] for n in range(2 * vs)]
        else:
            accs = mac_rows(
                rank_width,
                lambda k: column_ref[k].astype(F32),
                lambda k, n: rows_scr[
                    (n // vs) * late + t - early, pl.ds((n % vs) * rank_width + k, 1), :
                ],
                [jnp.zeros((voxels, leaves), F32) for _ in range(2 * vs)],
                8,
            )
        for n in range(2 * vs):
            place = first + n % vs
            near_ref = (near_mine, near_peer)[n // vs]
            inside = jnp.minimum(place, vh - 1)
            near = near_ref[pl.ds(pl.multiple_of(inside * voxels, voxels), voxels), :]
            store(place, n // vs, accs[n] + near.astype(F32))
    out_ref[...] = out_scr[...].reshape(voxels, vectors, leaves).astype(BF16)


def after(value, *others):
    return lax.optimization_barrier((value,) + others)[0]


def per_device(sizes, *args):
    (
        voxel_field, row_basis, near_block, up_transfer, coupling, parent_coupling,
        down_transfer, column_basis, parent_perm, partner_owner, partner_local,
        parent_owner, parent_local, block_count,
    ) = args
    owners, lvls, reps = sizes
    slab, vectors, leaves = voxel_field.shape
    rank_width = row_basis.shape[1]
    parents = parent_coupling.shape[4]
    children = leaves // parents
    slots = partner_owner.shape[2]
    pslots = parent_owner.shape[2]
    vh = vectors // reps
    vs = -(-vh // lvls)
    sds = jax.ShapeDtypeStruct

    me = lax.axis_index("clus")
    lvl = lax.axis_index("lvl")
    parity = lax.axis_index("rep")
    ids = jnp.concatenate([jnp.stack([me, lvl, parity]).astype(jnp.int32), parent_perm])

    def call(name, kernel, ins, outs, scratch=(), us=1.0, scalars=0, whole=()):
        specs = [
            smem() if i < scalars else pl.BlockSpec(memory_space=pltpu.HBM) if i in whole else vmem()
            for i in range(len(ins))
        ]
        with jax.named_scope(name):
            return pl.pallas_call(
                kernel,
                out_shape=outs,
                in_specs=specs,
                out_specs=jax.tree.map(lambda _: vmem(), outs),
                scratch_shapes=list(scratch),
                compiler_params=params(),
                cost_estimate=cost(0, int(us * 3.3e6)),
            )(*ins)

    def swap(value, axis, count, step):
        return lax.ppermute(value, axis, [(i, i ^ step) for i in range(count)])

    def swaps(values, axis, count, backward=True):
        order = range(count - 1, 0, -1) if backward else range(1, count)
        got = {n: swap(values[n], axis, count, n) for n in order}
        return [got[n] for n in range(1, count)]

    def other(value):
        return swap(value, "rep", reps, 1)

    with jax.named_scope("swap_row_basis"):
        row_peer = other(row_basis)

    with jax.named_scope("swap_parent_coupling"):
        pcouple = jnp.transpose(parent_coupling, (0, 2, 3, 4, 1)).reshape(
            rank_width, pslots * parents, rank_width
        )
        pcouple_peer = other(pcouple)

    with jax.named_scope("swap_self_blocks"):
        near_peer_block = other(near_block)

    chunk_rows = 2 * (slab // owners) * vh
    packed = call(
        "pack_field",
        functools.partial(pack_kernel, owners, vh, parents),
        (ids, voxel_field),
        sds((owners, chunk_rows, leaves), BF16),
        [pltpu.VMEM((slab * vectors, leaves), F32)],
        1.0, scalars=1,
    )
    with jax.named_scope("regroup_sends"):
        chunks = [packed[0]] + swaps([packed[s] for s in range(owners)], "clus", owners, False)
    codes = call(
        "place_codes",
        functools.partial(place_kernel, owners, parents),
        (after(ids, chunks[1]),),
        sds((8, leaves), jnp.int32),
        [pltpu.SMEM((parents + 1,), jnp.int32)],
        0.3, scalars=1,
    )
    with jax.named_scope("coupling_layout"):
        couple = jnp.moveaxis(after(coupling, chunks[1])[:, :, 0], 2, 0)

    with jax.named_scope("partner_codes"):
        held = lax.optimization_barrier(
            (partner_owner, partner_local, parent_owner, parent_local, block_count, chunks[1])
        )
        group = lvl * reps + parity
        slot_number = group * slots + jnp.arange(slots, dtype=jnp.int32)[:, None]
        leaf_code = (held[0][0] ^ me).T * leaves + held[1][0].T
        leaf_code = jnp.where(slot_number < held[4][None, :], leaf_code, -1)
        up_code = (held[2][0] ^ me).T * parents + held[3][0].T
        up_code = jnp.pad(up_code, ((0, 0), (0, leaves - parents)), constant_values=-1)
        partners = jnp.concatenate([leaf_code, up_code], axis=0)
        partners_peer = other(partners)
    codes = after(codes, couple, row_peer, partners_peer)

    field, field_send = call(
        "regroup_field",
        functools.partial(regroup_kernel, owners),
        (codes, *chunks),
        [sds((slab * vh, leaves), F32), sds((slab * vh, leaves), BF16)],
        (), 0.4,
    )
    with jax.named_scope("swap_field"):
        field_recv = other(field_send)
    coeff_own = call(
        "coeffs_own_slab",
        functools.partial(coeff_own_kernel, lvls, vh, vs),
        (ids, row_basis, field),
        sds((lvls * vs * rank_width, leaves), F32),
        (), 1.6, scalars=1,
    )
    outs = call(
        "coeffs_other_slab",
        functools.partial(coeff_peer_kernel, lvls, vh, vs),
        (ids, row_peer, field_recv, coeff_own),
        [sds((slab * vh, leaves), F32), sds((vs * rank_width, leaves), F32)]
        + [sds((vs * rank_width, leaves), BF16)] * (lvls - 1),
        (), 1.6, scalars=1,
    )
    field_peer, keep, sends = outs[0], outs[1], outs[2:]
    with jax.named_scope("coeff_sends"):
        recvs = swaps([None, *sends], "lvl", lvls, True)

    with jax.named_scope("swap_coupling"):
        couple_peer = other(after(couple, keep))

    def near_part(t, place):
        return call(
            "self_blocks",
            functools.partial(near_kernel, vh, t),
            (ids, place, field_peer, near_block, near_peer_block),
            sds((2 * vh * slab, leaves), F32 if t == 0 else BF16),
            [
                pltpu.VMEM((slab, 2 * slab, leaves), BF16),
                pltpu.VMEM((2 * vh * slab, leaves), F32),
                pltpu.SemaphoreType.DMA,
            ],
            2.4, scalars=1, whole=(4,),
        )

    near_parts = [None] * lvls
    near_parts[1] = near_part(1, after(field, keep))
    up_after = after(up_transfer, near_parts[1])

    block_rows = vs * rank_width + len(packs(vs, rank_width, leaves)) * parents
    block = call(
        "parent_coeffs",
        functools.partial(up_kernel, vs, parents),
        (keep, *recvs[::-1], up_after),
        sds((block_rows, leaves), BF16),
        [pltpu.VMEM((vs * rank_width, leaves), F32)],
        0.8,
    )
    with jax.named_scope("owner_sends"):
        blocks = [block] + swaps([block] * owners, "clus", owners, False)
    later = after(field, block)
    for t in range(2, lvls):
        near_parts[t] = near_part(t, later)
    with jax.named_scope("all_owners"):
        blocks = list(lax.optimization_barrier(tuple(blocks) + tuple(near_parts[2:])))[:owners]
        mine = jnp.concatenate(blocks, axis=0)
    with jax.named_scope("level_sends"):
        alls = [mine] + swaps([mine] * lvls, "lvl", lvls, False)

    later = after(field, mine)
    near_parts[0] = near_part(0, later)
    leaf_table, parent_table, pcouple_all = call(
        "partner_tables",
        functools.partial(table_kernel, owners, parents, slots),
        (after(partners, mine), partners_peer, pcouple, pcouple_peer),
        [
            sds((owners * leaves, 2 * slots * leaves), BF16),
            sds((2 * pslots * parents, owners * parents), BF16),
            sds((parents, 2 * pslots * rank_width, rank_width), BF16),
        ],
        [pltpu.VMEM((rank_width * pslots * parents, rank_width), F32)],
        1.5,
    )
    def far_part(t, block):
        extras = (near_parts[t],) if 0 < t < lvls - 1 else ()
        rows = block_rows + (2 * vh * slab if extras else 0)
        return call(
            "coupling_products",
            functools.partial(far_kernel, owners, vs, pslots),
            (leaf_table, parent_table, pcouple_all, block, *extras, couple, couple_peer),
            sds((rows, leaves), F32 if t == 0 else BF16),
            [
                pltpu.VMEM((2 * slots, vs * rank_width, leaves), F32),
                pltpu.VMEM((parents, 8, 2 * pslots * rank_width), F32),
                pltpu.VMEM((parents, 8, rank_width), F32),
                pltpu.VMEM((slots, rank_width, rank_width, leaves), BF16),
                pltpu.SemaphoreType.DMA((slots,)),
            ],
            3.2, whole=(5 + len(extras),),
        )

    alls[1] = after(alls[1], near_parts[0])
    far_parts = [far_part(t, alls[t]) for t in range(lvls)]
    with jax.named_scope("far_sends"):
        far_recvs = swaps(far_parts, "lvl", lvls, False)
    with jax.named_scope("self_sends"):
        last = lvls - 1
        near_recv = swap(after(near_parts[last], far_recvs[-1], far_parts[0]), "lvl", lvls, last)
    far = call(
        "down_products",
        functools.partial(down_kernel, vs, parents),
        (far_parts[0], *far_recvs, down_transfer),
        sds((vs * rank_width, leaves), BF16),
        [pltpu.VMEM((vs * rank_width, leaves), F32)],
        0.8,
    )
    with jax.named_scope("far_coeff_sends"):
        far_blocks = [far] + swaps([far] * lvls, "lvl", lvls, True)
        far_others = [other(value) for value in far_blocks]
    early = lvls - 1
    done = [
        call(
            "column_products_early",
            functools.partial(column_kernel, vs),
            (column_basis, far_blocks[t], far_others[t]),
            sds((2 * vs * slab, leaves), F32),
            [pltpu.VMEM((2, vs * rank_width, leaves), F32)],
            0.5,
        )
        for t in range(early)
    ]
    near_mine, near_send = call(
        "self_sums",
        functools.partial(near_sum_kernel, block_rows),
        (ids, after(near_parts[0], done[0]), near_recv, *far_recvs[:-1]),
        [sds((vh * slab, leaves), F32), sds((vh * slab, leaves), BF16)],
        (), 0.65, scalars=1,
    )
    with jax.named_scope("swap_self_sums"):
        near_peer = other(near_send)
    return call(
        "column_products",
        functools.partial(out_kernel, lvls, vh, vs, early),
        (
            ids, column_basis, near_mine, near_peer, *done,
            *far_blocks[early:], *far_others[early:],
        ),
        sds((slab, vectors, leaves), BF16),
        [
            pltpu.VMEM((2 * (lvls - early), vs * rank_width, leaves), F32),
            pltpu.VMEM((slab * vectors, leaves), F32),
        ],
        1.85, scalars=1,
    )


def solution(mesh):
    sizes = (mesh.shape["clus"], mesh.shape["lvl"], mesh.shape["rep"])
    return jax.shard_map(
        functools.partial(per_device, sizes),
        mesh=mesh,
        in_specs=(
            P(("lvl", "rep"), None, ("parts", "clus")),
            P(("lvl", "rep"), None, ("parts", "clus")),
            P(("lvl", "rep"), None, ("parts", "clus")),
            P(None, None, ("parts", "clus")),
            P(None, None, ("lvl", "rep"), None, ("parts", "clus")),
            P(None, None, ("lvl", "rep"), None, ("parts", "clus")),
            P(None, None, ("parts", "clus")),
            P(None, ("lvl", "rep"), ("parts", "clus")),
            P("parts"),
            P(("lvl", "rep"), ("parts", "clus"), None),
            P(("lvl", "rep"), ("parts", "clus"), None),
            P(("lvl", "rep"), ("parts", "clus"), None),
            P(("lvl", "rep"), ("parts", "clus"), None),
            P(("parts", "clus")),
        ),
        out_specs=P(("lvl", "rep"), None, ("parts", "clus")),
        check_vma=False,
    )
```

```python
import functools

import jax
import jax.numpy as jnp
from jax import lax
from jax.experimental import pallas as pl
from jax.experimental.pallas import tpu as pltpu
from jax.sharding import PartitionSpec as P

F32 = jnp.float32
BF16 = jnp.bfloat16
VMEM_LIMIT = 12 * 1024 * 1024


def vmem():
    return pl.BlockSpec(memory_space=pltpu.VMEM)


def smem():
    return pl.BlockSpec(memory_space=pltpu.SMEM)


def params(**more):
    return pltpu.CompilerParams(vmem_limit_bytes=VMEM_LIMIT, **more)


def cost(flops, nbytes):
    return pl.CostEstimate(flops=flops, bytes_accessed=nbytes, transcendentals=0)


def iota(shape, dim):
    return lax.broadcasted_iota(jnp.int32, shape, dim)


def row_of(ref, row):
    return ref[pl.ds(row, 1), :]


def mac_rows(total_steps, weight_at, row_at, accs, unroll):
    def body(step, carry):
        weight = weight_at(step)
        return tuple(acc + weight * row_at(step, n) for n, acc in enumerate(carry))

    return lax.fori_loop(0, total_steps, body, tuple(accs), unroll=unroll)


def pack_kernel(
    owners, vh, parents, ids_ref, perm_any, own_any, out_ref, rows_scr, perm_ref, own_ref, sems
):
    slab, vectors, leaves = own_ref.shape
    perm_copy = pltpu.make_async_copy(perm_any, perm_ref, sems.at[0])
    perm_copy.start()
    copies = []
    for c in range(4):
        part = slice(c * slab // 4, (c + 1) * slab // 4)
        copies.append(
            pltpu.make_async_copy(own_any.at[part], own_ref.at[part], sems.at[1 + c])
        )
        copies[-1].start()
    children = leaves // parents
    reps = vectors // vh
    width = leaves // owners
    me, parity = ids_ref[0], ids_ref[2]
    row = iota((leaves, leaves), 0)
    lane = iota((leaves, leaves), 1)
    parent_of_row = row // children
    target = row % children
    bits = 32 // owners
    counts = jnp.int32(0)
    perm_copy.wait()
    for parent in range(parents):
        owner = perm_ref[me * parents + parent] // parents
        shift = owner * bits
        rank = lax.shift_right_logical(counts, shift) & ((1 << bits) - 1)
        counts = counts + lax.shift_left(jnp.int32(1), shift)
        code = (owner ^ me) * leaves + rank * children
        target = target + jnp.where(parent_of_row == parent, code, 0)
    part = (slab // owners) * vh
    for copy in copies:
        copy.wait()
    rows_scr[...] = own_ref[...].reshape(slab * vectors, leaves).astype(F32)
    pieces = []
    for q in range(owners):
        start = q * (slab // owners) * vectors
        pieces.append(
            jnp.concatenate(
                [
                    rows_scr[pl.ds(start + first, part, stride=reps), :]
                    for first in (parity, 1 - parity)
                ],
                axis=0,
            ).astype(BF16)
        )
    for s in range(owners):
        total = jnp.zeros((2 * part, leaves), F32)
        for q in range(owners):
            onehot = jnp.where(target + (q * width - s * leaves) == lane, 1.0, 0.0).astype(BF16)
            total = total + jnp.dot(pieces[q], onehot, preferred_element_type=F32)
        out_ref[s] = total.astype(BF16)


def place_kernel(owners, parents, ids_ref, perm_any, out_ref, code_scr, perm_ref, sem):
    copy = pltpu.make_async_copy(perm_any, perm_ref, sem)
    copy.start()
    copy.wait()
    leaves = out_ref.shape[1]
    children = leaves // parents
    me = ids_ref[0]
    for source in range(owners):
        rank = jnp.int32(0)
        base = (source ^ me) * leaves
        for parent in range(parents):
            place = perm_ref[source * parents + parent]
            mine = (place // parents) == me
            slot = jnp.where(mine, place % parents, parents)
            code_scr[slot] = base + rank * children
            rank = rank + jnp.where(mine, 1, 0)
    lane = iota(out_ref.shape, 1)
    code = lane % children
    for parent in range(parents):
        code = code + jnp.where(lane // children == parent, code_scr[parent], 0)
    out_ref[...] = code


def regroup_kernel(owners, code_ref, *refs):
    chunks, mine_ref, other_ref = refs[:owners], refs[owners], refs[owners + 1]
    leaves = mine_ref.shape[1]
    width = leaves // owners
    part = mine_ref.shape[0] // owners
    code = jnp.broadcast_to(code_ref[0:1, :], (leaves, leaves))
    row = iota((leaves, leaves), 0)
    for q in range(owners):
        total = jnp.zeros((2 * part, leaves), F32)
        for s in range(owners):
            onehot = jnp.where(code + (q * width - s * leaves) == row, 1.0, 0.0).astype(BF16)
            total = total + jnp.dot(chunks[s][...], onehot, preferred_element_type=F32)
        mine_ref[q * part : (q + 1) * part, :] = total[:part]
        other_ref[q * part : (q + 1) * part, :] = total[part:].astype(BF16)


def coeff_products(lvl, lvls, vh, vs, basis_ref, field_ref, start_of, finish):
    slab, rank_width, leaves = basis_ref.shape
    half = rank_width // 2
    for first_t in range(0, lvls, 2):
        members = [(t, n) for t in (first_t, first_t + 1) for n in range(vs)]
        places = [jnp.minimum((lvl ^ t) * vs + n, vh - 1) for t, n in members]
        for low in range(0, rank_width, half):
            part = slice(low, low + half)
            accs = mac_rows(
                slab,
                lambda m: basis_ref[m, part, :].astype(F32),
                lambda m, n: row_of(field_ref, m * vh + places[n]),
                [start_of(t, n, low, half) for t, n in members],
                8,
            )
            for (t, n), acc in zip(members, accs):
                finish(t, n, low, half, acc)


def coeff_own_kernel(lvls, vh, vs, ids_ref, basis_ref, field_ref, out_ref):
    rank_width, leaves = basis_ref.shape[1:]

    def finish(t, n, low, half, acc):
        start = (t * vs + n) * rank_width + low
        out_ref[start : start + half, :] = acc

    coeff_products(
        ids_ref[1], lvls, vh, vs, basis_ref, field_ref,
        lambda t, n, low, half: jnp.zeros((half, leaves), F32), finish,
    )


def coeff_peer_kernel(
    lvls, vh, vs, ids_ref, basis_ref, field_ref, own_ref, wide_ref, keep_ref, *sends
):
    rank_width = basis_ref.shape[1]
    wide_ref[...] = field_ref[...].astype(F32)

    def start_of(t, n, low, half):
        start = (t * vs + n) * rank_width + low
        return own_ref[start : start + half, :]

    def finish(t, n, low, half, acc):
        start = n * rank_width + low
        if t == 0:
            keep_ref[start : start + half, :] = acc
        else:
            sends[t - 1][start : start + half, :] = acc.astype(BF16)

    coeff_products(ids_ref[1], lvls, vh, vs, basis_ref, wide_ref, start_of, finish)


def packs(vs, rank_width, leaves):
    per = max(1, leaves // rank_width)
    return [list(range(first, min(first + per, vs))) for first in range(0, vs, per)]


def up_kernel(vs, parents, keep_ref, *refs):
    recvs, up_ref, out_ref, coeff_scr = refs[:-3], refs[-3], refs[-2], refs[-1]
    rank_width, _, leaves = up_ref.shape
    total = keep_ref[...]
    for ref in recvs:
        total = total + ref[...].astype(F32)
    coeffs = total.astype(BF16)
    out_ref[0 : vs * rank_width, :] = coeffs
    coeff_scr[...] = coeffs.astype(F32)
    accs = mac_rows(
        rank_width,
        lambda j: up_ref[j].astype(F32),
        lambda j, n: row_of(coeff_scr, n * rank_width + j),
        [jnp.zeros((rank_width, leaves), F32) for _ in range(vs)],
        8,
    )
    mine = (iota((parents, leaves), 1) // (leaves // parents)) == iota((parents, leaves), 0)
    group = jnp.where(mine, 1.0, 0.0).astype(BF16)
    for b, members in enumerate(packs(vs, rank_width, leaves)):
        sums = []
        for n in members:
            rest, result = accs[n], jnp.zeros((parents, rank_width), F32)
            for _ in range(3):
                piece = rest.astype(BF16)
                result = result + lax.dot_general(
                    group, piece, (((1,), (1,)), ((), ())), preferred_element_type=F32
                )
                rest = rest - piece.astype(F32)
            sums.append(result)
        missing = leaves - len(sums) * rank_width
        if missing:
            sums.append(jnp.zeros((parents, missing), F32))
        start = vs * rank_width + b * parents
        out_ref[start : start + parents, :] = jnp.concatenate(sums, axis=1).astype(BF16)


def table_kernel(
    owners, parents, slots, own_codes, peer_codes, own_ref, peer_ref,
    leaf_out, parent_out, couple_out, rows_scr,
):
    leaves = own_codes.shape[1]
    sources = leaf_out.shape[0]
    count = parent_out.shape[0] // 2
    for half, codes in enumerate((own_codes, peer_codes)):
        for i in range(slots):
            hit = jnp.broadcast_to(codes[i : i + 1, :], (sources, leaves)) == iota(
                (sources, leaves), 0
            )
            start = (half * slots + i) * leaves
            leaf_out[:, start : start + leaves] = jnp.where(hit, 1.0, 0.0).astype(BF16)
        uppers = owners * parents
        same = iota((uppers, uppers), 0) == iota((uppers, uppers), 1)
        same = jnp.where(same, 1.0, 0.0).astype(BF16)
        pslots = count // parents
        for i in range(pslots):
            code = jnp.broadcast_to(codes[slots + i : slots + i + 1, :], (uppers, leaves))
            hit = jnp.where(code == iota(code.shape, 0), 1.0, 0.0).astype(BF16)
            turned = lax.dot_general(
                hit, same, (((0,), (0,)), ((), ())), preferred_element_type=F32
            )
            start = half * count + i * parents
            parent_out[start : start + parents, :] = turned[:parents].astype(BF16)
    rank_width, pslots = own_ref.shape[0], own_ref.shape[1] // parents
    for half, ref in enumerate((own_ref, peer_ref)):
        rows_scr[...] = ref[...].reshape(rank_width * pslots * parents, rank_width).astype(F32)
        for i in range(pslots):
            place = (half * pslots + i) * rank_width
            for parent in range(parents):
                block = rows_scr[pl.ds(i * parents + parent, rank_width, stride=pslots * parents), :]
                couple_out[parent, place : place + rank_width, :] = block.astype(BF16)


def far_kernel(owners, vs, pslots, leaf_table, parent_table, pcouple_ref, block_ref, *refs):
    extras = refs[:-8]
    own_ref, peer_any, out_ref, rows_scr, prows_scr, pout_scr, couple_scr, sems = refs[-8:]
    slots, rank_width, _, leaves = own_ref.shape
    parents = pcouple_ref.shape[0]
    copies = []
    for i in range(slots):
        copies.append(pltpu.make_async_copy(peer_any.at[i], couple_scr.at[i], sems.at[i]))
        copies[-1].start()
    per_block = block_ref.shape[0] // owners
    mine = vs * rank_width
    rows = jnp.zeros((mine, 2 * slots * leaves), F32)
    for o in range(0, owners, 2):
        pair = [block_ref[p * per_block : p * per_block + mine, :] for p in (o, o + 1)]
        rows = rows + jnp.dot(
            jnp.concatenate(pair, axis=1),
            leaf_table[o * leaves : (o + 2) * leaves, :],
            preferred_element_type=F32,
        )
    for i in range(2 * slots):
        rows_scr[i] = rows[:, i * leaves : (i + 1) * leaves]

    for b, members in enumerate(packs(vs, rank_width, leaves)):
        source = jnp.concatenate(
            [
                block_ref[pl.ds(o * per_block + mine + b * parents, parents), :]
                for o in range(owners)
            ],
            axis=0,
        )
        picked = jnp.dot(parent_table[...], source, preferred_element_type=F32)
        for i in range(2 * pslots):
            for k, n in enumerate(members):
                prows_scr[:, n, i * rank_width : (i + 1) * rank_width] = picked[
                    i * parents : (i + 1) * parents, k * rank_width : (k + 1) * rank_width
                ]
    start = mine + len(packs(vs, rank_width, leaves)) * parents
    for ref in extras:
        out_ref[start : start + ref.shape[0], :] = ref[...]
        start += ref.shape[0]

    accs = tuple(jnp.zeros((rank_width, leaves), F32) for _ in range(vs))
    turns = parents // (2 * slots)
    width = rank_width // turns
    for s in range(2 * slots):
        if s >= slots:
            copies[s - slots].wait()
        ref, i = (own_ref, s) if s < slots else (couple_scr, s - slots)

        def body(turn, carry, s=s, ref=ref, i=i):
            parent = s * turns + turn
            pout_scr[parent] = jnp.dot(
                prows_scr[parent].astype(BF16), pcouple_ref[parent], preferred_element_type=F32
            )
            for k in range(width):
                j = turn * width + k
                weight = ref[i, j].astype(F32)
                carry = tuple(
                    acc + weight * rows_scr[s, pl.ds(n * rank_width + j, 1), :]
                    for n, acc in enumerate(carry)
                )
            return carry

        accs = lax.fori_loop(0, turns, body, accs)
    for n in range(vs):
        out_ref[n * rank_width : (n + 1) * rank_width, :] = accs[n].astype(out_ref.dtype)
    for b, members in enumerate(packs(vs, rank_width, leaves)):
        parts = [pout_scr[:, n, :] for n in members]
        missing = leaves - len(parts) * rank_width
        if missing:
            parts.append(jnp.zeros((parents, missing), F32))
        out_ref[mine + b * parents : mine + (b + 1) * parents, :] = jnp.concatenate(
            parts, axis=1
        ).astype(out_ref.dtype)


def down_kernel(vs, parents, keep_ref, *refs):
    recvs, down_ref, out_ref, rows_scr = refs[:-3], refs[-3], refs[-2], refs[-1]
    rank_width, _, leaves = down_ref.shape
    total = keep_ref[...]
    for ref in recvs:
        total = total + ref[0 : total.shape[0], :].astype(F32)
    mine = vs * rank_width
    below = (iota((parents, leaves), 1) // (leaves // parents)) == iota((parents, leaves), 0)
    spread = jnp.where(below, 1.0, 0.0).astype(BF16)
    for b, members in enumerate(packs(vs, rank_width, leaves)):
        part = total[mine + b * parents : mine + (b + 1) * parents, :].astype(BF16)
        wide = lax.dot_general(
            part, spread, (((0,), (0,)), ((), ())), preferred_element_type=F32
        )
        count = len(members) * rank_width
        start = members[0] * rank_width
        rows_scr[start : start + count, :] = wide[:count]
    accs = mac_rows(
        rank_width,
        lambda j: down_ref[j].astype(F32),
        lambda j, n: row_of(rows_scr, n * rank_width + j),
        [total[n * rank_width : (n + 1) * rank_width, :] for n in range(vs)],
        8,
    )
    for n in range(vs):
        out_ref[n * rank_width : (n + 1) * rank_width, :] = accs[n].astype(BF16)


def near_kernel(
    vh, step, ids_ref, own_field, peer_field, own_ref, peer_any, out_ref, peer_scr, acc_scr, sems
):
    slab, _, leaves = own_ref.shape
    group = 6
    target = pl.multiple_of((ids_ref[1] ^ step) * (2 * slab), 2 * slab)
    copies = []
    for c in range(4):
        part = slice(c * slab // 4, (c + 1) * slab // 4)
        copies.append(
            pltpu.make_async_copy(
                peer_any.at[part, pl.ds(target, 2 * slab), :], peer_scr.at[part], sems.at[c]
            )
        )
        copies[-1].start()

    def products(field_ref, ref, base, first, half, accs):
        span = pl.ds(pl.multiple_of(base + half * slab, slab), slab)
        return mac_rows(
            slab,
            lambda p: ref[p, span, :].astype(F32),
            lambda p, n: row_of(field_ref, p * vh + first + n),
            accs,
            16,
        )

    places = [(half, first) for half in range(2) for first in range(0, vh, group)]
    for half, first in places:
        accs = [jnp.zeros((slab, leaves), F32) for _ in range(group)]
        accs = products(own_field, own_ref, target, first, half, accs)
        for n in range(group):
            start = (half * vh + first + n) * slab
            acc_scr[start : start + slab, :] = accs[n]
    for copy in copies:
        copy.wait()
    for half, first in places:
        starts = [(half * vh + first + n) * slab for n in range(group)]
        accs = [acc_scr[start : start + slab, :] for start in starts]
        accs = products(peer_field, peer_scr, 0, first, half, accs)
        for n, start in enumerate(starts):
            out_ref[start : start + slab, :] = accs[n].astype(out_ref.dtype)


def near_sum_kernel(skip, ids_ref, keep_ref, last_ref, *refs):
    recvs, mine_ref, send_ref = refs[:-2], refs[-2], refs[-1]
    count = mine_ref.shape[0]
    parity = ids_ref[2]

    def summed(start):
        start = pl.multiple_of(start, 16)
        total = keep_ref[pl.ds(start, count), :] + last_ref[pl.ds(start, count), :].astype(F32)
        for ref in recvs:
            total = total + ref[pl.ds(skip + start, count), :].astype(F32)
        return total

    mine_ref[...] = summed(parity * count)
    send_ref[...] = summed((1 - parity) * count).astype(BF16)


def column_kernel(vs, column_ref, mine_ref, other_ref, out_ref, rows_scr):
    rank_width, voxels, leaves = column_ref.shape
    rows_scr[0] = mine_ref[...].astype(F32)
    rows_scr[1] = other_ref[...].astype(F32)
    accs = mac_rows(
        rank_width,
        lambda k: column_ref[k].astype(F32),
        lambda k, n: rows_scr[n // vs, pl.ds((n % vs) * rank_width + k, 1), :],
        [jnp.zeros((voxels, leaves), F32) for _ in range(2 * vs)],
        8,
    )
    for n in range(2 * vs):
        out_ref[n * voxels : (n + 1) * voxels, :] = accs[n]


def out_kernel(lvls, vh, vs, early, ids_ref, column_ref, near_mine, near_peer, *refs):
    done, blocks = refs[:early], refs[early : -3]
    out_ref, rows_scr, out_scr = refs[-3:]
    rank_width, voxels, leaves = column_ref.shape
    vectors = out_ref.shape[1]
    lvl, parity = ids_ref[1], ids_ref[2]
    late = lvls - early
    for b, ref in enumerate(blocks):
        rows_scr[b] = ref[...].astype(F32)

    def store(place, rep, value):
        def write():
            vector = place * 2 + (parity if rep == 0 else 1 - parity)
            out_scr[pl.ds(vector, voxels, stride=vectors), :] = value

        if lvls * vs == vh:
            write()
        else:
            pl.when(place < vh)(write)

    for t in range(lvls):
        first = (lvl ^ t) * vs
        if t < early:
            accs = [done[t][n * voxels : (n + 1) * voxels, :] for n in range(2 * vs)]
        else:
            accs = mac_rows(
                rank_width,
                lambda k: column_ref[k].astype(F32),
                lambda k, n: rows_scr[
                    (n // vs) * late + t - early, pl.ds((n % vs) * rank_width + k, 1), :
                ],
                [jnp.zeros((voxels, leaves), F32) for _ in range(2 * vs)],
                8,
            )
        for n in range(2 * vs):
            place = first + n % vs
            near_ref = (near_mine, near_peer)[n // vs]
            inside = jnp.minimum(place, vh - 1)
            near = near_ref[pl.ds(pl.multiple_of(inside * voxels, voxels), voxels), :]
            store(place, n // vs, accs[n] + near.astype(F32))
    out_ref[...] = out_scr[...].reshape(voxels, vectors, leaves).astype(BF16)


def after(value, *others):
    return lax.optimization_barrier((value,) + others)[0]


def per_device(sizes, *args):
    (
        voxel_field, row_basis, near_block, up_transfer, coupling, parent_coupling,
        down_transfer, column_basis, parent_perm, partner_owner, partner_local,
        parent_owner, parent_local, block_count,
    ) = args
    owners, lvls, reps = sizes
    slab, vectors, leaves = voxel_field.shape
    rank_width = row_basis.shape[1]
    parents = parent_coupling.shape[4]
    children = leaves // parents
    slots = partner_owner.shape[2]
    pslots = parent_owner.shape[2]
    vh = vectors // reps
    vs = -(-vh // lvls)
    sds = jax.ShapeDtypeStruct

    me = lax.axis_index("clus")
    lvl = lax.axis_index("lvl")
    parity = lax.axis_index("rep")
    ids = jnp.stack([me, lvl, parity]).astype(jnp.int32)

    def call(name, kernel, ins, outs, scratch=(), us=1.0, scalars=0, whole=()):
        specs = [
            smem() if i < scalars else pl.BlockSpec(memory_space=pltpu.HBM) if i in whole else vmem()
            for i in range(len(ins))
        ]
        with jax.named_scope(name):
            return pl.pallas_call(
                kernel,
                out_shape=outs,
                in_specs=specs,
                out_specs=jax.tree.map(lambda _: vmem(), outs),
                scratch_shapes=list(scratch),
                compiler_params=params(),
                cost_estimate=cost(0, int(us * 3.3e6)),
            )(*ins)

    def swap(value, axis, count, step):
        return lax.ppermute(value, axis, [(i, i ^ step) for i in range(count)])

    def swaps(values, axis, count, backward=True):
        order = range(count - 1, 0, -1) if backward else range(1, count)
        got = {n: swap(values[n], axis, count, n) for n in order}
        return [got[n] for n in range(1, count)]

    def other(value):
        return swap(value, "rep", reps, 1)

    with jax.named_scope("swap_row_basis"):
        row_peer = other(row_basis)

    with jax.named_scope("swap_parent_coupling"):
        pcouple = jnp.transpose(parent_coupling, (0, 2, 3, 4, 1)).reshape(
            rank_width, pslots * parents, rank_width
        )
        pcouple_peer = other(pcouple)

    with jax.named_scope("swap_self_blocks"):
        near_peer_block = other(near_block)

    chunk_rows = 2 * (slab // owners) * vh
    packed = call(
        "pack_field",
        functools.partial(pack_kernel, owners, vh, parents),
        (
            ids,
            pltpu.with_memory_space_constraint(parent_perm, pltpu.HBM),
            pltpu.with_memory_space_constraint(voxel_field, pltpu.HBM),
        ),
        sds((owners, chunk_rows, leaves), BF16),
        [
            pltpu.VMEM((slab * vectors, leaves), F32),
            pltpu.SMEM(parent_perm.shape, jnp.int32),
            pltpu.VMEM(voxel_field.shape, BF16),
            pltpu.SemaphoreType.DMA((5,)),
        ],
        1.0, scalars=1, whole=(1, 2),
    )
    with jax.named_scope("regroup_sends"):
        chunks = [packed[0]] + swaps([packed[s] for s in range(owners)], "clus", owners, False)
    codes = call(
        "place_codes",
        functools.partial(place_kernel, owners, parents),
        (after(ids, chunks[1]), pltpu.with_memory_space_constraint(parent_perm, pltpu.HBM)),
        sds((8, leaves), jnp.int32),
        [
            pltpu.SMEM((parents + 1,), jnp.int32),
            pltpu.SMEM(parent_perm.shape, jnp.int32),
            pltpu.SemaphoreType.DMA,
        ],
        0.3, scalars=1, whole=(1,),
    )
    with jax.named_scope("coupling_layout"):
        couple = jnp.moveaxis(after(coupling, chunks[1])[:, :, 0], 2, 0)

    with jax.named_scope("partner_codes"):
        held = lax.optimization_barrier(
            (partner_owner, partner_local, parent_owner, parent_local, block_count, chunks[1])
        )
        group = lvl * reps + parity
        row = jnp.arange(slots + pslots, dtype=jnp.int32)[:, None]
        wide = ((0, 0), (0, leaves - parents))
        owner = jnp.concatenate([held[0][0].T, jnp.pad(held[2][0].T, wide)], axis=0) ^ me
        local = jnp.concatenate([held[1][0].T, jnp.pad(held[3][0].T, wide)], axis=0)
        live = (row >= slots) | (group * slots + row < held[4][None, :])
        partners = owner * jnp.where(row < slots, leaves, parents) + local
        partners = jnp.where(live, partners, -1)
        partners_peer = other(partners)
    codes = after(codes, couple, row_peer, partners_peer)

    field, field_send = call(
        "regroup_field",
        functools.partial(regroup_kernel, owners),
        (codes, *chunks),
        [sds((slab * vh, leaves), F32), sds((slab * vh, leaves), BF16)],
        (), 0.4,
    )
    with jax.named_scope("swap_field"):
        field_recv = other(field_send)
    coeff_own = call(
        "coeffs_own_slab",
        functools.partial(coeff_own_kernel, lvls, vh, vs),
        (ids, row_basis, field),
        sds((lvls * vs * rank_width, leaves), F32),
        (), 1.6, scalars=1,
    )
    outs = call(
        "coeffs_other_slab",
        functools.partial(coeff_peer_kernel, lvls, vh, vs),
        (ids, row_peer, field_recv, coeff_own),
        [sds((slab * vh, leaves), F32), sds((vs * rank_width, leaves), F32)]
        + [sds((vs * rank_width, leaves), BF16)] * (lvls - 1),
        (), 1.6, scalars=1,
    )
    field_peer, keep, sends = outs[0], outs[1], outs[2:]
    with jax.named_scope("coeff_sends"):
        recvs = swaps([None, *sends], "lvl", lvls, True)

    with jax.named_scope("swap_coupling"):
        couple_peer = other(after(couple, keep))

    def near_part(t, place):
        return call(
            "self_blocks",
            functools.partial(near_kernel, vh, t),
            (ids, place, field_peer, near_block, near_peer_block),
            sds((2 * vh * slab, leaves), F32 if t == 0 else BF16),
            [
                pltpu.VMEM((slab, 2 * slab, leaves), BF16),
                pltpu.VMEM((2 * vh * slab, leaves), F32),
                pltpu.SemaphoreType.DMA((4,)),
            ],
            2.4, scalars=1, whole=(4,),
        )

    near_parts = [None] * lvls
    near_parts[1] = near_part(1, after(field, keep))
    up_after = after(up_transfer, near_parts[1])

    block_rows = vs * rank_width + len(packs(vs, rank_width, leaves)) * parents
    block = call(
        "parent_coeffs",
        functools.partial(up_kernel, vs, parents),
        (keep, *recvs[::-1], up_after),
        sds((block_rows, leaves), BF16),
        [pltpu.VMEM((vs * rank_width, leaves), F32)],
        0.8,
    )
    with jax.named_scope("owner_sends"):
        blocks = [block] + swaps([block] * owners, "clus", owners, False)
    later = after(field, block)
    for t in range(2, lvls):
        near_parts[t] = near_part(t, later)
    with jax.named_scope("all_owners"):
        blocks = list(lax.optimization_barrier(tuple(blocks) + tuple(near_parts[2:])))[:owners]
        mine = jnp.concatenate(blocks, axis=0)
    with jax.named_scope("level_sends"):
        alls = [mine] + swaps([mine] * lvls, "lvl", lvls, False)

    later = after(field, mine)
    near_parts[0] = near_part(0, later)
    leaf_table, parent_table, pcouple_all = call(
        "partner_tables",
        functools.partial(table_kernel, owners, parents, slots),
        (after(partners, mine), partners_peer, pcouple, pcouple_peer),
        [
            sds((owners * leaves, 2 * slots * leaves), BF16),
            sds((2 * pslots * parents, owners * parents), BF16),
            sds((parents, 2 * pslots * rank_width, rank_width), BF16),
        ],
        [pltpu.VMEM((rank_width * pslots * parents, rank_width), F32)],
        1.5,
    )
    def far_part(t, block):
        extras = (near_parts[t],) if 0 < t < lvls - 1 else ()
        rows = block_rows + (2 * vh * slab if extras else 0)
        return call(
            "coupling_products",
            functools.partial(far_kernel, owners, vs, pslots),
            (leaf_table, parent_table, pcouple_all, block, *extras, couple, couple_peer),
            sds((rows, leaves), F32 if t == 0 else BF16),
            [
                pltpu.VMEM((2 * slots, vs * rank_width, leaves), F32),
                pltpu.VMEM((parents, 8, 2 * pslots * rank_width), F32),
                pltpu.VMEM((parents, 8, rank_width), F32),
                pltpu.VMEM((slots, rank_width, rank_width, leaves), BF16),
                pltpu.SemaphoreType.DMA((slots,)),
            ],
            3.2, whole=(5 + len(extras),),
        )

    alls[1] = after(alls[1], near_parts[0])
    far_parts = [far_part(t, alls[t]) for t in range(lvls)]
    with jax.named_scope("far_sends"):
        far_recvs = swaps(far_parts, "lvl", lvls, False)
    with jax.named_scope("self_sends"):
        last = lvls - 1
        near_recv = swap(after(near_parts[last], far_recvs[-1], far_parts[0]), "lvl", lvls, last)
    far = call(
        "down_products",
        functools.partial(down_kernel, vs, parents),
        (far_parts[0], *far_recvs, down_transfer),
        sds((vs * rank_width, leaves), BF16),
        [pltpu.VMEM((vs * rank_width, leaves), F32)],
        0.8,
    )
    with jax.named_scope("far_coeff_sends"):
        far_blocks = [far] + swaps([far] * lvls, "lvl", lvls, True)
        far_others = [other(value) for value in far_blocks]
    early = lvls - 1
    done = [
        call(
            "column_products_early",
            functools.partial(column_kernel, vs),
            (column_basis, far_blocks[t], far_others[t]),
            sds((2 * vs * slab, leaves), F32),
            [pltpu.VMEM((2, vs * rank_width, leaves), F32)],
            0.5,
        )
        for t in range(early)
    ]
    near_mine, near_send = call(
        "self_sums",
        functools.partial(near_sum_kernel, block_rows),
        (ids, after(near_parts[0], done[0]), near_recv, *far_recvs[:-1]),
        [sds((vh * slab, leaves), F32), sds((vh * slab, leaves), BF16)],
        (), 0.65, scalars=1,
    )
    with jax.named_scope("swap_self_sums"):
        near_peer = other(near_send)
    return call(
        "column_products",
        functools.partial(out_kernel, lvls, vh, vs, early),
        (
            ids, column_basis, near_mine, near_peer, *done,
            *far_blocks[early:], *far_others[early:],
        ),
        sds((slab, vectors, leaves), BF16),
        [
            pltpu.VMEM((2 * (lvls - early), vs * rank_width, leaves), F32),
            pltpu.VMEM((slab * vectors, leaves), F32),
        ],
        1.85, scalars=1,
    )


def solution(mesh):
    sizes = (mesh.shape["clus"], mesh.shape["lvl"], mesh.shape["rep"])
    return jax.shard_map(
        functools.partial(per_device, sizes),
        mesh=mesh,
        in_specs=(
            P(("lvl", "rep"), None, ("parts", "clus")),
            P(("lvl", "rep"), None, ("parts", "clus")),
            P(("lvl", "rep"), None, ("parts", "clus")),
            P(None, None, ("parts", "clus")),
            P(None, None, ("lvl", "rep"), None, ("parts", "clus")),
            P(None, None, ("lvl", "rep"), None, ("parts", "clus")),
            P(None, None, ("parts", "clus")),
            P(None, ("lvl", "rep"), ("parts", "clus")),
            P("parts"),
            P(("lvl", "rep"), ("parts", "clus"), None),
            P(("lvl", "rep"), ("parts", "clus"), None),
            P(("lvl", "rep"), ("parts", "clus"), None),
            P(("lvl", "rep"), ("parts", "clus"), None),
            P(("parts", "clus")),
        ),
        out_specs=P(("lvl", "rep"), None, ("parts", "clus")),
        check_vma=False,
    )
```

```python
import functools

import jax
import jax.numpy as jnp
from jax import lax
from jax.experimental import pallas as pl
from jax.experimental.pallas import tpu as pltpu
from jax.sharding import PartitionSpec as P

F32 = jnp.float32
BF16 = jnp.bfloat16
VMEM_LIMIT = 12 * 1024 * 1024


def vmem():
    return pl.BlockSpec(memory_space=pltpu.VMEM)


def smem():
    return pl.BlockSpec(memory_space=pltpu.SMEM)


def params(**more):
    return pltpu.CompilerParams(vmem_limit_bytes=VMEM_LIMIT, **more)


def cost(flops, nbytes):
    return pl.CostEstimate(flops=flops, bytes_accessed=nbytes, transcendentals=0)


def iota(shape, dim):
    return lax.broadcasted_iota(jnp.int32, shape, dim)


def row_of(ref, row):
    return ref[pl.ds(row, 1), :]


def mac_rows(total_steps, weight_at, row_at, accs, unroll):
    def body(step, carry):
        weight = weight_at(step)
        return tuple(acc + weight * row_at(step, n) for n, acc in enumerate(carry))

    return lax.fori_loop(0, total_steps, body, tuple(accs), unroll=unroll)


def pack_kernel(
    owners, vh, parents, ids_ref, perm_any, own_any, out_ref, rows_scr, perm_ref, own_ref, sems
):
    slab, vectors, leaves = own_ref.shape
    perm_copy = pltpu.make_async_copy(perm_any, perm_ref, sems.at[0])
    perm_copy.start()
    copies = []
    for c in range(4):
        part = slice(c * slab // 4, (c + 1) * slab // 4)
        copies.append(
            pltpu.make_async_copy(own_any.at[part], own_ref.at[part], sems.at[1 + c])
        )
        copies[-1].start()
    children = leaves // parents
    reps = vectors // vh
    width = leaves // owners
    me, parity = ids_ref[0], ids_ref[2]
    row = iota((leaves, leaves), 0)
    lane = iota((leaves, leaves), 1)
    parent_of_row = row // children
    target = row % children
    bits = 32 // owners
    counts = jnp.int32(0)
    perm_copy.wait()
    for parent in range(parents):
        owner = perm_ref[me * parents + parent] // parents
        shift = owner * bits
        rank = lax.shift_right_logical(counts, shift) & ((1 << bits) - 1)
        counts = counts + lax.shift_left(jnp.int32(1), shift)
        code = (owner ^ me) * leaves + rank * children
        target = target + jnp.where(parent_of_row == parent, code, 0)
    part = (slab // owners) * vh
    for copy in copies:
        copy.wait()
    rows_scr[0 : slab * vectors, :] = own_ref[...].reshape(slab * vectors, leaves).astype(F32)
    pieces = []
    for q in range(owners):
        start = q * (slab // owners) * vectors
        pieces.append(
            jnp.concatenate(
                [
                    rows_scr[pl.ds(start + first, part, stride=reps), :]
                    for first in (parity, 1 - parity)
                ],
                axis=0,
            ).astype(BF16)
        )
    for s in range(owners):
        total = jnp.zeros((2 * part, leaves), F32)
        for q in range(owners):
            onehot = jnp.where(target + (q * width - s * leaves) == lane, 1.0, 0.0).astype(BF16)
            total = total + jnp.dot(pieces[q], onehot, preferred_element_type=F32)
        out_ref[s] = total.astype(BF16)


def place_kernel(owners, parents, ids_ref, perm_any, out_ref, code_scr, perm_ref, sem):
    copy = pltpu.make_async_copy(perm_any, perm_ref, sem)
    copy.start()
    copy.wait()
    leaves = out_ref.shape[1]
    children = leaves // parents
    me = ids_ref[0]
    for source in range(owners):
        rank = jnp.int32(0)
        base = (source ^ me) * leaves
        for parent in range(parents):
            place = perm_ref[source * parents + parent]
            mine = (place // parents) == me
            slot = jnp.where(mine, place % parents, parents)
            code_scr[slot] = base + rank * children
            rank = rank + jnp.where(mine, 1, 0)
    lane = iota(out_ref.shape, 1)
    code = lane % children
    for parent in range(parents):
        code = code + jnp.where(lane // children == parent, code_scr[parent], 0)
    out_ref[...] = code


def regroup_kernel(owners, code_ref, *refs):
    chunks, mine_ref, other_ref = refs[:owners], refs[owners], refs[owners + 1]
    leaves = mine_ref.shape[1]
    width = leaves // owners
    part = mine_ref.shape[0] // owners
    code = jnp.broadcast_to(code_ref[0:1, :], (leaves, leaves))
    row = iota((leaves, leaves), 0)
    for q in range(owners):
        total = jnp.zeros((2 * part, leaves), F32)
        for s in range(owners):
            onehot = jnp.where(code + (q * width - s * leaves) == row, 1.0, 0.0).astype(BF16)
            total = total + jnp.dot(chunks[s][...], onehot, preferred_element_type=F32)
        mine_ref[q * part : (q + 1) * part, :] = total[:part]
        other_ref[q * part : (q + 1) * part, :] = total[part:].astype(BF16)


def coeff_products(lvl, lvls, vh, vs, basis_ref, field_ref, start_of, finish):
    slab, rank_width, leaves = basis_ref.shape
    half = rank_width // 2
    for first_t in range(0, lvls, 2):
        members = [(t, n) for t in (first_t, first_t + 1) for n in range(vs)]
        places = [jnp.minimum((lvl ^ t) * vs + n, vh - 1) for t, n in members]
        for low in range(0, rank_width, half):
            part = slice(low, low + half)
            accs = mac_rows(
                slab,
                lambda m: basis_ref[m, part, :].astype(F32),
                lambda m, n: row_of(field_ref, m * vh + places[n]),
                [start_of(t, n, low, half) for t, n in members],
                8,
            )
            for (t, n), acc in zip(members, accs):
                finish(t, n, low, half, acc)


def coeff_own_kernel(lvls, vh, vs, ids_ref, basis_ref, field_ref, out_ref):
    rank_width, leaves = basis_ref.shape[1:]

    def finish(t, n, low, half, acc):
        start = (t * vs + n) * rank_width + low
        out_ref[start : start + half, :] = acc

    coeff_products(
        ids_ref[1], lvls, vh, vs, basis_ref, field_ref,
        lambda t, n, low, half: jnp.zeros((half, leaves), F32), finish,
    )


def coeff_peer_kernel(
    lvls, vh, vs, ids_ref, basis_ref, field_ref, own_ref, wide_ref, keep_ref, *sends
):
    rank_width = basis_ref.shape[1]
    wide_ref[...] = field_ref[...].astype(F32)

    def start_of(t, n, low, half):
        start = (t * vs + n) * rank_width + low
        return own_ref[start : start + half, :]

    def finish(t, n, low, half, acc):
        start = n * rank_width + low
        if t == 0:
            keep_ref[start : start + half, :] = acc
        else:
            sends[t - 1][start : start + half, :] = acc.astype(BF16)

    coeff_products(ids_ref[1], lvls, vh, vs, basis_ref, wide_ref, start_of, finish)


def packs(vs, rank_width, leaves):
    per = max(1, leaves // rank_width)
    return [list(range(first, min(first + per, vs))) for first in range(0, vs, per)]


def up_kernel(vs, parents, keep_ref, *refs):
    recvs, up_ref, out_ref, coeff_scr = refs[:-3], refs[-3], refs[-2], refs[-1]
    rank_width, _, leaves = up_ref.shape
    total = keep_ref[...]
    for ref in recvs:
        total = total + ref[...].astype(F32)
    coeffs = total.astype(BF16)
    out_ref[0 : vs * rank_width, :] = coeffs
    coeff_scr[...] = coeffs.astype(F32)
    accs = mac_rows(
        rank_width,
        lambda j: up_ref[j].astype(F32),
        lambda j, n: row_of(coeff_scr, n * rank_width + j),
        [jnp.zeros((rank_width, leaves), F32) for _ in range(vs)],
        8,
    )
    mine = (iota((parents, leaves), 1) // (leaves // parents)) == iota((parents, leaves), 0)
    group = jnp.where(mine, 1.0, 0.0).astype(BF16)
    for b, members in enumerate(packs(vs, rank_width, leaves)):
        sums = []
        for n in members:
            rest, result = accs[n], jnp.zeros((parents, rank_width), F32)
            for _ in range(3):
                piece = rest.astype(BF16)
                result = result + lax.dot_general(
                    group, piece, (((1,), (1,)), ((), ())), preferred_element_type=F32
                )
                rest = rest - piece.astype(F32)
            sums.append(result)
        missing = leaves - len(sums) * rank_width
        if missing:
            sums.append(jnp.zeros((parents, missing), F32))
        start = vs * rank_width + b * parents
        out_ref[start : start + parents, :] = jnp.concatenate(sums, axis=1).astype(BF16)


def table_kernel(
    owners, parents, slots, own_codes, peer_codes, own_ref, peer_ref,
    leaf_out, parent_out, couple_out, rows_scr,
):
    leaves = own_codes.shape[1]
    sources = leaf_out.shape[0]
    count = parent_out.shape[0] // 2
    for half, codes in enumerate((own_codes, peer_codes)):
        for i in range(slots):
            hit = jnp.broadcast_to(codes[i : i + 1, :], (sources, leaves)) == iota(
                (sources, leaves), 0
            )
            start = (half * slots + i) * leaves
            leaf_out[:, start : start + leaves] = jnp.where(hit, 1.0, 0.0).astype(BF16)
        uppers = owners * parents
        same = iota((uppers, uppers), 0) == iota((uppers, uppers), 1)
        same = jnp.where(same, 1.0, 0.0).astype(BF16)
        pslots = count // parents
        for i in range(pslots):
            code = jnp.broadcast_to(codes[slots + i : slots + i + 1, :], (uppers, leaves))
            hit = jnp.where(code == iota(code.shape, 0), 1.0, 0.0).astype(BF16)
            turned = lax.dot_general(
                hit, same, (((0,), (0,)), ((), ())), preferred_element_type=F32
            )
            start = half * count + i * parents
            parent_out[start : start + parents, :] = turned[:parents].astype(BF16)
    rank_width, pslots = own_ref.shape[0], own_ref.shape[1] // parents
    for half, ref in enumerate((own_ref, peer_ref)):
        blocks = ref[...].reshape(rank_width * pslots * parents, rank_width)
        rows_scr[0 : blocks.shape[0], :] = blocks.astype(F32)
        for i in range(pslots):
            place = (half * pslots + i) * rank_width
            for parent in range(parents):
                block = rows_scr[pl.ds(i * parents + parent, rank_width, stride=pslots * parents), :]
                couple_out[parent, place : place + rank_width, :] = block.astype(BF16)


def far_kernel(owners, vs, pslots, leaf_table, parent_table, pcouple_ref, block_ref, *refs):
    extras = refs[:-8]
    own_ref, peer_any, out_ref, rows_scr, prows_scr, pout_scr, couple_scr, sems = refs[-8:]
    slots, rank_width, _, leaves = own_ref.shape
    parents = pcouple_ref.shape[0]
    copies = []
    for i in range(slots):
        copies.append(pltpu.make_async_copy(peer_any.at[i], couple_scr.at[i], sems.at[i]))
        copies[-1].start()
    per_block = block_ref.shape[0] // owners
    mine = vs * rank_width
    rows = jnp.zeros((mine, 2 * slots * leaves), F32)
    for o in range(0, owners, 2):
        pair = [block_ref[p * per_block : p * per_block + mine, :] for p in (o, o + 1)]
        rows = rows + jnp.dot(
            jnp.concatenate(pair, axis=1),
            leaf_table[o * leaves : (o + 2) * leaves, :],
            preferred_element_type=F32,
        )
    for i in range(2 * slots):
        rows_scr[i] = rows[:, i * leaves : (i + 1) * leaves]

    for b, members in enumerate(packs(vs, rank_width, leaves)):
        source = jnp.concatenate(
            [
                block_ref[pl.ds(o * per_block + mine + b * parents, parents), :]
                for o in range(owners)
            ],
            axis=0,
        )
        picked = jnp.dot(parent_table[...], source, preferred_element_type=F32)
        for i in range(2 * pslots):
            for k, n in enumerate(members):
                prows_scr[:, n, i * rank_width : (i + 1) * rank_width] = picked[
                    i * parents : (i + 1) * parents, k * rank_width : (k + 1) * rank_width
                ]
    start = mine + len(packs(vs, rank_width, leaves)) * parents
    for ref in extras:
        out_ref[start : start + ref.shape[0], :] = ref[...]
        start += ref.shape[0]

    accs = tuple(jnp.zeros((rank_width, leaves), F32) for _ in range(vs))
    turns = parents // (2 * slots)
    width = rank_width // turns
    for s in range(2 * slots):
        if s >= slots:
            copies[s - slots].wait()
        ref, i = (own_ref, s) if s < slots else (couple_scr, s - slots)

        def body(turn, carry, s=s, ref=ref, i=i):
            parent = s * turns + turn
            pout_scr[parent] = jnp.dot(
                prows_scr[parent].astype(BF16), pcouple_ref[parent], preferred_element_type=F32
            )
            for k in range(width):
                j = turn * width + k
                weight = ref[i, j].astype(F32)
                carry = tuple(
                    acc + weight * rows_scr[s, pl.ds(n * rank_width + j, 1), :]
                    for n, acc in enumerate(carry)
                )
            return carry

        accs = lax.fori_loop(0, turns, body, accs)
    for n in range(vs):
        out_ref[n * rank_width : (n + 1) * rank_width, :] = accs[n].astype(out_ref.dtype)
    for b, members in enumerate(packs(vs, rank_width, leaves)):
        parts = [pout_scr[:, n, :] for n in members]
        missing = leaves - len(parts) * rank_width
        if missing:
            parts.append(jnp.zeros((parents, missing), F32))
        out_ref[mine + b * parents : mine + (b + 1) * parents, :] = jnp.concatenate(
            parts, axis=1
        ).astype(out_ref.dtype)


def down_kernel(vs, parents, keep_ref, *refs):
    recvs, down_ref, out_ref, rows_scr = refs[:-3], refs[-3], refs[-2], refs[-1]
    rank_width, _, leaves = down_ref.shape
    total = keep_ref[...]
    for ref in recvs:
        total = total + ref[0 : total.shape[0], :].astype(F32)
    mine = vs * rank_width
    below = (iota((parents, leaves), 1) // (leaves // parents)) == iota((parents, leaves), 0)
    spread = jnp.where(below, 1.0, 0.0).astype(BF16)
    for b, members in enumerate(packs(vs, rank_width, leaves)):
        part = total[mine + b * parents : mine + (b + 1) * parents, :].astype(BF16)
        wide = lax.dot_general(
            part, spread, (((0,), (0,)), ((), ())), preferred_element_type=F32
        )
        count = len(members) * rank_width
        start = members[0] * rank_width
        rows_scr[start : start + count, :] = wide[:count]
    accs = mac_rows(
        rank_width,
        lambda j: down_ref[j].astype(F32),
        lambda j, n: row_of(rows_scr, n * rank_width + j),
        [total[n * rank_width : (n + 1) * rank_width, :] for n in range(vs)],
        8,
    )
    for n in range(vs):
        out_ref[n * rank_width : (n + 1) * rank_width, :] = accs[n].astype(BF16)


def near_kernel(
    vh, step, ids_ref, own_field, peer_field, own_ref, peer_any, out_ref, peer_scr, acc_scr, sems
):
    slab, _, leaves = own_ref.shape
    group = 6
    target = pl.multiple_of((ids_ref[1] ^ step) * (2 * slab), 2 * slab)
    copies = []
    for c in range(4):
        part = slice(c * slab // 4, (c + 1) * slab // 4)
        copies.append(
            pltpu.make_async_copy(
                peer_any.at[part, pl.ds(target, 2 * slab), :], peer_scr.at[part], sems.at[c]
            )
        )
        copies[-1].start()

    def products(field_ref, ref, base, first, half, accs):
        span = pl.ds(pl.multiple_of(base + half * slab, slab), slab)
        return mac_rows(
            slab,
            lambda p: ref[p, span, :].astype(F32),
            lambda p, n: row_of(field_ref, p * vh + first + n),
            accs,
            16,
        )

    places = [(half, first) for half in range(2) for first in range(0, vh, group)]
    for half, first in places:
        accs = [jnp.zeros((slab, leaves), F32) for _ in range(group)]
        accs = products(own_field, own_ref, target, first, half, accs)
        for n in range(group):
            start = (half * vh + first + n) * slab
            acc_scr[start : start + slab, :] = accs[n]
    for copy in copies:
        copy.wait()
    for half, first in places:
        starts = [(half * vh + first + n) * slab for n in range(group)]
        accs = [acc_scr[start : start + slab, :] for start in starts]
        accs = products(peer_field, peer_scr, 0, first, half, accs)
        for n, start in enumerate(starts):
            out_ref[start : start + slab, :] = accs[n].astype(out_ref.dtype)


def near_sum_kernel(skip, ids_ref, keep_ref, last_ref, *refs):
    recvs, mine_ref, send_ref = refs[:-2], refs[-2], refs[-1]
    count = mine_ref.shape[0]
    parity = ids_ref[2]

    def summed(start):
        start = pl.multiple_of(start, 16)
        total = keep_ref[pl.ds(start, count), :] + last_ref[pl.ds(start, count), :].astype(F32)
        for ref in recvs:
            total = total + ref[pl.ds(skip + start, count), :].astype(F32)
        return total

    mine_ref[...] = summed(parity * count)
    send_ref[...] = summed((1 - parity) * count).astype(BF16)


def column_kernel(vs, column_ref, mine_ref, other_ref, out_ref, rows_scr):
    rank_width, voxels, leaves = column_ref.shape
    rows_scr[0] = mine_ref[...].astype(F32)
    rows_scr[1] = other_ref[...].astype(F32)
    accs = mac_rows(
        rank_width,
        lambda k: column_ref[k].astype(F32),
        lambda k, n: rows_scr[n // vs, pl.ds((n % vs) * rank_width + k, 1), :],
        [jnp.zeros((voxels, leaves), F32) for _ in range(2 * vs)],
        8,
    )
    for n in range(2 * vs):
        out_ref[n * voxels : (n + 1) * voxels, :] = accs[n]


def out_kernel(lvls, vh, vs, early, ids_ref, column_ref, near_mine, near_peer, *refs):
    done, blocks = refs[:early], refs[early : -3]
    out_ref, rows_scr, out_scr = refs[-3:]
    rank_width, voxels, leaves = column_ref.shape
    vectors = out_ref.shape[1]
    lvl, parity = ids_ref[1], ids_ref[2]
    late = lvls - early
    for b, ref in enumerate(blocks):
        rows_scr[b] = ref[...].astype(F32)

    def store(place, rep, value):
        def write():
            vector = place * 2 + (parity if rep == 0 else 1 - parity)
            out_scr[pl.ds(vector, voxels, stride=vectors), :] = value

        if lvls * vs == vh:
            write()
        else:
            pl.when(place < vh)(write)

    for t in range(lvls):
        first = (lvl ^ t) * vs
        if t < early:
            accs = [done[t][n * voxels : (n + 1) * voxels, :] for n in range(2 * vs)]
        else:
            accs = mac_rows(
                rank_width,
                lambda k: column_ref[k].astype(F32),
                lambda k, n: rows_scr[
                    (n // vs) * late + t - early, pl.ds((n % vs) * rank_width + k, 1), :
                ],
                [jnp.zeros((voxels, leaves), F32) for _ in range(2 * vs)],
                8,
            )
        for n in range(2 * vs):
            place = first + n % vs
            near_ref = (near_mine, near_peer)[n // vs]
            inside = jnp.minimum(place, vh - 1)
            near = near_ref[pl.ds(pl.multiple_of(inside * voxels, voxels), voxels), :]
            store(place, n // vs, accs[n] + near.astype(F32))
    whole = out_scr[0 : voxels * vectors, :]
    out_ref[...] = whole.reshape(voxels, vectors, leaves).astype(BF16)


def after(value, *others):
    return lax.optimization_barrier((value,) + others)[0]


def per_device(sizes, *args):
    (
        voxel_field, row_basis, near_block, up_transfer, coupling, parent_coupling,
        down_transfer, column_basis, parent_perm, partner_owner, partner_local,
        parent_owner, parent_local, block_count,
    ) = args
    owners, lvls, reps = sizes
    slab, vectors, leaves = voxel_field.shape
    rank_width = row_basis.shape[1]
    parents = parent_coupling.shape[4]
    children = leaves // parents
    slots = partner_owner.shape[2]
    pslots = parent_owner.shape[2]
    vh = vectors // reps
    vs = -(-vh // lvls)
    sds = jax.ShapeDtypeStruct

    me = lax.axis_index("clus")
    lvl = lax.axis_index("lvl")
    parity = lax.axis_index("rep")
    ids = jnp.stack([me, lvl, parity]).astype(jnp.int32)

    def call(name, kernel, ins, outs, scratch=(), us=1.0, scalars=0, whole=()):
        specs = [
            smem() if i < scalars else pl.BlockSpec(memory_space=pltpu.HBM) if i in whole else vmem()
            for i in range(len(ins))
        ]
        with jax.named_scope(name):
            return pl.pallas_call(
                kernel,
                out_shape=outs,
                in_specs=specs,
                out_specs=jax.tree.map(lambda _: vmem(), outs),
                scratch_shapes=list(scratch),
                compiler_params=params(),
                cost_estimate=cost(0, int(us * 3.3e6)),
            )(*ins)

    def swap(value, axis, count, step):
        return lax.ppermute(value, axis, [(i, i ^ step) for i in range(count)])

    def swaps(values, axis, count, backward=True):
        order = range(count - 1, 0, -1) if backward else range(1, count)
        got = {n: swap(values[n], axis, count, n) for n in order}
        return [got[n] for n in range(1, count)]

    def other(value):
        return swap(value, "rep", reps, 1)

    with jax.named_scope("swap_row_basis"):
        row_peer = other(row_basis)

    with jax.named_scope("swap_parent_coupling"):
        pcouple = jnp.transpose(parent_coupling, (0, 2, 3, 4, 1)).reshape(
            rank_width, pslots * parents, rank_width
        )
        pcouple_peer = other(pcouple)

    with jax.named_scope("swap_self_blocks"):
        near_peer_block = other(near_block)

    chunk_rows = 2 * (slab // owners) * vh
    packed = call(
        "pack_field",
        functools.partial(pack_kernel, owners, vh, parents),
        (
            ids,
            pltpu.with_memory_space_constraint(parent_perm, pltpu.HBM),
            pltpu.with_memory_space_constraint(voxel_field, pltpu.HBM),
        ),
        sds((owners, chunk_rows, leaves), BF16),
        [
            pltpu.VMEM((slab * vectors + 8, leaves), F32),
            pltpu.SMEM(parent_perm.shape, jnp.int32),
            pltpu.VMEM(voxel_field.shape, BF16),
            pltpu.SemaphoreType.DMA((5,)),
        ],
        1.0, scalars=1, whole=(1, 2),
    )
    with jax.named_scope("regroup_sends"):
        chunks = [packed[0]] + swaps([packed[s] for s in range(owners)], "clus", owners, False)
    codes = call(
        "place_codes",
        functools.partial(place_kernel, owners, parents),
        (after(ids, chunks[1]), pltpu.with_memory_space_constraint(parent_perm, pltpu.HBM)),
        sds((8, leaves), jnp.int32),
        [
            pltpu.SMEM((parents + 1,), jnp.int32),
            pltpu.SMEM(parent_perm.shape, jnp.int32),
            pltpu.SemaphoreType.DMA,
        ],
        0.3, scalars=1, whole=(1,),
    )
    with jax.named_scope("coupling_layout"):
        couple = jnp.moveaxis(after(coupling, chunks[1])[:, :, 0], 2, 0)

    with jax.named_scope("partner_codes"):
        held = lax.optimization_barrier(
            (partner_owner, partner_local, parent_owner, parent_local, block_count, chunks[1])
        )
        group = lvl * reps + parity
        row = jnp.arange(slots + pslots, dtype=jnp.int32)[:, None]
        wide = ((0, 0), (0, leaves - parents))
        owner = jnp.concatenate([held[0][0].T, jnp.pad(held[2][0].T, wide)], axis=0) ^ me
        local = jnp.concatenate([held[1][0].T, jnp.pad(held[3][0].T, wide)], axis=0)
        live = (row >= slots) | (group * slots + row < held[4][None, :])
        partners = owner * jnp.where(row < slots, leaves, parents) + local
        partners = jnp.where(live, partners, -1)
        partners_peer = other(partners)
    codes = after(codes, couple, row_peer, partners_peer)

    field, field_send = call(
        "regroup_field",
        functools.partial(regroup_kernel, owners),
        (codes, *chunks),
        [sds((slab * vh, leaves), F32), sds((slab * vh, leaves), BF16)],
        (), 0.4,
    )
    with jax.named_scope("swap_field"):
        field_recv = other(field_send)
    coeff_own = call(
        "coeffs_own_slab",
        functools.partial(coeff_own_kernel, lvls, vh, vs),
        (ids, row_basis, field),
        sds((lvls * vs * rank_width, leaves), F32),
        (), 1.6, scalars=1,
    )
    outs = call(
        "coeffs_other_slab",
        functools.partial(coeff_peer_kernel, lvls, vh, vs),
        (ids, row_peer, field_recv, coeff_own),
        [sds((slab * vh, leaves), F32), sds((vs * rank_width, leaves), F32)]
        + [sds((vs * rank_width, leaves), BF16)] * (lvls - 1),
        (), 1.6, scalars=1,
    )
    field_peer, keep, sends = outs[0], outs[1], outs[2:]
    with jax.named_scope("coeff_sends"):
        recvs = swaps([None, *sends], "lvl", lvls, True)

    with jax.named_scope("swap_coupling"):
        couple_peer = other(after(couple, keep))

    def near_part(t, place):
        return call(
            "self_blocks",
            functools.partial(near_kernel, vh, t),
            (ids, place, field_peer, near_block, near_peer_block),
            sds((2 * vh * slab, leaves), F32 if t == 0 else BF16),
            [
                pltpu.VMEM((slab, 2 * slab, leaves), BF16),
                pltpu.VMEM((2 * vh * slab, leaves), F32),
                pltpu.SemaphoreType.DMA((4,)),
            ],
            2.4, scalars=1, whole=(4,),
        )

    near_parts = [None] * lvls
    near_parts[1] = near_part(1, after(field, keep))
    up_after = after(up_transfer, near_parts[1])

    block_rows = vs * rank_width + len(packs(vs, rank_width, leaves)) * parents
    block = call(
        "parent_coeffs",
        functools.partial(up_kernel, vs, parents),
        (keep, *recvs[::-1], up_after),
        sds((block_rows, leaves), BF16),
        [pltpu.VMEM((vs * rank_width, leaves), F32)],
        0.8,
    )
    with jax.named_scope("owner_sends"):
        blocks = [block] + swaps([block] * owners, "clus", owners, False)
    later = after(field, block)
    for t in range(2, lvls):
        near_parts[t] = near_part(t, later)
    with jax.named_scope("all_owners"):
        blocks = list(lax.optimization_barrier(tuple(blocks) + tuple(near_parts[2:])))[:owners]
        mine = jnp.concatenate(blocks, axis=0)
    with jax.named_scope("level_sends"):
        alls = [mine] + swaps([mine] * lvls, "lvl", lvls, False)

    later = after(field, mine)
    near_parts[0] = near_part(0, later)
    leaf_table, parent_table, pcouple_all = call(
        "partner_tables",
        functools.partial(table_kernel, owners, parents, slots),
        (after(partners, mine), partners_peer, pcouple, pcouple_peer),
        [
            sds((owners * leaves, 2 * slots * leaves), BF16),
            sds((2 * pslots * parents, owners * parents), BF16),
            sds((parents, 2 * pslots * rank_width, rank_width), BF16),
        ],
        [pltpu.VMEM(((rank_width + 1) * pslots * parents, rank_width), F32)],
        1.5,
    )
    def far_part(t, block):
        extras = (near_parts[t],) if 0 < t < lvls - 1 else ()
        rows = block_rows + (2 * vh * slab if extras else 0)
        return call(
            "coupling_products",
            functools.partial(far_kernel, owners, vs, pslots),
            (leaf_table, parent_table, pcouple_all, block, *extras, couple, couple_peer),
            sds((rows, leaves), F32 if t == 0 else BF16),
            [
                pltpu.VMEM((2 * slots, vs * rank_width, leaves), F32),
                pltpu.VMEM((parents, 8, 2 * pslots * rank_width), F32),
                pltpu.VMEM((parents, 8, rank_width), F32),
                pltpu.VMEM((slots, rank_width, rank_width, leaves), BF16),
                pltpu.SemaphoreType.DMA((slots,)),
            ],
            3.2, whole=(5 + len(extras),),
        )

    alls[1] = after(alls[1], near_parts[0])
    far_parts = [far_part(t, alls[t]) for t in range(lvls)]
    with jax.named_scope("far_sends"):
        far_recvs = swaps(far_parts, "lvl", lvls, False)
    with jax.named_scope("self_sends"):
        last = lvls - 1
        near_recv = swap(after(near_parts[last], far_recvs[-1], far_parts[0]), "lvl", lvls, last)
    far = call(
        "down_products",
        functools.partial(down_kernel, vs, parents),
        (far_parts[0], *far_recvs, down_transfer),
        sds((vs * rank_width, leaves), BF16),
        [pltpu.VMEM((vs * rank_width, leaves), F32)],
        0.8,
    )
    with jax.named_scope("far_coeff_sends"):
        far_blocks = [far] + swaps([far] * lvls, "lvl", lvls, True)
        far_others = [other(value) for value in far_blocks]
    early = lvls - 1
    done = [
        call(
            "column_products_early",
            functools.partial(column_kernel, vs),
            (column_basis, far_blocks[t], far_others[t]),
            sds((2 * vs * slab, leaves), F32),
            [pltpu.VMEM((2, vs * rank_width, leaves), F32)],
            0.5,
        )
        for t in range(early)
    ]
    near_mine, near_send = call(
        "self_sums",
        functools.partial(near_sum_kernel, block_rows),
        (ids, after(near_parts[0], done[0]), near_recv, *far_recvs[:-1]),
        [sds((vh * slab, leaves), F32), sds((vh * slab, leaves), BF16)],
        (), 0.65, scalars=1,
    )
    with jax.named_scope("swap_self_sums"):
        near_peer = other(near_send)
    return call(
        "column_products",
        functools.partial(out_kernel, lvls, vh, vs, early),
        (
            ids, column_basis, near_mine, near_peer, *done,
            *far_blocks[early:], *far_others[early:],
        ),
        sds((slab, vectors, leaves), BF16),
        [
            pltpu.VMEM((2 * (lvls - early), vs * rank_width, leaves), F32),
            pltpu.VMEM(((slab + 1) * vectors, leaves), F32),
        ],
        1.85, scalars=1,
    )


def solution(mesh):
    sizes = (mesh.shape["clus"], mesh.shape["lvl"], mesh.shape["rep"])
    return jax.shard_map(
        functools.partial(per_device, sizes),
        mesh=mesh,
        in_specs=(
            P(("lvl", "rep"), None, ("parts", "clus")),
            P(("lvl", "rep"), None, ("parts", "clus")),
            P(("lvl", "rep"), None, ("parts", "clus")),
            P(None, None, ("parts", "clus")),
            P(None, None, ("lvl", "rep"), None, ("parts", "clus")),
            P(None, None, ("lvl", "rep"), None, ("parts", "clus")),
            P(None, None, ("parts", "clus")),
            P(None, ("lvl", "rep"), ("parts", "clus")),
            P("parts"),
            P(("lvl", "rep"), ("parts", "clus"), None),
            P(("lvl", "rep"), ("parts", "clus"), None),
            P(("lvl", "rep"), ("parts", "clus"), None),
            P(("lvl", "rep"), ("parts", "clus"), None),
            P(("parts", "clus")),
        ),
        out_specs=P(("lvl", "rep"), None, ("parts", "clus")),
        check_vma=False,
    )
```

```python
import functools

import jax
import jax.numpy as jnp
from jax import lax
from jax.experimental import pallas as pl
from jax.experimental.pallas import tpu as pltpu
from jax.sharding import PartitionSpec as P

F32 = jnp.float32
BF16 = jnp.bfloat16
VMEM_LIMIT = 12 * 1024 * 1024


def vmem():
    return pl.BlockSpec(memory_space=pltpu.VMEM)


def smem():
    return pl.BlockSpec(memory_space=pltpu.SMEM)


def params(**more):
    return pltpu.CompilerParams(vmem_limit_bytes=VMEM_LIMIT, **more)


def cost(flops, nbytes):
    return pl.CostEstimate(flops=flops, bytes_accessed=nbytes, transcendentals=0)


def iota(shape, dim):
    return lax.broadcasted_iota(jnp.int32, shape, dim)


def row_of(ref, row):
    return ref[pl.ds(row, 1), :]


def mac_rows(total_steps, weight_at, row_at, accs, unroll):
    def body(step, carry):
        weight = weight_at(step)
        return tuple(acc + weight * row_at(step, n) for n, acc in enumerate(carry))

    return lax.fori_loop(0, total_steps, body, tuple(accs), unroll=unroll)


def pack_kernel(
    owners, vh, parents, ids_ref, perm_any, own_any, out_ref, rows_scr, perm_ref, own_ref, sems
):
    slab, vectors, leaves = own_ref.shape
    perm_copy = pltpu.make_async_copy(perm_any, perm_ref, sems.at[0])
    perm_copy.start()
    copies = []
    for c in range(4):
        part = slice(c * slab // 4, (c + 1) * slab // 4)
        copies.append(
            pltpu.make_async_copy(own_any.at[part], own_ref.at[part], sems.at[1 + c])
        )
        copies[-1].start()
    children = leaves // parents
    reps = vectors // vh
    width = leaves // owners
    me, parity = ids_ref[0], ids_ref[2]
    row = iota((leaves, leaves), 0)
    lane = iota((leaves, leaves), 1)
    parent_of_row = row // children
    target = row % children
    bits = 32 // owners
    counts = jnp.int32(0)
    perm_copy.wait()
    for parent in range(parents):
        owner = perm_ref[me * parents + parent] // parents
        shift = owner * bits
        rank = lax.shift_right_logical(counts, shift) & ((1 << bits) - 1)
        counts = counts + lax.shift_left(jnp.int32(1), shift)
        code = (owner ^ me) * leaves + rank * children
        target = target + jnp.where(parent_of_row == parent, code, 0)
    part = (slab // owners) * vh
    for copy in copies:
        copy.wait()
    rows_scr[0 : slab * vectors, :] = own_ref[...].reshape(slab * vectors, leaves).astype(F32)
    pieces = []
    for q in range(owners):
        start = q * (slab // owners) * vectors
        pieces.append(
            jnp.concatenate(
                [
                    rows_scr[pl.ds(start + first, part, stride=reps), :]
                    for first in (parity, 1 - parity)
                ],
                axis=0,
            ).astype(BF16)
        )
    for s in range(owners):
        total = jnp.zeros((2 * part, leaves), F32)
        for q in range(owners):
            onehot = jnp.where(target + (q * width - s * leaves) == lane, 1.0, 0.0).astype(BF16)
            total = total + jnp.dot(pieces[q], onehot, preferred_element_type=F32)
        out_ref[s] = total.astype(BF16)


def place_kernel(owners, parents, ids_ref, perm_any, out_ref, code_scr, perm_ref, sem):
    copy = pltpu.make_async_copy(perm_any, perm_ref, sem)
    copy.start()
    copy.wait()
    leaves = out_ref.shape[1]
    children = leaves // parents
    me = ids_ref[0]
    for source in range(owners):
        rank = jnp.int32(0)
        base = (source ^ me) * leaves
        for parent in range(parents):
            place = perm_ref[source * parents + parent]
            mine = (place // parents) == me
            slot = jnp.where(mine, place % parents, parents)
            code_scr[slot] = base + rank * children
            rank = rank + jnp.where(mine, 1, 0)
    lane = iota(out_ref.shape, 1)
    code = lane % children
    for parent in range(parents):
        code = code + jnp.where(lane // children == parent, code_scr[parent], 0)
    out_ref[...] = code


def regroup_kernel(owners, code_ref, *refs):
    chunks, mine_ref, other_ref = refs[:owners], refs[owners], refs[owners + 1]
    leaves = mine_ref.shape[1]
    width = leaves // owners
    part = mine_ref.shape[0] // owners
    code = jnp.broadcast_to(code_ref[0:1, :], (leaves, leaves))
    row = iota((leaves, leaves), 0)
    for q in range(owners):
        total = jnp.zeros((2 * part, leaves), F32)
        for s in range(owners):
            onehot = jnp.where(code + (q * width - s * leaves) == row, 1.0, 0.0).astype(BF16)
            total = total + jnp.dot(chunks[s][...], onehot, preferred_element_type=F32)
        mine_ref[q * part : (q + 1) * part, :] = total[:part]
        other_ref[q * part : (q + 1) * part, :] = total[part:].astype(BF16)


def coeff_products(lvl, lvls, vh, vs, basis_ref, field_ref, start_of, finish):
    slab, rank_width, leaves = basis_ref.shape
    half = rank_width // 2
    for first_t in range(0, lvls, 2):
        members = [(t, n) for t in (first_t, first_t + 1) for n in range(vs)]
        places = [jnp.minimum((lvl ^ t) * vs + n, vh - 1) for t, n in members]
        for low in range(0, rank_width, half):
            part = slice(low, low + half)
            accs = mac_rows(
                slab,
                lambda m: basis_ref[m, part, :].astype(F32),
                lambda m, n: row_of(field_ref, m * vh + places[n]),
                [start_of(t, n, low, half) for t, n in members],
                8,
            )
            for (t, n), acc in zip(members, accs):
                finish(t, n, low, half, acc)


def coeff_own_kernel(lvls, vh, vs, ids_ref, basis_ref, field_ref, out_ref):
    rank_width, leaves = basis_ref.shape[1:]

    def finish(t, n, low, half, acc):
        start = (t * vs + n) * rank_width + low
        out_ref[start : start + half, :] = acc

    coeff_products(
        ids_ref[1], lvls, vh, vs, basis_ref, field_ref,
        lambda t, n, low, half: jnp.zeros((half, leaves), F32), finish,
    )


def coeff_peer_kernel(
    lvls, vh, vs, ids_ref, basis_ref, field_ref, own_ref, wide_ref, keep_ref, *sends
):
    rank_width = basis_ref.shape[1]
    wide_ref[...] = field_ref[...].astype(F32)

    def start_of(t, n, low, half):
        start = (t * vs + n) * rank_width + low
        return own_ref[start : start + half, :]

    def finish(t, n, low, half, acc):
        start = n * rank_width + low
        if t == 0:
            keep_ref[start : start + half, :] = acc
        else:
            sends[t - 1][start : start + half, :] = acc.astype(BF16)

    coeff_products(ids_ref[1], lvls, vh, vs, basis_ref, wide_ref, start_of, finish)


def packs(vs, rank_width, leaves):
    per = max(1, leaves // rank_width)
    return [list(range(first, min(first + per, vs))) for first in range(0, vs, per)]


def up_kernel(vs, parents, keep_ref, *refs):
    recvs, up_ref, out_ref, coeff_scr = refs[:-3], refs[-3], refs[-2], refs[-1]
    rank_width, _, leaves = up_ref.shape
    total = keep_ref[...]
    for ref in recvs:
        total = total + ref[...].astype(F32)
    coeffs = total.astype(BF16)
    out_ref[0 : vs * rank_width, :] = coeffs
    coeff_scr[...] = coeffs.astype(F32)
    accs = mac_rows(
        rank_width,
        lambda j: up_ref[j].astype(F32),
        lambda j, n: row_of(coeff_scr, n * rank_width + j),
        [jnp.zeros((rank_width, leaves), F32) for _ in range(vs)],
        8,
    )
    mine = (iota((parents, leaves), 1) // (leaves // parents)) == iota((parents, leaves), 0)
    group = jnp.where(mine, 1.0, 0.0).astype(BF16)
    for b, members in enumerate(packs(vs, rank_width, leaves)):
        sums = []
        for n in members:
            rest, result = accs[n], jnp.zeros((parents, rank_width), F32)
            for _ in range(3):
                piece = rest.astype(BF16)
                result = result + lax.dot_general(
                    group, piece, (((1,), (1,)), ((), ())), preferred_element_type=F32
                )
                rest = rest - piece.astype(F32)
            sums.append(result)
        missing = leaves - len(sums) * rank_width
        if missing:
            sums.append(jnp.zeros((parents, missing), F32))
        start = vs * rank_width + b * parents
        out_ref[start : start + parents, :] = jnp.concatenate(sums, axis=1).astype(BF16)


def table_kernel(
    owners, parents, slots, own_codes, peer_codes, own_ref, peer_ref,
    leaf_out, parent_out, couple_out, rows_scr,
):
    leaves = own_codes.shape[1]
    sources = leaf_out.shape[0]
    count = parent_out.shape[0] // 2
    for half, codes in enumerate((own_codes, peer_codes)):
        for i in range(slots):
            hit = jnp.broadcast_to(codes[i : i + 1, :], (sources, leaves)) == iota(
                (sources, leaves), 0
            )
            start = (half * slots + i) * leaves
            leaf_out[:, start : start + leaves] = jnp.where(hit, 1.0, 0.0).astype(BF16)
        uppers = owners * parents
        same = iota((uppers, uppers), 0) == iota((uppers, uppers), 1)
        same = jnp.where(same, 1.0, 0.0).astype(BF16)
        pslots = count // parents
        for i in range(pslots):
            code = jnp.broadcast_to(codes[slots + i : slots + i + 1, :], (uppers, leaves))
            hit = jnp.where(code == iota(code.shape, 0), 1.0, 0.0).astype(BF16)
            turned = lax.dot_general(
                hit, same, (((0,), (0,)), ((), ())), preferred_element_type=F32
            )
            start = half * count + i * parents
            parent_out[start : start + parents, :] = turned[:parents].astype(BF16)
    rank_width, pslots = own_ref.shape[0], own_ref.shape[1] // parents
    for half, ref in enumerate((own_ref, peer_ref)):
        blocks = ref[...].reshape(rank_width * pslots * parents, rank_width)
        rows_scr[0 : blocks.shape[0], :] = blocks.astype(F32)
        for i in range(pslots):
            place = (half * pslots + i) * rank_width
            for parent in range(parents):
                block = rows_scr[pl.ds(i * parents + parent, rank_width, stride=pslots * parents), :]
                couple_out[parent, place : place + rank_width, :] = block.astype(BF16)


def far_kernel(owners, vs, pslots, leaf_table, parent_table, pcouple_ref, block_ref, *refs):
    extras = refs[:-8]
    own_ref, peer_any, out_ref, rows_scr, prows_scr, pout_scr, couple_scr, sems = refs[-8:]
    slots, rank_width, _, leaves = own_ref.shape
    parents = pcouple_ref.shape[0]
    copies = []
    for i in range(slots):
        copies.append(pltpu.make_async_copy(peer_any.at[i], couple_scr.at[i], sems.at[i]))
        copies[-1].start()
    per_block = block_ref.shape[0] // owners
    mine = vs * rank_width
    rows = jnp.zeros((mine, 2 * slots * leaves), F32)
    for o in range(0, owners, 2):
        pair = [block_ref[p * per_block : p * per_block + mine, :] for p in (o, o + 1)]
        rows = rows + jnp.dot(
            jnp.concatenate(pair, axis=1),
            leaf_table[o * leaves : (o + 2) * leaves, :],
            preferred_element_type=F32,
        )
    for i in range(2 * slots):
        rows_scr[i] = rows[:, i * leaves : (i + 1) * leaves]

    for b, members in enumerate(packs(vs, rank_width, leaves)):
        source = jnp.concatenate(
            [
                block_ref[pl.ds(o * per_block + mine + b * parents, parents), :]
                for o in range(owners)
            ],
            axis=0,
        )
        picked = jnp.dot(parent_table[...], source, preferred_element_type=F32)
        for i in range(2 * pslots):
            for k, n in enumerate(members):
                prows_scr[:, n, i * rank_width : (i + 1) * rank_width] = picked[
                    i * parents : (i + 1) * parents, k * rank_width : (k + 1) * rank_width
                ]
    start = mine + len(packs(vs, rank_width, leaves)) * parents
    for ref in extras:
        out_ref[start : start + ref.shape[0], :] = ref[...]
        start += ref.shape[0]

    accs = tuple(jnp.zeros((rank_width, leaves), F32) for _ in range(vs))
    turns = parents // (2 * slots)
    width = rank_width // turns
    for s in range(2 * slots):
        if s >= slots:
            copies[s - slots].wait()
        ref, i = (own_ref, s) if s < slots else (couple_scr, s - slots)

        def body(turn, carry, s=s, ref=ref, i=i):
            parent = s * turns + turn
            pout_scr[parent] = jnp.dot(
                prows_scr[parent].astype(BF16), pcouple_ref[parent], preferred_element_type=F32
            )
            for k in range(width):
                j = turn * width + k
                weight = ref[i, j].astype(F32)
                carry = tuple(
                    acc + weight * rows_scr[s, pl.ds(n * rank_width + j, 1), :]
                    for n, acc in enumerate(carry)
                )
            return carry

        accs = lax.fori_loop(0, turns, body, accs)
    for n in range(vs):
        out_ref[n * rank_width : (n + 1) * rank_width, :] = accs[n].astype(out_ref.dtype)
    for b, members in enumerate(packs(vs, rank_width, leaves)):
        parts = [pout_scr[:, n, :] for n in members]
        missing = leaves - len(parts) * rank_width
        if missing:
            parts.append(jnp.zeros((parents, missing), F32))
        out_ref[mine + b * parents : mine + (b + 1) * parents, :] = jnp.concatenate(
            parts, axis=1
        ).astype(out_ref.dtype)


def down_kernel(vs, parents, keep_ref, *refs):
    recvs, down_ref, out_ref, rows_scr = refs[:-3], refs[-3], refs[-2], refs[-1]
    rank_width, _, leaves = down_ref.shape
    total = keep_ref[...]
    for ref in recvs:
        total = total + ref[0 : total.shape[0], :].astype(F32)
    mine = vs * rank_width
    below = (iota((parents, leaves), 1) // (leaves // parents)) == iota((parents, leaves), 0)
    spread = jnp.where(below, 1.0, 0.0).astype(BF16)
    for b, members in enumerate(packs(vs, rank_width, leaves)):
        part = total[mine + b * parents : mine + (b + 1) * parents, :].astype(BF16)
        wide = lax.dot_general(
            part, spread, (((0,), (0,)), ((), ())), preferred_element_type=F32
        )
        count = len(members) * rank_width
        start = members[0] * rank_width
        rows_scr[start : start + count, :] = wide[:count]
    accs = mac_rows(
        rank_width,
        lambda j: down_ref[j].astype(F32),
        lambda j, n: row_of(rows_scr, n * rank_width + j),
        [total[n * rank_width : (n + 1) * rank_width, :] for n in range(vs)],
        8,
    )
    for n in range(vs):
        out_ref[n * rank_width : (n + 1) * rank_width, :] = accs[n].astype(BF16)


def near_kernel(
    vh, step, ids_ref, own_field, peer_field, own_ref, peer_any, out_ref, peer_scr, acc_scr, sems
):
    slab, _, leaves = own_ref.shape
    group = 6
    target = pl.multiple_of((ids_ref[1] ^ step) * (2 * slab), 2 * slab)
    copies = []
    for c in range(4):
        part = slice(c * slab // 4, (c + 1) * slab // 4)
        copies.append(
            pltpu.make_async_copy(
                peer_any.at[part, pl.ds(target, 2 * slab), :], peer_scr.at[part], sems.at[c]
            )
        )
        copies[-1].start()

    def products(field_ref, ref, base, first, half, accs):
        span = pl.ds(pl.multiple_of(base + half * slab, slab), slab)
        return mac_rows(
            slab,
            lambda p: ref[p, span, :].astype(F32),
            lambda p, n: row_of(field_ref, p * vh + first + n),
            accs,
            16,
        )

    places = [(half, first) for half in range(2) for first in range(0, vh, group)]
    for half, first in places:
        accs = [jnp.zeros((slab, leaves), F32) for _ in range(group)]
        accs = products(own_field, own_ref, target, first, half, accs)
        for n in range(group):
            start = (half * vh + first + n) * slab
            acc_scr[start : start + slab, :] = accs[n]
    for copy in copies:
        copy.wait()
    for half, first in places:
        starts = [(half * vh + first + n) * slab for n in range(group)]
        accs = [acc_scr[start : start + slab, :] for start in starts]
        accs = products(peer_field, peer_scr, 0, first, half, accs)
        for n, start in enumerate(starts):
            out_ref[start : start + slab, :] = accs[n].astype(out_ref.dtype)


def near_sum_kernel(skip, ids_ref, keep_ref, last_ref, *refs):
    recvs, mine_ref, send_ref = refs[:-2], refs[-2], refs[-1]
    count = mine_ref.shape[0]
    parity = ids_ref[2]

    def summed(start):
        start = pl.multiple_of(start, 16)
        total = keep_ref[pl.ds(start, count), :] + last_ref[pl.ds(start, count), :].astype(F32)
        for ref in recvs:
            total = total + ref[pl.ds(skip + start, count), :].astype(F32)
        return total

    mine_ref[...] = summed(parity * count)
    send_ref[...] = summed((1 - parity) * count).astype(BF16)


def column_kernel(vs, column_ref, *refs):
    blocks, out_ref, rows_scr = refs[:-2], refs[-2], refs[-1]
    rank_width, voxels, leaves = column_ref.shape
    for b, ref in enumerate(blocks):
        rows_scr[b] = ref[...].astype(F32)
    count = len(blocks) * vs
    accs = mac_rows(
        rank_width,
        lambda k: column_ref[k].astype(F32),
        lambda k, n: rows_scr[n // vs, pl.ds((n % vs) * rank_width + k, 1), :],
        [jnp.zeros((voxels, leaves), F32) for _ in range(count)],
        8,
    )
    for n in range(count):
        out_ref[n * voxels : (n + 1) * voxels, :] = accs[n]


def out_kernel(lvls, vh, vs, early, ids_ref, column_ref, near_mine, near_peer, *refs):
    done, last_mine, last_other = refs[:early], refs[early], refs[early + 1]
    out_ref, rows_scr, out_scr = refs[-3:]
    rank_width, voxels, leaves = column_ref.shape
    vectors = out_ref.shape[1]
    lvl, parity = ids_ref[1], ids_ref[2]
    rows_scr[...] = last_other[...].astype(F32)

    def store(place, rep, value):
        def write():
            vector = place * 2 + (parity if rep == 0 else 1 - parity)
            out_scr[pl.ds(vector, voxels, stride=vectors), :] = value

        if lvls * vs == vh:
            write()
        else:
            pl.when(place < vh)(write)

    for t in range(lvls):
        first = (lvl ^ t) * vs
        if t < early:
            accs = [done[t][n * voxels : (n + 1) * voxels, :] for n in range(2 * vs)]
        else:
            accs = [last_mine[n * voxels : (n + 1) * voxels, :] for n in range(vs)]
            accs += mac_rows(
                rank_width,
                lambda k: column_ref[k].astype(F32),
                lambda k, n: row_of(rows_scr, n * rank_width + k),
                [jnp.zeros((voxels, leaves), F32) for _ in range(vs)],
                8,
            )
        for n in range(2 * vs):
            place = first + n % vs
            near_ref = (near_mine, near_peer)[n // vs]
            inside = jnp.minimum(place, vh - 1)
            near = near_ref[pl.ds(pl.multiple_of(inside * voxels, voxels), voxels), :]
            store(place, n // vs, accs[n] + near.astype(F32))
    whole = out_scr[0 : voxels * vectors, :]
    out_ref[...] = whole.reshape(voxels, vectors, leaves).astype(BF16)


def after(value, *others):
    return lax.optimization_barrier((value,) + others)[0]


def per_device(sizes, *args):
    (
        voxel_field, row_basis, near_block, up_transfer, coupling, parent_coupling,
        down_transfer, column_basis, parent_perm, partner_owner, partner_local,
        parent_owner, parent_local, block_count,
    ) = args
    owners, lvls, reps = sizes
    slab, vectors, leaves = voxel_field.shape
    rank_width = row_basis.shape[1]
    parents = parent_coupling.shape[4]
    children = leaves // parents
    slots = partner_owner.shape[2]
    pslots = parent_owner.shape[2]
    vh = vectors // reps
    vs = -(-vh // lvls)
    sds = jax.ShapeDtypeStruct

    me = lax.axis_index("clus")
    lvl = lax.axis_index("lvl")
    parity = lax.axis_index("rep")
    ids = jnp.stack([me, lvl, parity]).astype(jnp.int32)

    def call(name, kernel, ins, outs, scratch=(), us=1.0, scalars=0, whole=()):
        specs = [
            smem() if i < scalars else pl.BlockSpec(memory_space=pltpu.HBM) if i in whole else vmem()
            for i in range(len(ins))
        ]
        with jax.named_scope(name):
            return pl.pallas_call(
                kernel,
                out_shape=outs,
                in_specs=specs,
                out_specs=jax.tree.map(lambda _: vmem(), outs),
                scratch_shapes=list(scratch),
                compiler_params=params(),
                cost_estimate=cost(0, int(us * 3.3e6)),
            )(*ins)

    def swap(value, axis, count, step):
        return lax.ppermute(value, axis, [(i, i ^ step) for i in range(count)])

    def swaps(values, axis, count, backward=True):
        order = range(count - 1, 0, -1) if backward else range(1, count)
        got = {n: swap(values[n], axis, count, n) for n in order}
        return [got[n] for n in range(1, count)]

    def other(value):
        return swap(value, "rep", reps, 1)

    with jax.named_scope("swap_row_basis"):
        row_peer = other(row_basis)

    with jax.named_scope("swap_parent_coupling"):
        pcouple = jnp.transpose(parent_coupling, (0, 2, 3, 4, 1)).reshape(
            rank_width, pslots * parents, rank_width
        )
        pcouple_peer = other(pcouple)

    with jax.named_scope("swap_self_blocks"):
        near_peer_block = other(near_block)

    chunk_rows = 2 * (slab // owners) * vh
    packed = call(
        "pack_field",
        functools.partial(pack_kernel, owners, vh, parents),
        (
            ids,
            pltpu.with_memory_space_constraint(parent_perm, pltpu.HBM),
            pltpu.with_memory_space_constraint(voxel_field, pltpu.HBM),
        ),
        sds((owners, chunk_rows, leaves), BF16),
        [
            pltpu.VMEM((slab * vectors + 8, leaves), F32),
            pltpu.SMEM(parent_perm.shape, jnp.int32),
            pltpu.VMEM(voxel_field.shape, BF16),
            pltpu.SemaphoreType.DMA((5,)),
        ],
        1.0, scalars=1, whole=(1, 2),
    )
    with jax.named_scope("regroup_sends"):
        chunks = [packed[0]] + swaps([packed[s] for s in range(owners)], "clus", owners, False)
    codes = call(
        "place_codes",
        functools.partial(place_kernel, owners, parents),
        (after(ids, chunks[1]), pltpu.with_memory_space_constraint(parent_perm, pltpu.HBM)),
        sds((8, leaves), jnp.int32),
        [
            pltpu.SMEM((parents + 1,), jnp.int32),
            pltpu.SMEM(parent_perm.shape, jnp.int32),
            pltpu.SemaphoreType.DMA,
        ],
        0.3, scalars=1, whole=(1,),
    )
    with jax.named_scope("coupling_layout"):
        couple = jnp.moveaxis(after(coupling, chunks[1])[:, :, 0], 2, 0)

    with jax.named_scope("partner_codes"):
        held = lax.optimization_barrier(
            (partner_owner, partner_local, parent_owner, parent_local, block_count, chunks[1])
        )
        group = lvl * reps + parity
        row = jnp.arange(slots + pslots, dtype=jnp.int32)[:, None]
        wide = ((0, 0), (0, leaves - parents))
        owner = jnp.concatenate([held[0][0].T, jnp.pad(held[2][0].T, wide)], axis=0) ^ me
        local = jnp.concatenate([held[1][0].T, jnp.pad(held[3][0].T, wide)], axis=0)
        live = (row >= slots) | (group * slots + row < held[4][None, :])
        partners = owner * jnp.where(row < slots, leaves, parents) + local
        partners = jnp.where(live, partners, -1)
        partners_peer = other(partners)
    codes = after(codes, couple, row_peer, partners_peer)

    field, field_send = call(
        "regroup_field",
        functools.partial(regroup_kernel, owners),
        (codes, *chunks),
        [sds((slab * vh, leaves), F32), sds((slab * vh, leaves), BF16)],
        (), 0.4,
    )
    with jax.named_scope("swap_field"):
        field_recv = other(field_send)
    coeff_own = call(
        "coeffs_own_slab",
        functools.partial(coeff_own_kernel, lvls, vh, vs),
        (ids, row_basis, field),
        sds((lvls * vs * rank_width, leaves), F32),
        (), 1.6, scalars=1,
    )
    outs = call(
        "coeffs_other_slab",
        functools.partial(coeff_peer_kernel, lvls, vh, vs),
        (ids, row_peer, field_recv, coeff_own),
        [sds((slab * vh, leaves), F32), sds((vs * rank_width, leaves), F32)]
        + [sds((vs * rank_width, leaves), BF16)] * (lvls - 1),
        (), 1.6, scalars=1,
    )
    field_peer, keep, sends = outs[0], outs[1], outs[2:]
    with jax.named_scope("coeff_sends"):
        recvs = swaps([None, *sends], "lvl", lvls, True)

    with jax.named_scope("swap_coupling"):
        couple_peer = other(after(couple, keep))

    def near_part(t, place):
        return call(
            "self_blocks",
            functools.partial(near_kernel, vh, t),
            (ids, place, field_peer, near_block, near_peer_block),
            sds((2 * vh * slab, leaves), F32 if t == 0 else BF16),
            [
                pltpu.VMEM((slab, 2 * slab, leaves), BF16),
                pltpu.VMEM((2 * vh * slab, leaves), F32),
                pltpu.SemaphoreType.DMA((4,)),
            ],
            2.4, scalars=1, whole=(4,),
        )

    near_parts = [None] * lvls
    near_parts[1] = near_part(1, after(field, keep))
    up_after = after(up_transfer, near_parts[1])

    block_rows = vs * rank_width + len(packs(vs, rank_width, leaves)) * parents
    block = call(
        "parent_coeffs",
        functools.partial(up_kernel, vs, parents),
        (keep, *recvs[::-1], up_after),
        sds((block_rows, leaves), BF16),
        [pltpu.VMEM((vs * rank_width, leaves), F32)],
        0.8,
    )
    with jax.named_scope("owner_sends"):
        blocks = [block] + swaps([block] * owners, "clus", owners, False)
    later = after(field, block)
    for t in range(2, lvls):
        near_parts[t] = near_part(t, later)
    with jax.named_scope("all_owners"):
        blocks = list(lax.optimization_barrier(tuple(blocks) + tuple(near_parts[2:])))[:owners]
        mine = jnp.concatenate(blocks, axis=0)
    with jax.named_scope("level_sends"):
        alls = [mine] + swaps([mine] * lvls, "lvl", lvls, False)

    later = after(field, mine)
    near_parts[0] = near_part(0, later)
    leaf_table, parent_table, pcouple_all = call(
        "partner_tables",
        functools.partial(table_kernel, owners, parents, slots),
        (after(partners, mine), partners_peer, pcouple, pcouple_peer),
        [
            sds((owners * leaves, 2 * slots * leaves), BF16),
            sds((2 * pslots * parents, owners * parents), BF16),
            sds((parents, 2 * pslots * rank_width, rank_width), BF16),
        ],
        [pltpu.VMEM(((rank_width + 1) * pslots * parents, rank_width), F32)],
        1.5,
    )
    def far_part(t, block):
        extras = (near_parts[t],) if 0 < t < lvls - 1 else ()
        rows = block_rows + (2 * vh * slab if extras else 0)
        return call(
            "coupling_products",
            functools.partial(far_kernel, owners, vs, pslots),
            (leaf_table, parent_table, pcouple_all, block, *extras, couple, couple_peer),
            sds((rows, leaves), F32 if t == 0 else BF16),
            [
                pltpu.VMEM((2 * slots, vs * rank_width, leaves), F32),
                pltpu.VMEM((parents, 8, 2 * pslots * rank_width), F32),
                pltpu.VMEM((parents, 8, rank_width), F32),
                pltpu.VMEM((slots, rank_width, rank_width, leaves), BF16),
                pltpu.SemaphoreType.DMA((slots,)),
            ],
            3.2, whole=(5 + len(extras),),
        )

    alls[1] = after(alls[1], near_parts[0])
    far_parts = [far_part(t, alls[t]) for t in range(lvls)]
    with jax.named_scope("far_sends"):
        far_recvs = swaps(far_parts, "lvl", lvls, False)
    with jax.named_scope("self_sends"):
        last = lvls - 1
        near_recv = swap(after(near_parts[last], far_recvs[-1], far_parts[0]), "lvl", lvls, last)
    far = call(
        "down_products",
        functools.partial(down_kernel, vs, parents),
        (far_parts[0], *far_recvs, down_transfer),
        sds((vs * rank_width, leaves), BF16),
        [pltpu.VMEM((vs * rank_width, leaves), F32)],
        0.8,
    )
    with jax.named_scope("far_coeff_sends"):
        far_blocks = [far] + swaps([far] * lvls, "lvl", lvls, True)
        far_others = [other(value) for value in far_blocks]
    early = lvls - 1

    def column_part(*blocks):
        return call(
            "column_products_early",
            functools.partial(column_kernel, vs),
            (column_basis, *blocks),
            sds((len(blocks) * vs * slab, leaves), F32),
            [pltpu.VMEM((len(blocks), vs * rank_width, leaves), F32)],
            0.25 * len(blocks),
        )

    done = [column_part(far_blocks[t], far_others[t]) for t in range(early)]
    last_mine = column_part(far_blocks[early])
    near_mine, near_send = call(
        "self_sums",
        functools.partial(near_sum_kernel, block_rows),
        (ids, after(near_parts[0], done[0]), near_recv, *far_recvs[:-1]),
        [sds((vh * slab, leaves), F32), sds((vh * slab, leaves), BF16)],
        (), 0.65, scalars=1,
    )
    with jax.named_scope("swap_self_sums"):
        near_peer = other(near_send)
    return call(
        "column_products",
        functools.partial(out_kernel, lvls, vh, vs, early),
        (
            ids, column_basis, near_mine, near_peer, *done,
            last_mine, far_others[early],
        ),
        sds((slab, vectors, leaves), BF16),
        [
            pltpu.VMEM((vs * rank_width, leaves), F32),
            pltpu.VMEM(((slab + 1) * vectors, leaves), F32),
        ],
        1.85, scalars=1,
    )


def solution(mesh):
    sizes = (mesh.shape["clus"], mesh.shape["lvl"], mesh.shape["rep"])
    return jax.shard_map(
        functools.partial(per_device, sizes),
        mesh=mesh,
        in_specs=(
            P(("lvl", "rep"), None, ("parts", "clus")),
            P(("lvl", "rep"), None, ("parts", "clus")),
            P(("lvl", "rep"), None, ("parts", "clus")),
            P(None, None, ("parts", "clus")),
            P(None, None, ("lvl", "rep"), None, ("parts", "clus")),
            P(None, None, ("lvl", "rep"), None, ("parts", "clus")),
            P(None, None, ("parts", "clus")),
            P(None, ("lvl", "rep"), ("parts", "clus")),
            P("parts"),
            P(("lvl", "rep"), ("parts", "clus"), None),
            P(("lvl", "rep"), ("parts", "clus"), None),
            P(("lvl", "rep"), ("parts", "clus"), None),
            P(("lvl", "rep"), ("parts", "clus"), None),
            P(("parts", "clus")),
        ),
        out_specs=P(("lvl", "rep"), None, ("parts", "clus")),
        check_vma=False,
    )
```

```python
import functools

import jax
import jax.numpy as jnp
from jax import lax
from jax.experimental import pallas as pl
from jax.experimental.pallas import tpu as pltpu
from jax.sharding import PartitionSpec as P

F32 = jnp.float32
BF16 = jnp.bfloat16
VMEM_LIMIT = 12 * 1024 * 1024


def vmem():
    return pl.BlockSpec(memory_space=pltpu.VMEM)


def smem():
    return pl.BlockSpec(memory_space=pltpu.SMEM)


def params(**more):
    return pltpu.CompilerParams(vmem_limit_bytes=VMEM_LIMIT, **more)


def cost(flops, nbytes):
    return pl.CostEstimate(flops=flops, bytes_accessed=nbytes, transcendentals=0)


def iota(shape, dim):
    return lax.broadcasted_iota(jnp.int32, shape, dim)


def row_of(ref, row):
    return ref[pl.ds(row, 1), :]


def mac_rows(total_steps, weight_at, row_at, accs, unroll):
    def body(step, carry):
        weight = weight_at(step)
        return tuple(acc + weight * row_at(step, n) for n, acc in enumerate(carry))

    return lax.fori_loop(0, total_steps, body, tuple(accs), unroll=unroll)


def pack_kernel(
    owners, vh, parents, ids_ref, perm_any, own_any, out_ref, rows_scr, perm_ref, own_ref, sems
):
    slab, vectors, leaves = own_ref.shape
    perm_copy = pltpu.make_async_copy(perm_any, perm_ref, sems.at[0])
    perm_copy.start()
    copies = []
    for c in range(4):
        part = slice(c * slab // 4, (c + 1) * slab // 4)
        copies.append(
            pltpu.make_async_copy(own_any.at[part], own_ref.at[part], sems.at[1 + c])
        )
        copies[-1].start()
    children = leaves // parents
    reps = vectors // vh
    width = leaves // owners
    me, parity = ids_ref[0], ids_ref[2]
    row = iota((leaves, leaves), 0)
    lane = iota((leaves, leaves), 1)
    parent_of_row = row // children
    target = row % children
    bits = 32 // owners
    counts = jnp.int32(0)
    perm_copy.wait()
    for parent in range(parents):
        owner = perm_ref[me * parents + parent] // parents
        shift = owner * bits
        rank = lax.shift_right_logical(counts, shift) & ((1 << bits) - 1)
        counts = counts + lax.shift_left(jnp.int32(1), shift)
        code = (owner ^ me) * leaves + rank * children
        target = target + jnp.where(parent_of_row == parent, code, 0)
    part = (slab // owners) * vh
    for copy in copies:
        copy.wait()
    rows_scr[0 : slab * vectors, :] = own_ref[...].reshape(slab * vectors, leaves).astype(F32)
    pieces = []
    for q in range(owners):
        start = q * (slab // owners) * vectors
        pieces.append(
            jnp.concatenate(
                [
                    rows_scr[pl.ds(start + first, part, stride=reps), :]
                    for first in (parity, 1 - parity)
                ],
                axis=0,
            ).astype(BF16)
        )
    for s in range(owners):
        total = jnp.zeros((2 * part, leaves), F32)
        for q in range(owners):
            onehot = jnp.where(target + (q * width - s * leaves) == lane, 1.0, 0.0).astype(BF16)
            total = total + jnp.dot(pieces[q], onehot, preferred_element_type=F32)
        out_ref[s] = total.astype(BF16)


def place_kernel(owners, parents, ids_ref, perm_any, out_ref, code_scr, perm_ref, sem):
    copy = pltpu.make_async_copy(perm_any, perm_ref, sem)
    copy.start()
    copy.wait()
    leaves = out_ref.shape[1]
    children = leaves // parents
    me = ids_ref[0]
    for source in range(owners):
        rank = jnp.int32(0)
        base = (source ^ me) * leaves
        for parent in range(parents):
            place = perm_ref[source * parents + parent]
            mine = (place // parents) == me
            slot = jnp.where(mine, place % parents, parents)
            code_scr[slot] = base + rank * children
            rank = rank + jnp.where(mine, 1, 0)
    lane = iota(out_ref.shape, 1)
    code = lane % children
    for parent in range(parents):
        code = code + jnp.where(lane // children == parent, code_scr[parent], 0)
    out_ref[...] = code


def regroup_kernel(owners, code_ref, *refs):
    chunks, mine_ref, other_ref = refs[:owners], refs[owners], refs[owners + 1]
    leaves = mine_ref.shape[1]
    width = leaves // owners
    part = mine_ref.shape[0] // owners
    code = jnp.broadcast_to(code_ref[0:1, :], (leaves, leaves))
    row = iota((leaves, leaves), 0)
    for q in range(owners):
        total = jnp.zeros((2 * part, leaves), F32)
        for s in range(owners):
            onehot = jnp.where(code + (q * width - s * leaves) == row, 1.0, 0.0).astype(BF16)
            total = total + jnp.dot(chunks[s][...], onehot, preferred_element_type=F32)
        mine_ref[q * part : (q + 1) * part, :] = total[:part]
        other_ref[q * part : (q + 1) * part, :] = total[part:].astype(BF16)


def coeff_products(lvl, lvls, vh, vs, basis_ref, field_ref, start_of, finish):
    slab, rank_width, leaves = basis_ref.shape
    half = rank_width // 2
    for first_t in range(0, lvls, 2):
        members = [(t, n) for t in (first_t, first_t + 1) for n in range(vs)]
        places = [jnp.minimum((lvl ^ t) * vs + n, vh - 1) for t, n in members]
        for low in range(0, rank_width, half):
            part = slice(low, low + half)
            accs = mac_rows(
                slab,
                lambda m: basis_ref[m, part, :].astype(F32),
                lambda m, n: row_of(field_ref, m * vh + places[n]),
                [start_of(t, n, low, half) for t, n in members],
                8,
            )
            for (t, n), acc in zip(members, accs):
                finish(t, n, low, half, acc)


def coeff_own_kernel(lvls, vh, vs, ids_ref, basis_ref, field_ref, out_ref):
    rank_width, leaves = basis_ref.shape[1:]

    def finish(t, n, low, half, acc):
        start = (t * vs + n) * rank_width + low
        out_ref[start : start + half, :] = acc

    coeff_products(
        ids_ref[1], lvls, vh, vs, basis_ref, field_ref,
        lambda t, n, low, half: jnp.zeros((half, leaves), F32), finish,
    )


def coeff_peer_kernel(
    lvls, vh, vs, ids_ref, basis_ref, field_ref, own_ref, wide_ref, keep_ref, *sends
):
    rank_width = basis_ref.shape[1]
    wide_ref[...] = field_ref[...].astype(F32)

    def start_of(t, n, low, half):
        start = (t * vs + n) * rank_width + low
        return own_ref[start : start + half, :]

    def finish(t, n, low, half, acc):
        start = n * rank_width + low
        if t == 0:
            keep_ref[start : start + half, :] = acc
        else:
            sends[t - 1][start : start + half, :] = acc.astype(BF16)

    coeff_products(ids_ref[1], lvls, vh, vs, basis_ref, wide_ref, start_of, finish)


def packs(vs, rank_width, leaves):
    per = max(1, leaves // rank_width)
    return [list(range(first, min(first + per, vs))) for first in range(0, vs, per)]


def up_kernel(vs, parents, keep_ref, *refs):
    recvs, up_ref, out_ref, coeff_scr = refs[:-3], refs[-3], refs[-2], refs[-1]
    rank_width, _, leaves = up_ref.shape
    total = keep_ref[...]
    for ref in recvs:
        total = total + ref[...].astype(F32)
    coeffs = total.astype(BF16)
    out_ref[0 : vs * rank_width, :] = coeffs
    coeff_scr[...] = coeffs.astype(F32)
    accs = mac_rows(
        rank_width,
        lambda j: up_ref[j].astype(F32),
        lambda j, n: row_of(coeff_scr, n * rank_width + j),
        [jnp.zeros((rank_width, leaves), F32) for _ in range(vs)],
        8,
    )
    mine = (iota((parents, leaves), 1) // (leaves // parents)) == iota((parents, leaves), 0)
    group = jnp.where(mine, 1.0, 0.0).astype(BF16)
    for b, members in enumerate(packs(vs, rank_width, leaves)):
        sums = []
        for n in members:
            rest, result = accs[n], jnp.zeros((parents, rank_width), F32)
            for _ in range(3):
                piece = rest.astype(BF16)
                result = result + lax.dot_general(
                    group, piece, (((1,), (1,)), ((), ())), preferred_element_type=F32
                )
                rest = rest - piece.astype(F32)
            sums.append(result)
        missing = leaves - len(sums) * rank_width
        if missing:
            sums.append(jnp.zeros((parents, missing), F32))
        start = vs * rank_width + b * parents
        out_ref[start : start + parents, :] = jnp.concatenate(sums, axis=1).astype(BF16)


def table_kernel(
    owners, parents, slots, own_codes, peer_codes, own_ref, peer_ref,
    leaf_out, parent_out, couple_out, rows_scr,
):
    leaves = own_codes.shape[1]
    sources = leaf_out.shape[0]
    count = parent_out.shape[0] // 2
    for half, codes in enumerate((own_codes, peer_codes)):
        for i in range(slots):
            hit = jnp.broadcast_to(codes[i : i + 1, :], (sources, leaves)) == iota(
                (sources, leaves), 0
            )
            start = (half * slots + i) * leaves
            leaf_out[:, start : start + leaves] = jnp.where(hit, 1.0, 0.0).astype(BF16)
        uppers = owners * parents
        same = iota((uppers, uppers), 0) == iota((uppers, uppers), 1)
        same = jnp.where(same, 1.0, 0.0).astype(BF16)
        pslots = count // parents
        for i in range(pslots):
            code = jnp.broadcast_to(codes[slots + i : slots + i + 1, :], (uppers, leaves))
            hit = jnp.where(code == iota(code.shape, 0), 1.0, 0.0).astype(BF16)
            turned = lax.dot_general(
                hit, same, (((0,), (0,)), ((), ())), preferred_element_type=F32
            )
            start = half * count + i * parents
            parent_out[start : start + parents, :] = turned[:parents].astype(BF16)
    rank_width, pslots = own_ref.shape[0], own_ref.shape[1] // parents
    for half, ref in enumerate((own_ref, peer_ref)):
        blocks = ref[...].reshape(rank_width * pslots * parents, rank_width)
        rows_scr[0 : blocks.shape[0], :] = blocks.astype(F32)
        for i in range(pslots):
            place = (half * pslots + i) * rank_width
            for parent in range(parents):
                block = rows_scr[pl.ds(i * parents + parent, rank_width, stride=pslots * parents), :]
                couple_out[parent, place : place + rank_width, :] = block.astype(BF16)


def far_kernel(owners, vs, pslots, leaf_table, parent_table, pcouple_ref, block_ref, *refs):
    extras = refs[:-8]
    own_ref, peer_any, out_ref, rows_scr, prows_scr, pout_scr, couple_scr, sems = refs[-8:]
    slots, rank_width, _, leaves = own_ref.shape
    parents = pcouple_ref.shape[0]
    copies = []
    for i in range(slots):
        copies.append(pltpu.make_async_copy(peer_any.at[i], couple_scr.at[i], sems.at[i]))
        copies[-1].start()
    per_block = block_ref.shape[0] // owners
    mine = vs * rank_width
    rows = jnp.zeros((mine, 2 * slots * leaves), F32)
    for o in range(0, owners, 2):
        pair = [block_ref[p * per_block : p * per_block + mine, :] for p in (o, o + 1)]
        rows = rows + jnp.dot(
            jnp.concatenate(pair, axis=1),
            leaf_table[o * leaves : (o + 2) * leaves, :],
            preferred_element_type=F32,
        )
    for i in range(2 * slots):
        rows_scr[i] = rows[:, i * leaves : (i + 1) * leaves]

    for b, members in enumerate(packs(vs, rank_width, leaves)):
        source = jnp.concatenate(
            [
                block_ref[pl.ds(o * per_block + mine + b * parents, parents), :]
                for o in range(owners)
            ],
            axis=0,
        )
        picked = jnp.dot(parent_table[...], source, preferred_element_type=F32)
        for i in range(2 * pslots):
            for k, n in enumerate(members):
                prows_scr[:, n, i * rank_width : (i + 1) * rank_width] = picked[
                    i * parents : (i + 1) * parents, k * rank_width : (k + 1) * rank_width
                ]
    start = mine + len(packs(vs, rank_width, leaves)) * parents
    for ref in extras:
        out_ref[start : start + ref.shape[0], :] = ref[...]
        start += ref.shape[0]

    accs = tuple(jnp.zeros((rank_width, leaves), F32) for _ in range(vs))
    turns = parents // (2 * slots)
    width = rank_width // turns
    for s in range(2 * slots):
        if s >= slots:
            copies[s - slots].wait()
        ref, i = (own_ref, s) if s < slots else (couple_scr, s - slots)

        def body(turn, carry, s=s, ref=ref, i=i):
            parent = s * turns + turn
            pout_scr[parent] = jnp.dot(
                prows_scr[parent].astype(BF16), pcouple_ref[parent], preferred_element_type=F32
            )
            for k in range(width):
                j = turn * width + k
                weight = ref[i, j].astype(F32)
                carry = tuple(
                    acc + weight * rows_scr[s, pl.ds(n * rank_width + j, 1), :]
                    for n, acc in enumerate(carry)
                )
            return carry

        accs = lax.fori_loop(0, turns, body, accs)
    for n in range(vs):
        out_ref[n * rank_width : (n + 1) * rank_width, :] = accs[n].astype(out_ref.dtype)
    for b, members in enumerate(packs(vs, rank_width, leaves)):
        parts = [pout_scr[:, n, :] for n in members]
        missing = leaves - len(parts) * rank_width
        if missing:
            parts.append(jnp.zeros((parents, missing), F32))
        out_ref[mine + b * parents : mine + (b + 1) * parents, :] = jnp.concatenate(
            parts, axis=1
        ).astype(out_ref.dtype)


def down_kernel(vs, parents, keep_ref, *refs):
    recvs, down_ref, out_ref, rows_scr = refs[:-3], refs[-3], refs[-2], refs[-1]
    rank_width, _, leaves = down_ref.shape
    total = keep_ref[...]
    for ref in recvs:
        total = total + ref[0 : total.shape[0], :].astype(F32)
    mine = vs * rank_width
    below = (iota((parents, leaves), 1) // (leaves // parents)) == iota((parents, leaves), 0)
    spread = jnp.where(below, 1.0, 0.0).astype(BF16)
    for b, members in enumerate(packs(vs, rank_width, leaves)):
        part = total[mine + b * parents : mine + (b + 1) * parents, :].astype(BF16)
        wide = lax.dot_general(
            part, spread, (((0,), (0,)), ((), ())), preferred_element_type=F32
        )
        count = len(members) * rank_width
        start = members[0] * rank_width
        rows_scr[start : start + count, :] = wide[:count]
    accs = mac_rows(
        rank_width,
        lambda j: down_ref[j].astype(F32),
        lambda j, n: row_of(rows_scr, n * rank_width + j),
        [total[n * rank_width : (n + 1) * rank_width, :] for n in range(vs)],
        8,
    )
    for n in range(vs):
        out_ref[n * rank_width : (n + 1) * rank_width, :] = accs[n].astype(BF16)


def near_kernel(
    vh, step, ids_ref, own_field, peer_field, own_ref, peer_any, out_ref, peer_scr, acc_scr, sems
):
    slab, _, leaves = own_ref.shape
    group = 6
    target = pl.multiple_of((ids_ref[1] ^ step) * (2 * slab), 2 * slab)
    copies = []
    for c in range(4):
        part = slice(c * slab // 4, (c + 1) * slab // 4)
        copies.append(
            pltpu.make_async_copy(
                peer_any.at[part, pl.ds(target, 2 * slab), :], peer_scr.at[part], sems.at[c]
            )
        )
        copies[-1].start()

    def products(field_ref, ref, base, first, half, accs):
        span = pl.ds(pl.multiple_of(base + half * slab, slab), slab)
        return mac_rows(
            slab,
            lambda p: ref[p, span, :].astype(F32),
            lambda p, n: row_of(field_ref, p * vh + first + n),
            accs,
            16,
        )

    places = [(half, first) for half in range(2) for first in range(0, vh, group)]
    for half, first in places:
        accs = [jnp.zeros((slab, leaves), F32) for _ in range(group)]
        accs = products(own_field, own_ref, target, first, half, accs)
        for n in range(group):
            start = (half * vh + first + n) * slab
            acc_scr[start : start + slab, :] = accs[n]
    for copy in copies:
        copy.wait()
    for half, first in places:
        starts = [(half * vh + first + n) * slab for n in range(group)]
        accs = [acc_scr[start : start + slab, :] for start in starts]
        accs = products(peer_field, peer_scr, 0, first, half, accs)
        for n, start in enumerate(starts):
            out_ref[start : start + slab, :] = accs[n].astype(out_ref.dtype)


def near_sum_kernel(skip, ids_ref, keep_ref, last_ref, *refs):
    recvs, mine_ref, send_ref = refs[:-2], refs[-2], refs[-1]
    count = mine_ref.shape[0]
    parity = ids_ref[2]

    def summed(start):
        start = pl.multiple_of(start, 16)
        total = keep_ref[pl.ds(start, count), :] + last_ref[pl.ds(start, count), :].astype(F32)
        for ref in recvs:
            total = total + ref[pl.ds(skip + start, count), :].astype(F32)
        return total

    mine_ref[...] = summed(parity * count)
    send_ref[...] = summed((1 - parity) * count).astype(BF16)


def column_kernel(vs, column_ref, mine_ref, other_ref, out_ref, rows_scr):
    rank_width, voxels, leaves = column_ref.shape
    rows_scr[0] = mine_ref[...].astype(F32)
    rows_scr[1] = other_ref[...].astype(F32)
    accs = mac_rows(
        rank_width,
        lambda k: column_ref[k].astype(F32),
        lambda k, n: rows_scr[n // vs, pl.ds((n % vs) * rank_width + k, 1), :],
        [jnp.zeros((voxels, leaves), F32) for _ in range(2 * vs)],
        8,
    )
    for n in range(2 * vs):
        out_ref[n * voxels : (n + 1) * voxels, :] = accs[n]


def out_kernel(lvls, vh, vs, early, ids_ref, column_ref, near_mine, near_peer, *refs):
    done, blocks = refs[:early], refs[early : -3]
    out_ref, rows_scr, out_scr = refs[-3:]
    rank_width, voxels, leaves = column_ref.shape
    vectors = out_ref.shape[1]
    lvl, parity = ids_ref[1], ids_ref[2]
    late = lvls - early
    for b, ref in enumerate(blocks):
        rows_scr[b] = ref[...].astype(F32)

    def store(place, rep, value):
        def write():
            vector = place * 2 + (parity if rep == 0 else 1 - parity)
            out_scr[pl.ds(vector, voxels, stride=vectors), :] = value

        if lvls * vs == vh:
            write()
        else:
            pl.when(place < vh)(write)

    for t in range(lvls):
        first = (lvl ^ t) * vs
        if t < early:
            accs = [done[t][n * voxels : (n + 1) * voxels, :] for n in range(2 * vs)]
        else:
            accs = mac_rows(
                rank_width,
                lambda k: column_ref[k].astype(F32),
                lambda k, n: rows_scr[
                    (n // vs) * late + t - early, pl.ds((n % vs) * rank_width + k, 1), :
                ],
                [jnp.zeros((voxels, leaves), F32) for _ in range(2 * vs)],
                8,
            )
        for n in range(2 * vs):
            place = first + n % vs
            near_ref = (near_mine, near_peer)[n // vs]
            inside = jnp.minimum(place, vh - 1)
            near = near_ref[pl.ds(pl.multiple_of(inside * voxels, voxels), voxels), :]
            store(place, n // vs, accs[n] + near.astype(F32))
    whole = out_scr[0 : voxels * vectors, :]
    out_ref[...] = whole.reshape(voxels, vectors, leaves).astype(BF16)


def after(value, *others):
    return lax.optimization_barrier((value,) + others)[0]


def per_device(sizes, *args):
    (
        voxel_field, row_basis, near_block, up_transfer, coupling, parent_coupling,
        down_transfer, column_basis, parent_perm, partner_owner, partner_local,
        parent_owner, parent_local, block_count,
    ) = args
    owners, lvls, reps = sizes
    slab, vectors, leaves = voxel_field.shape
    rank_width = row_basis.shape[1]
    parents = parent_coupling.shape[4]
    children = leaves // parents
    slots = partner_owner.shape[2]
    pslots = parent_owner.shape[2]
    vh = vectors // reps
    vs = -(-vh // lvls)
    sds = jax.ShapeDtypeStruct

    me = lax.axis_index("clus")
    lvl = lax.axis_index("lvl")
    parity = lax.axis_index("rep")
    ids = jnp.stack([me, lvl, parity]).astype(jnp.int32)

    def call(name, kernel, ins, outs, scratch=(), us=1.0, scalars=0, whole=()):
        specs = [
            smem() if i < scalars else pl.BlockSpec(memory_space=pltpu.HBM) if i in whole else vmem()
            for i in range(len(ins))
        ]
        with jax.named_scope(name):
            return pl.pallas_call(
                kernel,
                out_shape=outs,
                in_specs=specs,
                out_specs=jax.tree.map(lambda _: vmem(), outs),
                scratch_shapes=list(scratch),
                compiler_params=params(),
                cost_estimate=cost(0, int(us * 3.3e6)),
            )(*ins)

    def swap(value, axis, count, step):
        return lax.ppermute(value, axis, [(i, i ^ step) for i in range(count)])

    def swaps(values, axis, count, backward=True):
        order = range(count - 1, 0, -1) if backward else range(1, count)
        got = {n: swap(values[n], axis, count, n) for n in order}
        return [got[n] for n in range(1, count)]

    def other(value):
        return swap(value, "rep", reps, 1)

    with jax.named_scope("swap_row_basis"):
        row_peer = other(row_basis)

    with jax.named_scope("swap_parent_coupling"):
        pcouple = jnp.transpose(parent_coupling, (0, 2, 3, 4, 1)).reshape(
            rank_width, pslots * parents, rank_width
        )
        pcouple_peer = other(pcouple)

    with jax.named_scope("swap_self_blocks"):
        near_peer_block = other(near_block)

    chunk_rows = 2 * (slab // owners) * vh
    packed = call(
        "pack_field",
        functools.partial(pack_kernel, owners, vh, parents),
        (
            ids,
            pltpu.with_memory_space_constraint(parent_perm, pltpu.HBM),
            pltpu.with_memory_space_constraint(voxel_field, pltpu.HBM),
        ),
        sds((owners, chunk_rows, leaves), BF16),
        [
            pltpu.VMEM((slab * vectors + 8, leaves), F32),
            pltpu.SMEM(parent_perm.shape, jnp.int32),
            pltpu.VMEM(voxel_field.shape, BF16),
            pltpu.SemaphoreType.DMA((5,)),
        ],
        1.0, scalars=1, whole=(1, 2),
    )
    with jax.named_scope("regroup_sends"):
        chunks = [packed[0]] + swaps([packed[s] for s in range(owners)], "clus", owners, True)
    codes = call(
        "place_codes",
        functools.partial(place_kernel, owners, parents),
        (after(ids, chunks[1]), pltpu.with_memory_space_constraint(parent_perm, pltpu.HBM)),
        sds((8, leaves), jnp.int32),
        [
            pltpu.SMEM((parents + 1,), jnp.int32),
            pltpu.SMEM(parent_perm.shape, jnp.int32),
            pltpu.SemaphoreType.DMA,
        ],
        0.3, scalars=1, whole=(1,),
    )
    with jax.named_scope("coupling_layout"):
        couple = jnp.moveaxis(after(coupling, chunks[1])[:, :, 0], 2, 0)

    with jax.named_scope("partner_codes"):
        held = lax.optimization_barrier(
            (partner_owner, partner_local, parent_owner, parent_local, block_count, chunks[1])
        )
        group = lvl * reps + parity
        row = jnp.arange(slots + pslots, dtype=jnp.int32)[:, None]
        wide = ((0, 0), (0, leaves - parents))
        owner = jnp.concatenate([held[0][0].T, jnp.pad(held[2][0].T, wide)], axis=0) ^ me
        local = jnp.concatenate([held[1][0].T, jnp.pad(held[3][0].T, wide)], axis=0)
        live = (row >= slots) | (group * slots + row < held[4][None, :])
        partners = owner * jnp.where(row < slots, leaves, parents) + local
        partners = jnp.where(live, partners, -1)
        partners_peer = other(partners)
    codes = after(codes, couple, row_peer, partners_peer)

    field, field_send = call(
        "regroup_field",
        functools.partial(regroup_kernel, owners),
        (codes, *chunks),
        [sds((slab * vh, leaves), F32), sds((slab * vh, leaves), BF16)],
        (), 0.4,
    )
    with jax.named_scope("swap_field"):
        field_recv = other(field_send)
    coeff_own = call(
        "coeffs_own_slab",
        functools.partial(coeff_own_kernel, lvls, vh, vs),
        (ids, row_basis, field),
        sds((lvls * vs * rank_width, leaves), F32),
        (), 1.6, scalars=1,
    )
    outs = call(
        "coeffs_other_slab",
        functools.partial(coeff_peer_kernel, lvls, vh, vs),
        (ids, row_peer, field_recv, coeff_own),
        [sds((slab * vh, leaves), F32), sds((vs * rank_width, leaves), F32)]
        + [sds((vs * rank_width, leaves), BF16)] * (lvls - 1),
        (), 1.6, scalars=1,
    )
    field_peer, keep, sends = outs[0], outs[1], outs[2:]
    with jax.named_scope("coeff_sends"):
        recvs = swaps([None, *sends], "lvl", lvls, True)

    with jax.named_scope("swap_coupling"):
        couple_peer = other(after(couple, keep))

    def near_part(t, place):
        return call(
            "self_blocks",
            functools.partial(near_kernel, vh, t),
            (ids, place, field_peer, near_block, near_peer_block),
            sds((2 * vh * slab, leaves), F32 if t == 0 else BF16),
            [
                pltpu.VMEM((slab, 2 * slab, leaves), BF16),
                pltpu.VMEM((2 * vh * slab, leaves), F32),
                pltpu.SemaphoreType.DMA((4,)),
            ],
            2.4, scalars=1, whole=(4,),
        )

    near_parts = [None] * lvls
    near_parts[1] = near_part(1, after(field, keep))
    up_after = after(up_transfer, near_parts[1])

    block_rows = vs * rank_width + len(packs(vs, rank_width, leaves)) * parents
    block = call(
        "parent_coeffs",
        functools.partial(up_kernel, vs, parents),
        (keep, *recvs[::-1], up_after),
        sds((block_rows, leaves), BF16),
        [pltpu.VMEM((vs * rank_width, leaves), F32)],
        0.8,
    )
    with jax.named_scope("owner_sends"):
        blocks = [block] + swaps([block] * owners, "clus", owners, True)
    later = after(field, block)
    for t in range(2, lvls):
        near_parts[t] = near_part(t, later)
    with jax.named_scope("all_owners"):
        blocks = list(lax.optimization_barrier(tuple(blocks) + tuple(near_parts[2:])))[:owners]
        mine = jnp.concatenate(blocks, axis=0)
    with jax.named_scope("level_sends"):
        alls = [mine] + swaps([mine] * lvls, "lvl", lvls, False)

    later = after(field, mine)
    near_parts[0] = near_part(0, later)
    leaf_table, parent_table, pcouple_all = call(
        "partner_tables",
        functools.partial(table_kernel, owners, parents, slots),
        (after(partners, mine), partners_peer, pcouple, pcouple_peer),
        [
            sds((owners * leaves, 2 * slots * leaves), BF16),
            sds((2 * pslots * parents, owners * parents), BF16),
            sds((parents, 2 * pslots * rank_width, rank_width), BF16),
        ],
        [pltpu.VMEM(((rank_width + 1) * pslots * parents, rank_width), F32)],
        1.5,
    )
    def far_part(t, block):
        extras = (near_parts[t],) if 0 < t < lvls - 1 else ()
        rows = block_rows + (2 * vh * slab if extras else 0)
        return call(
            "coupling_products",
            functools.partial(far_kernel, owners, vs, pslots),
            (leaf_table, parent_table, pcouple_all, block, *extras, couple, couple_peer),
            sds((rows, leaves), F32 if t == 0 else BF16),
            [
                pltpu.VMEM((2 * slots, vs * rank_width, leaves), F32),
                pltpu.VMEM((parents, 8, 2 * pslots * rank_width), F32),
                pltpu.VMEM((parents, 8, rank_width), F32),
                pltpu.VMEM((slots, rank_width, rank_width, leaves), BF16),
                pltpu.SemaphoreType.DMA((slots,)),
            ],
            3.2, whole=(5 + len(extras),),
        )

    alls[1] = after(alls[1], near_parts[0])
    far_parts = [far_part(t, alls[t]) for t in range(lvls)]
    with jax.named_scope("far_sends"):
        far_recvs = swaps(far_parts, "lvl", lvls, False)
    with jax.named_scope("self_sends"):
        last = lvls - 1
        near_recv = swap(after(near_parts[last], far_recvs[-1], far_parts[0]), "lvl", lvls, last)
    far = call(
        "down_products",
        functools.partial(down_kernel, vs, parents),
        (far_parts[0], *far_recvs, down_transfer),
        sds((vs * rank_width, leaves), BF16),
        [pltpu.VMEM((vs * rank_width, leaves), F32)],
        0.8,
    )
    with jax.named_scope("far_coeff_sends"):
        far_blocks = [far] + swaps([far] * lvls, "lvl", lvls, True)
        far_others = [other(value) for value in far_blocks]
    early = lvls - 1
    done = [
        call(
            "column_products_early",
            functools.partial(column_kernel, vs),
            (column_basis, far_blocks[t], far_others[t]),
            sds((2 * vs * slab, leaves), F32),
            [pltpu.VMEM((2, vs * rank_width, leaves), F32)],
            0.5,
        )
        for t in range(early)
    ]
    near_mine, near_send = call(
        "self_sums",
        functools.partial(near_sum_kernel, block_rows),
        (ids, after(near_parts[0], done[0]), near_recv, *far_recvs[:-1]),
        [sds((vh * slab, leaves), F32), sds((vh * slab, leaves), BF16)],
        (), 0.65, scalars=1,
    )
    with jax.named_scope("swap_self_sums"):
        near_peer = other(near_send)
    return call(
        "column_products",
        functools.partial(out_kernel, lvls, vh, vs, early),
        (
            ids, column_basis, near_mine, near_peer, *done,
            *far_blocks[early:], *far_others[early:],
        ),
        sds((slab, vectors, leaves), BF16),
        [
            pltpu.VMEM((2 * (lvls - early), vs * rank_width, leaves), F32),
            pltpu.VMEM(((slab + 1) * vectors, leaves), F32),
        ],
        1.85, scalars=1,
    )


def solution(mesh):
    sizes = (mesh.shape["clus"], mesh.shape["lvl"], mesh.shape["rep"])
    return jax.shard_map(
        functools.partial(per_device, sizes),
        mesh=mesh,
        in_specs=(
            P(("lvl", "rep"), None, ("parts", "clus")),
            P(("lvl", "rep"), None, ("parts", "clus")),
            P(("lvl", "rep"), None, ("parts", "clus")),
            P(None, None, ("parts", "clus")),
            P(None, None, ("lvl", "rep"), None, ("parts", "clus")),
            P(None, None, ("lvl", "rep"), None, ("parts", "clus")),
            P(None, None, ("parts", "clus")),
            P(None, ("lvl", "rep"), ("parts", "clus")),
            P("parts"),
            P(("lvl", "rep"), ("parts", "clus"), None),
            P(("lvl", "rep"), ("parts", "clus"), None),
            P(("lvl", "rep"), ("parts", "clus"), None),
            P(("lvl", "rep"), ("parts", "clus"), None),
            P(("parts", "clus")),
        ),
        out_specs=P(("lvl", "rep"), None, ("parts", "clus")),
        check_vma=False,
    )
```
